32 devices in a mesh: dp: 8 (over y, x, core), tensor: 4 (over z).
Axes of the slice: x: 2, y: 2, z: 4, core: 2. Of those that a mesh axis runs over, the one named last changes fastest.
Arguments:
- layer_in: bfloat16 [8, 2048, 1536], P('dp', 'tensor'), may hold values from -6 to 6
- cotangent: bfloat16 [8, 2048, 1536], P('dp', 'tensor'), may hold values from -6 to 6
- segment_ids: int32 [8, 2048], P('dp'), may hold values from 0 to 4, as said below
- adapter_ids: int32 [8], P('dp'), may hold values from 0 to 7
- norm_gain: float32 [1536], replicated, may hold values from 0.5 to 1.5
- inner_weight: bfloat16 [1536, 2, 3072], P('dp', None, 'tensor'), may hold values from -0.15625 to 0.15625
- map_weight: bfloat16 [1536, 256], P('dp'), may hold values from -0.15625 to 0.15625
- step_weight: bfloat16 [1536, 48], P('dp', 'tensor'), may hold values from -0.15625 to 0.15625
- conv_inner_weight: float32 [4, 3072], P(None, 'tensor'), may hold values from -3 to 3
- conv_inner_bias: float32 [3072], P('tensor'), may hold values from -3 to 3
- conv_map_weight: float32 [4, 256], replicated, may hold values from -3 to 3
- conv_map_bias: float32 [256], replicated, may hold values from -3 to 3
- step_bias: float32 [48], P('tensor'), may hold values from -6 to -2
- decay_log: float32 [48], P('tensor'), may hold values from -3 to 1.5
- skip_gain: float32 [48], P('tensor'), may hold values from 0.5 to 1.5
- gate_gain: float32 [3072], P('tensor'), may hold values from 0.5 to 1.5
- out_weight: bfloat16 [3072, 1536], P('tensor', 'dp'), may hold values from -0.109375 to 0.109375
- adapter_down: bfloat16 [8, 1536, 16], replicated, may hold values from -0.15625 to 0.15625
- adapter_inner: bfloat16 [8, 16, 2, 3072], P(None, None, None, 'tensor'), may hold values from -0.75 to 0.75
- adapter_map: bfloat16 [8, 16, 256], replicated, may hold values from -0.75 to 0.75
- adapter_step: bfloat16 [8, 16, 48], P(None, None, 'tensor'), may hold values from -0.75 to 0.75
- adapter_mixed: bfloat16 [8, 3072, 16], P(None, 'tensor'), may hold values from -0.109375 to 0.109375
- adapter_up: bfloat16 [8, 16, 1536], replicated, may hold values from -0.75 to 0.75
Outputs:
- layer_out: bfloat16 [8, 2048, 1536], P('dp', 'tensor')
- input_grad: float32 [8, 2048, 1536], P('dp', 'tensor')
- grad_adapter_down: float32 [8, 1536, 16], replicated
- grad_adapter_inner: float32 [8, 16, 2, 3072], P(None, None, None, 'tensor')
- adjoint_projector_table: float32 [8, 16, 256], replicated
- grad_adapter_step: float32 [8, 16, 48], P(None, None, 'tensor')
- grad_adapter_mixed: float32 [8, 3072, 16], P(None, 'tensor')
- grad_adapter_up: float32 [8, 16, 1536], replicated
The draws below stay inside these ranges and needn't reach their ends.
Inputs may be any that keep to these rules, and one draw needn't show every extreme that they name: `segment_ids`: each row starts at 0 and rises by one where a document starts; every row holds 5 documents of 60 to 800 tokens, one of exactly 800.
All inputs are finite; a program needn't handle non-finite values.
Results may differ from the reference program's by a relative error of at most 0.0095.
Values may be sent and summed in bfloat16 or wider, within the bound.
No kernel may reach another device: no remote copies, remote signals or barrier semaphores. Data moves between devices by JAX's collectives and lax.ppermute only.
A program may use at most 256 MiB of HBM per device.

```python
import jax
import jax.numpy as jnp
from jax import lax

D = 1536
H = 48
P_SIZE = 64
N = 128
CONV = 4
BLOCK = 256
RANK = 16
ADAPTERS = 8
SEQ_LEN = 2048
DOCS = 5
DOC_MIN = 60
DOC_MOST = 800
DI = 3072
SEQS = 8


def draw_segment_ids(key, part):
    key = jax.random.fold_in(key, 17)
    first_key, second_key = jax.random.split(key)
    weights = jax.random.randint(first_key, (SEQS, DOCS - 1), 1, 8)
    total = jnp.sum(weights, axis=1, keepdims=True)
    extra = SEQ_LEN - DOC_MOST - (DOCS - 1) * DOC_MIN
    shares = extra * weights // total
    left = extra - jnp.sum(shares, axis=1, keepdims=True)
    first = (jnp.arange(DOCS - 1) == 0)[None, :]
    others = DOC_MIN + shares + jnp.where(first, left, 0)
    spot = jax.random.randint(second_key, (SEQS, 1), 0, DOCS)
    index = jnp.arange(DOCS)[None, :]
    before = jnp.concatenate([others[:, :1], others], axis=1)
    after = jnp.concatenate([others, others[:, -1:]], axis=1)
    lengths = jnp.where(index == spot, DOC_MOST, jnp.where(index < spot, after, before))
    ends = jnp.cumsum(lengths, axis=1)
    position = jnp.arange(SEQ_LEN)
    segment = jnp.sum((position[None, :, None] >= ends[:, None, :]).astype(jnp.int32), axis=2)
    return segment.astype(jnp.int32)


def touch_ends(array, key, least, largest):
    extent = array.shape
    index_at = [jax.random.randint(jax.random.fold_in(key, axis), (), 0, extent[axis]) for axis in range(len(extent))]
    array = array.at[tuple(index_at)].set(least)
    longest = extent.index(max(extent))
    index_at[longest] = (index_at[longest] + 1) % extent[longest]
    return array.at[tuple(index_at)].set(largest)


def shard_levels(key, extent, shards, low, largest):
    factor_of = 1.0
    for dim, blocks in shards:
        draws = jax.random.uniform(jax.random.fold_in(jax.random.fold_in(key, 6), dim), (blocks,), jnp.float32, low / len(shards), largest / len(shards))
        factor_of = factor_of * jnp.repeat(jnp.exp(draws), extent[dim] // blocks).reshape((-1,) + (1,) * (len(extent) - 1 - dim))
    return factor_of


def bell_draw(key, dims, deviation, limit, shards=(), kind=jnp.bfloat16):
    array = jax.random.normal(key, dims, jnp.float32) * deviation
    if len(shards) > 0:
        array = shard_levels(key, dims, shards, -0.22, 0.18) * array
    return jnp.clip(array, min=-limit, max=limit).astype(kind)


def setup_inputs(seed: int = 0) -> dict:
    splits = jax.random.split(jax.random.key(seed), 24)
    layer_in = bell_draw(splits[0], (SEQS, SEQ_LEN, D), 1.0, 6.0, ((0, 8), (1, 4)))
    cotangent = bell_draw(splits[1], (SEQS, SEQ_LEN, D), 1.0, 6.0, ((0, 8), (1, 4)))
    segment_ids = draw_segment_ids(jax.random.fold_in(splits[23], 71), 0)
    adapter_ids = touch_ends(jax.random.randint(splits[3], (SEQS,), 0, ADAPTERS), jax.random.fold_in(splits[3], 1), 0, ADAPTERS - 1).astype(jnp.int32)
    norm_gain = jnp.clip(1.0 + 0.1 * jax.random.normal(splits[4], (D,), jnp.float32), 0.5, 1.5)
    inner_weight = bell_draw(splits[5], (D, 2, DI), D ** -0.5, 0.15625, ((0, 8), (2, 4)))
    map_weight = bell_draw(splits[6], (D, 2 * N), D ** -0.5, 0.15625, ((0, 8),))
    step_weight = bell_draw(splits[7], (D, H), D ** -0.5, 0.15625, ((0, 8), (1, 4)))
    conv_inner_weight = bell_draw(splits[8], (CONV, DI), CONV ** -0.5, 3.0, ((1, 4),), jnp.float32)
    conv_inner_bias = bell_draw(splits[9], (DI,), 0.5, 3.0, ((0, 4),), jnp.float32)
    conv_map_weight = bell_draw(splits[10], (CONV, 2 * N), CONV ** -0.5, 3.0, (), jnp.float32)
    conv_map_bias = bell_draw(splits[11], (2 * N,), 0.5, 3.0, (), jnp.float32)
    step_bias = jnp.clip(-6.0 + 4.0 * jax.random.uniform(splits[12], (H,), jnp.float32) ** shard_levels(splits[12], (H,), ((0, 4),), -0.2, 0.2), -6.0, -2.0)
    decay_log = jnp.clip(-3.0 + 4.5 * jax.random.uniform(splits[13], (H,), jnp.float32) ** shard_levels(splits[13], (H,), ((0, 4),), -0.2, 0.2), -3.0, 1.5)
    skip_gain = jnp.clip(0.5 + 1.0 * jax.random.uniform(splits[14], (H,), jnp.float32) ** shard_levels(splits[14], (H,), ((0, 4),), -0.2, 0.2), 0.5, 1.5)
    gate_gain = jnp.clip(1.0 + 0.1 * jax.random.normal(splits[15], (DI,), jnp.float32), 0.5, 1.5)
    out_weight = bell_draw(splits[16], (DI, D), DI ** -0.5, 0.109375, ((0, 4), (1, 8)))
    adapter_down = bell_draw(splits[17], (ADAPTERS, D, RANK), D ** -0.5, 0.15625)
    adapter_inner = bell_draw(splits[18], (ADAPTERS, RANK, 2, DI), (4 * RANK) ** -0.5, 0.75, ((3, 4),))
    adapter_map = bell_draw(splits[19], (ADAPTERS, RANK, 2 * N), (4 * RANK) ** -0.5, 0.75)
    adapter_step = bell_draw(splits[20], (ADAPTERS, RANK, H), (4 * RANK) ** -0.5, 0.75, ((2, 4),))
    adapter_mixed = bell_draw(splits[21], (ADAPTERS, DI, RANK), DI ** -0.5, 0.109375, ((1, 4),))
    adapter_up = bell_draw(splits[22], (ADAPTERS, RANK, D), (4 * RANK) ** -0.5, 0.75)
    return {"layer_in": layer_in, "cotangent": cotangent, "segment_ids": segment_ids, "adapter_ids": adapter_ids, "norm_gain": norm_gain, "inner_weight": inner_weight, "map_weight": map_weight, "step_weight": step_weight, "conv_inner_weight": conv_inner_weight, "conv_inner_bias": conv_inner_bias, "conv_map_weight": conv_map_weight, "conv_map_bias": conv_map_bias, "step_bias": step_bias, "decay_log": decay_log, "skip_gain": skip_gain, "gate_gain": gate_gain, "out_weight": out_weight, "adapter_down": adapter_down, "adapter_inner": adapter_inner, "adapter_map": adapter_map, "adapter_step": adapter_step, "adapter_mixed": adapter_mixed, "adapter_up": adapter_up}


EPSILON = 1e-05
EXACT_ARITHMETIC = lax.Precision.HIGHEST

@jax.custom_vjp
def low(v):
    return lax.optimization_barrier(v.astype(jnp.bfloat16)).astype(jnp.float32)

@jax.custom_vjp
def low_back(v):
    return v

def low_keep(v):
    return (low(v), None)

def low_pass(kept, grad):
    return (grad,)

def back_keep(v):
    return (v, None)

def back_low(kept, grad):
    return (low(grad),)
low.defvjp(low_keep, low_pass)
low_back.defvjp(back_keep, back_low)

def exact_dot(left, right):
    return jnp.dot(left, right, precision=EXACT_ARITHMETIC)

def conv_reset(inputs, weight, bias, segment):
    length = inputs.shape[0]
    result = bias[None, :] + weight[0][None, :] * inputs
    for lag in range(1, weight.shape[0]):
        moved = jnp.concatenate([jnp.zeros((lag, inputs.shape[1]), inputs.dtype), inputs[:length - lag]], axis=0)
        moved_segment = jnp.concatenate([jnp.full((lag,), -1, jnp.int32), segment[:length - lag]], axis=0)
        keep = (moved_segment == segment)[:, None]
        result = result + weight[lag][None, :] * jnp.where(keep, moved, 0.0)
    return result

def state_space(values, step, rate, in_map, out_map, segment):
    length, heads, width = values.shape
    blocks = length // BLOCK
    value_blocks = values.reshape(blocks, BLOCK, heads, width)
    step_blocks = step.reshape(blocks, BLOCK, heads)
    in_blocks = in_map.reshape(blocks, BLOCK, -1)
    out_blocks = out_map.reshape(blocks, BLOCK, -1)
    segment_blocks = segment.reshape(blocks, BLOCK)
    log_decay = jnp.cumsum(step_blocks * rate, axis=1)
    block_total = log_decay[:, -1, :]
    last_segment = segment_blocks[:, -1]
    own = (segment_blocks == last_segment[:, None])[:, :, None]
    to_end = jnp.where(own, jnp.exp(block_total[:, None, :] - log_decay), 0.0) * step_blocks
    block_states = jnp.einsum('csn,cshp->chnp', in_blocks, to_end[..., None] * value_blocks, precision=EXACT_ARITHMETIC)
    before_segment = jnp.concatenate([jnp.full((1,), -1, jnp.int32), last_segment[:-1]])
    propagated_multiplier = jnp.where((last_segment == before_segment)[:, None], jnp.exp(block_total), 0.0)

    def advance(state, inputs):
        return (inputs[1][:, None, None] * state + inputs[0], state)
    _, incoming = lax.scan(advance, jnp.zeros_like(block_states[0]), (block_states, propagated_multiplier))
    causal = jnp.arange(BLOCK)[:, None] >= jnp.arange(BLOCK)[None, :]

    def one_block(inputs):
        value_part, step_part, in_part, out_part, segment_part, decay_part, state_part, prior_segment = inputs
        scores = jnp.dot(out_part, in_part.T, precision=EXACT_ARITHMETIC)
        allowed = (causal & (segment_part[:, None] == segment_part[None, :]))[:, :, None]
        spread = jnp.where(allowed, decay_part[:, None, :] - decay_part[None, :, :], 0.0)
        mixing = jnp.where(allowed, jnp.exp(spread), 0.0) * scores[:, :, None] * step_part[None, :, :]
        inside_segment = jnp.einsum('tsh,shp->thp', mixing, value_part, precision=EXACT_ARITHMETIC)
        enter = jnp.where((segment_part == prior_segment)[:, None], jnp.exp(decay_part), 0.0)
        carried = jnp.einsum('tn,hnp->thp', out_part, state_part, precision=EXACT_ARITHMETIC) * enter[:, :, None]
        return inside_segment + carried
    outputs = lax.map(jax.checkpoint(one_block), (value_blocks, step_blocks, in_blocks, out_blocks, segment_blocks, log_decay, incoming, before_segment))
    return outputs.reshape(length, heads, width)

def block_forward(row, tables, segment, pick, frozen):
    adapter_down, adapter_inner, adapter_map, adapter_step, adapter_mixed, adapter_up = tables
    norm_gain, inner_weight, map_weight, step_weight, conv_inner_weight, conv_inner_bias, conv_map_weight, conv_map_bias, step_bias, decay_log, skip_gain, gate_gain, out_weight = frozen
    length = row.shape[0]
    normed = low(row * lax.rsqrt(lax.optimization_barrier(jnp.mean(row * row, axis=-1, keepdims=True)) + EPSILON) * norm_gain)
    adapter_low = exact_dot(normed, adapter_down[pick])
    proj_inner = low_back(jnp.einsum('ld,dkc->lkc', normed, inner_weight, precision=EXACT_ARITHMETIC) + jnp.einsum('lr,rkc->lkc', adapter_low, adapter_inner[pick], precision=EXACT_ARITHMETIC))
    proj_map = exact_dot(normed, map_weight) + exact_dot(adapter_low, adapter_map[pick])
    proj_step = low_back(exact_dot(normed, step_weight) + exact_dot(adapter_low, adapter_step[pick]))
    values_low = low(jax.nn.silu(conv_reset(proj_inner[:, 1], conv_inner_weight, conv_inner_bias, segment)))
    maps_conv = jax.nn.silu(conv_reset(proj_map, conv_map_weight, conv_map_bias, segment))
    in_map = low(maps_conv[:, :N])
    out_map = low(maps_conv[:, N:])
    step = jax.nn.softplus(proj_step + step_bias)
    heads = values_low.reshape(length, H, P_SIZE)
    ssd_out = state_space(heads, step, -jnp.exp(decay_log), in_map, out_map, segment) + skip_gain[:, None] * heads
    gated = ssd_out.reshape(length, DI) * jax.nn.silu(proj_inner[:, 0])
    blended_values = low(gated * lax.rsqrt(lax.optimization_barrier(jnp.mean(gated * gated, axis=-1, keepdims=True)) + EPSILON) * gate_gain)
    blended_lowrank = exact_dot(blended_values, adapter_mixed[pick])
    return row + exact_dot(blended_values, out_weight) + exact_dot(blended_lowrank, adapter_up[pick])

def reference(layer_in, cotangent, segment_ids, adapter_ids, norm_gain, inner_weight, map_weight, step_weight, conv_inner_weight, conv_inner_bias, conv_map_weight, conv_map_bias, step_bias, decay_log, skip_gain, gate_gain, out_weight, adapter_down, adapter_inner, adapter_map, adapter_step, adapter_mixed, adapter_up):
    frozen = tuple((item.astype(jnp.float32) for item in (norm_gain, inner_weight, map_weight, step_weight, conv_inner_weight, conv_inner_bias, conv_map_weight, conv_map_bias, step_bias, decay_log, skip_gain, gate_gain, out_weight)))
    tables = tuple((item.astype(jnp.float32) for item in (adapter_down, adapter_inner, adapter_map, adapter_step, adapter_mixed, adapter_up)))

    def one_sequence(totals, inputs):
        row, row_cotangent, segment, pick = inputs

        def run(row_in, tables_in):
            return block_forward(row_in, tables_in, segment, pick, frozen)
        result, pull_back = jax.vjp(run, row.astype(jnp.float32), tables)
        row_grad, table_grads = pull_back(row_cotangent.astype(jnp.float32))
        totals = tuple((summed + extra for summed, extra in zip(totals, table_grads)))
        return (totals, (result.astype(jnp.bfloat16), row_grad))
    start = tuple((jnp.zeros_like(item) for item in tables))
    totals, (layer_out, input_grad) = lax.scan(one_sequence, start, (layer_in, cotangent, segment_ids, adapter_ids))
    return (layer_out, input_grad, totals[0], totals[1], totals[2], totals[3], totals[4], totals[5])
```

```python
import functools

import jax
import jax.numpy as jnp
from jax import lax
from jax.experimental import pallas as pl
from jax.experimental.pallas import tpu as pltpu
from jax.sharding import PartitionSpec as P

EPSILON = 1e-05
HALO = 16
CHUNK = 128
COLS = 256
DOC_MOST = 800
LOG2E = 1.4426950408889634
F32 = jnp.float32
BF16 = jnp.bfloat16
EXACT = lax.Precision.HIGHEST


def dot(a, b, precision=None):
    return lax.dot_general(
        a, b, (((1,), (0,)), ((), ())), precision=precision, preferred_element_type=F32
    )


def dot_nt(a, b, precision=None):
    return lax.dot_general(
        a, b, (((1,), (1,)), ((), ())), precision=precision, preferred_element_type=F32
    )


def sigmoid(v):
    return 0.5 * jnp.tanh(0.5 * v) + 0.5


def split3(v):
    hi = v.astype(BF16)
    rest = v - hi.astype(F32)
    mid = rest.astype(BF16)
    lo = (rest - mid.astype(F32)).astype(BF16)
    return jnp.concatenate([hi, mid, lo], axis=1)


def spread_matrix(heads, cols, base, width):
    k = lax.broadcasted_iota(jnp.int32, (3 * heads, cols), 0)
    k = jnp.where(k >= 2 * heads, k - 2 * heads, jnp.where(k >= heads, k - heads, k))
    l = lax.broadcasted_iota(jnp.int32, (3 * heads, cols), 1)
    return jnp.where(k == base + l // width, 1.0, 0.0).astype(BF16)


def row_matrix(heads, rows, base):
    k = lax.broadcasted_iota(jnp.int32, (rows, 3 * heads), 1)
    k = jnp.where(k >= 2 * heads, k - 2 * heads, jnp.where(k >= heads, k - heads, k))
    i = lax.broadcasted_iota(jnp.int32, (rows, 3 * heads), 0)
    return jnp.where(k == base + i, 1.0, 0.0).astype(BF16)


def gather_matrix(cols, base, width):
    l = lax.broadcasted_iota(jnp.int32, (cols, 128), 0)
    lane = lax.broadcasted_iota(jnp.int32, (cols, 128), 1)
    return jnp.where(lane == base + l // width, 1.0, 0.0).astype(BF16)


def two_heads(v, lane_low):
    return jnp.concatenate(
        [jnp.where(lane_low, v, 0.0), jnp.where(lane_low, 0.0, v)], axis=0
    ).astype(BF16)


def triangle(strict_lower=False, upper=False):
    r = lax.broadcasted_iota(jnp.int32, (CHUNK, CHUNK), 0)
    c = lax.broadcasted_iota(jnp.int32, (CHUNK, CHUNK), 1)
    keep = (r <= c) if upper else ((r > c) if strict_lower else (r >= c))
    return jnp.where(keep, 1.0, 0.0)


def conv_forward(buffer, tokens, weight, bias, cols):
    result = bias + weight[0:1] * buffer[HALO : HALO + tokens, :]
    for lag in range(1, 4):
        moved = buffer[HALO - lag : HALO - lag + tokens, :]
        result = result + weight[lag : lag + 1] * (moved * cols[:, lag - 1 : lag])
    return result


def front_kernel(
    heads, groups, x, gain, down, mw, sw, amap, astep, cmw, cmb, sbias, dlog, cols,
    nrm, scale, low, maps, pre_map, quant, step_out, sig_out, buffer,
):
    tokens = maps.shape[0]
    xf = x[...].astype(F32)
    q = lax.rsqrt(jnp.mean(xf * xf, axis=-1, keepdims=True) + EPSILON)
    normed = (xf * q * gain[...]).astype(BF16)
    scale[...] = jnp.broadcast_to(q[HALO:], scale.shape)
    width = normed.shape[1] // groups
    for g in range(groups):
        nrm[g] = normed[:, g * width : (g + 1) * width]
    adapter_low = dot(normed, down[...]).astype(BF16)
    low[...] = adapter_low
    buffer[...] = dot(normed, mw[...]) + dot(adapter_low, amap[...])
    pre = conv_forward(buffer, tokens, cmw[...], cmb[...], cols[...])
    pre_map[...] = pre
    maps[...] = (pre * sigmoid(pre)).astype(BF16)
    raw = dot(normed[HALO:], sw[...]) + dot(adapter_low[HALO:], astep[...]) + sbias[...]
    step = jnp.maximum(raw, 0.0) + jnp.log(1.0 + jnp.exp(-jnp.abs(raw)))
    step_out[...] = step
    sig_out[...] = sigmoid(raw)
    rate = -jnp.exp(dlog[...])
    drop = step * rate * LOG2E
    lower = triangle()
    sums = []
    for c in range(tokens // CHUNK):
        sums.append(dot(lower, drop[c * CHUNK : (c + 1) * CHUNK], precision=EXACT))
    base = jnp.zeros_like(sums[0][0:1])
    bases = []
    for c in range(tokens // CHUNK):
        bases.append(base)
        base = base + sums[c][CHUNK - 1 : CHUNK]
    column = cols[...]
    cum = jnp.concatenate(sums, axis=0)
    whole = jnp.concatenate([s + b for s, b in zip(sums, bases)], axis=0)
    left = jnp.concatenate([s[CHUNK - 1 : CHUNK] - s for s in sums], axis=0)
    quant[0] = split3(cum)
    quant[1] = split3(step)
    quant[2] = split3(jnp.exp2(cum) * column[:, 3:4])
    quant[3] = split3(jnp.exp2(left) * column[:, 4:5])
    quant[4] = split3(jnp.exp2(whole) * column[:, 5:6])
    quant[5] = split3(jnp.exp2(base - whole) * column[:, 6:7])


def chunk_rows(c):
    return slice(c * CHUNK, (c + 1) * CHUNK)


def allowed_mask(cols, rows, c, transposed=False):
    r = lax.broadcasted_iota(jnp.int32, (CHUNK, CHUNK), 0)
    l = lax.broadcasted_iota(jnp.int32, (CHUNK, CHUNK), 1)
    same = cols[chunk_rows(c), 7:8] == rows[0:1, chunk_rows(c)]
    return same & ((r <= l) if transposed else (r >= l))


def project(total, nrm, lead, w_refs, shift, skip_rows=0):
    index = 0
    for ref in w_refs:
        for g in range(ref.shape[0]):
            part = nrm[index ^ shift] if lead > 1 else nrm[0]
            total = total + dot(part[skip_rows:], ref[g, 0])
            index += 1
    return total


def values_kernel(
    heads, n_w, scalars, nrm, low, aw, cw, cb, maps, quant, cols, rows, *rest
):
    w_refs = rest[:n_w]
    values, pre_out, y_out, s_out, masked, in_t, buffer = rest[n_w:]
    j = pl.program_id(0)
    tokens = maps.shape[0]
    chunks = tokens // CHUNK
    n = maps.shape[1] // 2

    @pl.when(j == 0)
    def _():
        for c in range(chunks):
            b = maps[chunk_rows(c), :n]
            scores = dot_nt(maps[chunk_rows(c), n:], b)
            masked[c] = jnp.where(allowed_mask(cols, rows, c), scores, 0.0)
            in_t[c] = b.astype(F32).T.astype(BF16)

    base = scalars[1 + j // scalars[5]] * scalars[5] + lax.rem(j, scalars[5])
    base = base * (COLS // 64)
    buffer[...] = project(dot(low[...], aw[...]), nrm, nrm.shape[0], w_refs, scalars[0])
    pre = conv_forward(buffer, tokens, cw[...], cb[...], cols[...])
    pre_out[...] = pre.astype(BF16)
    v = (pre * sigmoid(pre)).astype(BF16)
    values[...] = v
    wide = spread_matrix(heads, COLS, base, 64)
    v = v.astype(F32)
    vp = dot(quant[1], wide) * v
    row = dot_nt(row_matrix(heads, 8, base), quant[0])
    lane_low = lax.broadcasted_iota(jnp.int32, (CHUNK, 128), 1) < 64
    pair_wide = [spread_matrix(heads, 2 * CHUNK, base + 2 * p, CHUNK) for p in range(2)]
    state = None
    for c in range(chunks):
        rs = chunk_rows(c)
        cum_c = quant[0, rs]
        mask2 = jnp.concatenate([masked[c], masked[c]], axis=1)
        inside = []
        for p in range(2):
            r2 = jnp.concatenate([row[2 * p : 2 * p + 1, rs], row[2 * p + 1 : 2 * p + 2, rs]], axis=1)
            decay = jnp.exp2(jnp.minimum(dot(cum_c, pair_wide[p]) - r2, 0.0))
            vbd = two_heads(vp[rs, p * 128 : (p + 1) * 128], lane_low)
            inside.append(dot((decay * mask2).astype(BF16), vbd))
        y = jnp.concatenate(inside, axis=1)
        enter = dot(quant[2, rs], wide)
        if c > 0:
            y = y + enter * dot(maps[rs, n:], state.astype(BF16))
        y_out[rs] = y.astype(y_out.dtype)
        end = dot(quant[3, rs], wide)
        fresh = dot(in_t[c], (end * vp[rs]).astype(BF16))
        state = fresh if c == 0 else state * enter[CHUNK - 1 : CHUNK] + fresh
    s_out[...] = state.astype(s_out.dtype)


def gate_kernel(
    heads, n_w, count, scalars, nrm, low, aw, maps, quant, y_in, values, s_in, skip, gain, *rest
):
    w_refs = rest[:n_w]
    gate_out, y_out, gg_out, r_out, squares = rest[n_w:]
    j = pl.program_id(0)
    n = maps.shape[1] // 2
    base = scalars[1 + j // scalars[5]] * scalars[5] + lax.rem(j, scalars[5])
    base = base * (COLS // 64)
    gate = project(
        dot(low[HALO:], aw[...]), nrm, nrm.shape[0], w_refs, scalars[0], skip_rows=HALO
    )
    wide = spread_matrix(heads, COLS, base, 64)
    carry = dot(quant[0], wide) * dot(maps[:, n:], s_in[...])
    y = y_in[...].astype(F32) + carry + skip[...] * values[...].astype(F32)
    gated = y * (gate * sigmoid(gate))
    gate_out[...] = gate.astype(BF16)
    y_out[...] = y.astype(BF16)
    gg_out[...] = (gated * gain[...]).astype(BF16)
    part = jnp.sum(gated * gated, axis=-1, keepdims=True)

    @pl.when(j == 0)
    def _():
        squares[...] = jnp.zeros_like(squares)

    squares[...] += part

    @pl.when(j == count - 1)
    def _():
        mean = squares[...] / (count * COLS)
        r_out[...] = jnp.broadcast_to(lax.rsqrt(mean + EPSILON), r_out.shape)


def gated_kernel(
    heads, n_w, count, scalars, cot, up, amixed, gg, gate, y_in, gain, r_in, quant, maps, *rest
):
    w_refs = rest[:n_w]
    gy_out, gz_out, gml_out, g_out, grad, inner, cot_parts, out_t = rest[n_w:]
    j = pl.program_id(0)
    n = maps.shape[1] // 2
    groups = cot_parts.shape[0]
    width = cot_parts.shape[2]

    @pl.when(j == 0)
    def _():
        gml_out[...] = dot_nt(cot[...], up[...])
        inner[...] = jnp.zeros_like(inner)
        for g in range(groups):
            cot_parts[g] = cot[:, g * width : (g + 1) * width]
        out_t[...] = maps[:, n:].astype(F32).T.astype(BF16)

    @pl.when(j < count)
    def _():
        first = dot(gml_out[...].astype(BF16), amixed[...])
        total = project(first, cot_parts, groups, w_refs, scalars[0])
        grad[j] = total
        inner[...] += jnp.sum(gg[...].astype(F32) * total, axis=-1, keepdims=True)

    @pl.when(j >= count)
    def _():
        i = j - count
        base = scalars[1 + i // scalars[5]] * scalars[5] + lax.rem(i, scalars[5])
        base = base * (COLS // 64)
        r = r_in[:, 0:1]
        mean = inner[...] / (count * COLS)
        g = gate[...].astype(F32)
        y = y_in[...].astype(F32)
        s = sigmoid(g)
        act = g * s
        gated = y * act
        grad_gated = (grad[i] * gain[...]) * r - gated * (r * r * r * mean)
        gy = grad_gated * act
        gy_out[...] = gy.astype(BF16)
        gz_out[...] = (grad_gated * y * (s * (1.0 + g * (1.0 - s)))).astype(BF16)
        enter = dot(quant[0], spread_matrix(heads, COLS, base, 64))
        g_out[...] = dot(out_t[...], (enter * gy).astype(BF16)).astype(g_out.dtype)


def backward_kernel(
    heads, count, scalars, values, gy_in, s_in, maps, quant, cols, rows,
    dx_out, gmaps_out, r_out, masked, allowed, mixed, grad_b, grad_c, col_p, row_p, carry_a, carry_b, ends,
    in_b, out_b,
):
    j = pl.program_id(0)
    tokens = maps.shape[0]
    chunks = tokens // CHUNK
    n = maps.shape[1] // 2

    @pl.when(j == 0)
    def _():
        for c in range(chunks):
            rs = chunk_rows(c)
            ok = allowed_mask(cols, rows, c, transposed=True)
            scores = dot_nt(maps[rs, :n], maps[rs, n:])
            masked[c] = jnp.where(ok, scores, 0.0)
            allowed[c] = jnp.where(ok, 1.0, 0.0)
            in_b[c] = maps[rs, :n].astype(F32).T.astype(BF16)
            out_b[c] = maps[rs, n:].astype(F32).T.astype(BF16)
        for ref in (mixed, grad_b, grad_c, col_p, row_p, carry_a, carry_b, ends):
            ref[...] = jnp.zeros_like(ref)

    base = scalars[1 + j // scalars[5]] * scalars[5] + lax.rem(j, scalars[5])
    base = base * (COLS // 64)
    wide = spread_matrix(heads, COLS, base, 64)
    v = values[...].astype(F32)
    vp = dot(quant[1], wide) * v
    row = dot_nt(row_matrix(heads, 8, base), quant[0])
    pair_wide = [spread_matrix(heads, 2 * CHUNK, base + 2 * p, CHUNK) for p in range(2)]
    pair_sum = [gather_matrix(2 * CHUNK, base + 2 * p, CHUNK) for p in range(2)]
    head_sum = gather_matrix(COLS, base, 64)
    lane_low = lax.broadcasted_iota(jnp.int32, (CHUNK, 128), 1) < 64
    enters, lefts, states = [], [], []
    state = s_in[...].astype(F32)
    for c in range(chunks):
        rs = chunk_rows(c)
        enters.append(dot(quant[2, rs], wide))
        lefts.append(dot(quant[3, rs], wide))
        states.append(state)
        if c < chunks - 1:
            fresh = dot(in_b[c], (lefts[c] * vp[rs]).astype(BF16))
            state = state * enters[c][CHUNK - 1 : CHUNK] + fresh
    sub = lax.broadcasted_iota(jnp.int32, (heads, CHUNK), 0)
    adjoint = None
    for c in range(chunks - 1, -1, -1):
        rs = chunk_rows(c)
        cum_c = quant[0, rs]
        gy = gy_in[rs].astype(F32)
        mask2 = jnp.concatenate([masked[c], masked[c]], axis=1)
        dx = []
        for p in range(2):
            lanes = slice(p * 128, (p + 1) * 128)
            r2 = jnp.concatenate([row[2 * p : 2 * p + 1, rs], row[2 * p + 1 : 2 * p + 2, rs]], axis=1)
            decay = jnp.exp2(jnp.minimum(r2 - dot(cum_c, pair_wide[p]), 0.0))
            gbd = two_heads(gy[:, lanes], lane_low)
            dx.append(dot((decay * mask2).astype(BF16), gbd))
            part = decay * dot_nt(vp[rs, lanes].astype(BF16), gbd)
            mixed[c] += part[:, :CHUNK] + part[:, CHUNK:]
            weighed = (part * mask2).astype(BF16)
            col_p[rs] += dot(weighed, pair_sum[p])
            for q in range(2):
                pick = jnp.where(sub == base + 2 * p + q, 1.0, 0.0).astype(BF16)
                row_p[:, rs] += dot(pick, weighed[:, q * CHUNK : (q + 1) * CHUNK])
        dx = jnp.concatenate(dx, axis=1)
        entering = enters[c] * gy
        carried = entering * dot(maps[rs, n:], states[c].astype(BF16))
        carry_a[rs] += dot(carried.astype(BF16), head_sum)
        entering = entering.astype(BF16)
        grad_c[rs] += dot_nt(entering, states[c].astype(BF16))
        if adjoint is not None:
            adj = adjoint.astype(BF16)
            leaving = lefts[c] * dot(maps[rs, :n], adj)
            dx = dx + leaving
            carry_b[rs] += dot((vp[rs] * leaving).astype(BF16), head_sum)
            grad_b[rs] += dot_nt((lefts[c] * vp[rs]).astype(BF16), adj)
            last = enters[c][CHUNK - 1 : CHUNK]
            through = jnp.sum(adjoint * states[c], axis=0, keepdims=True) * last
            ends[c * 8 : c * 8 + 8] += dot(
                jnp.broadcast_to(through, (8, COLS)), head_sum.astype(F32), precision=EXACT
            )
        dx_out[rs] = dx.astype(dx_out.dtype)
        if c > 0:
            fresh = dot(out_b[c], entering)
            adjoint = fresh if adjoint is None else adjoint * last + fresh

    @pl.when(j == count - 1)
    def _():
        suffix = triangle(upper=True)
        prefix = triangle(strict_lower=True)
        for c in range(chunks):
            rs = chunk_rows(c)
            w = mixed[c] * allowed[c]
            gb = grad_b[rs] + dot(w.astype(BF16), maps[rs, n:])
            gc = grad_c[rs] + dot(w.T.astype(BF16), maps[rs, :n])
            gmaps_out[rs] = jnp.concatenate([gb, gc], axis=1)
            rowsum = jnp.concatenate(
                [row_p[:, rs].T, jnp.zeros((CHUNK, 128 - heads), F32)], axis=1
            )
            first = rowsum - col_p[rs] + carry_a[rs]
            r_out[rs] = (
                dot(suffix, first, precision=EXACT)
                + dot(prefix, carry_b[rs], precision=EXACT)
                + ends[c * 8 : c * 8 + 1]
            )


def finish_kernel(
    heads, count, scalars, values, dx_in, gy_in, pre, g_in, s_in, maps, quant, skip, gmaps, r_in, sig, dlog, pre_map,
    c_out, cmap_out, gstep_out, col_g, carry_b, grad_b, ends,
):
    j = pl.program_id(0)
    tokens = maps.shape[0]
    n = maps.shape[1] // 2
    base = scalars[1 + j // scalars[5]] * scalars[5] + lax.rem(j, scalars[5])
    base = base * (COLS // 64)

    @pl.when(j == 0)
    def _():
        for ref in (col_g, carry_b, grad_b, ends):
            ref[...] = jnp.zeros_like(ref)

    wide = spread_matrix(heads, COLS, base, 64)
    head_sum = gather_matrix(COLS, base, 64)
    v = values[...].astype(F32)
    step = dot(quant[0], wide)
    left = dot(quant[2], wide)
    vp = step * v
    adjoint = g_in[...]
    more = left * dot(maps[:, :n], adjoint)
    dx = dx_in[...].astype(F32) + more
    carry_b[...] += dot((vp * more).astype(BF16), head_sum)
    col_g[...] += dot((v * dx).astype(BF16), head_sum)
    grad_b[...] += dot_nt((left * vp).astype(BF16), adjoint)
    last = dot(quant[1, tokens - 16 :], wide)[15:16]
    through = jnp.sum(adjoint.astype(F32) * s_in[...].astype(F32), axis=0, keepdims=True) * last
    ends[...] += dot(jnp.broadcast_to(through, (8, COLS)), head_sum.astype(F32), precision=EXACT)
    dv = step * dx + skip[...] * gy_in[...].astype(F32)
    pre_f = pre[...].astype(F32)
    s = sigmoid(pre_f)
    c_out[...] = (dv * (s * (1.0 + pre_f * (1.0 - s)))).astype(BF16)

    @pl.when(j == count - 1)
    def _():
        prefix = triangle(strict_lower=True)
        run = ends[0:1]
        rate = -jnp.exp(dlog[...])
        for c in range(tokens // CHUNK):
            rs = chunk_rows(c)
            total = r_in[rs] + dot(prefix, carry_b[rs], precision=EXACT) + run
            run = run + jnp.sum(carry_b[rs], axis=0, keepdims=True)
            raw = (col_g[rs][:, :heads] + rate * total[:, :heads]) * sig[rs]
            gstep_out[rs] = raw.astype(BF16)
        gb = gmaps[:, :n] + grad_b[...]
        g = jnp.concatenate([gb, gmaps[:, n:]], axis=1)
        pm = pre_map[...]
        sm = sigmoid(pm)
        cmap_out[...] = (g * (sm * (1.0 + pm * (1.0 - sm)))).astype(cmap_out.dtype)


def conv_backward(buffer, tokens, weight, cols):
    result = weight[0:1] * buffer[0:tokens, :]
    for lag in range(1, 4):
        result = result + weight[lag : lag + 1] * (
            buffer[lag : lag + tokens, :] * cols[:, 7 + lag : 8 + lag]
        )
    return result


def tables_kernel(
    count, groups, c_in, c_halo, cmap, cmap_halo, gz, cw, cmw, agate, ainner, amap, astep, gstep, low, nrm, cols,
    gi_out, gmap_out, glow_out, tab_gate, tab_inner, tab_map, tab_step, tab_down, buffer, glow, low_t,
):
    j = pl.program_id(0)
    tokens = gi_out.shape[0]

    @pl.when(j == 0)
    def _():
        low_t[...] = low[HALO:].astype(F32).T.astype(BF16)
        buffer[:tokens] = cmap[...].astype(F32)
        buffer[tokens:] = cmap_halo[...].astype(F32)
        gmap = conv_backward(buffer, tokens, cmw[...], cols[...]).astype(BF16)
        gmap_out[...] = gmap
        tab_map[...] = dot(low_t[...], gmap)
        tab_step[...] = dot(low_t[...], gstep[...])
        glow[...] = dot_nt(gmap, amap[...]) + dot_nt(gstep[...], astep[...])

    buffer[:tokens] = c_in[...].astype(F32)
    buffer[tokens:] = c_halo[...].astype(F32)
    gi = conv_backward(buffer, tokens, cw[...], cols[...]).astype(BF16)
    gi_out[...] = gi
    glow[...] += dot_nt(gi, ainner[...]) + dot_nt(gz[...], agate[...])
    tab_gate[...] = dot(low_t[...], gz[...])
    tab_inner[...] = dot(low_t[...], gi)

    @pl.when(j == count - 1)
    def _():
        gl = glow[...].astype(BF16)
        glow_out[...] = gl
        gl_t = glow[...].T.astype(BF16)
        for g in range(groups):
            tab_down[g] = dot(gl_t, nrm[g, HALO:])


def assemble(parts, out_ref, finish):
    groups, tokens, width = parts.shape
    out_ref[...] = finish(jnp.concatenate([parts[g] for g in range(groups)], axis=1))


def back_gate_kernel(n_w, scalars, gz, *rest):
    w_refs = rest[:n_w]
    (out,) = rest[n_w:]
    total = None
    for k in range(w_refs[0].shape[0]):
        slot = scalars[1 + k]
        term = dot_nt(gz[slot], w_refs[0][k])
        total = term if total is None else total + term
    out[...] = total


def out_kernel(count, scalars, x, gg, w, amixed, up, r_in, gml, cot, out, tab_up, tab_mixed, parts):
    j = pl.program_id(0)
    total = None
    for k in range(w.shape[1]):
        term = dot_nt(gg[scalars[1 + k]], w[0, k])
        total = term if total is None else total + term
    parts[j ^ scalars[0]] = total

    @pl.when(j == count - 1)
    def _():
        r = r_in[:, 0:1]
        low = None
        for z in range(gg.shape[0]):
            term = dot_nt(gg[z], amixed[z])
            low = term if low is None else low + term
        low = low * r
        scaled = (gml[...] * r).T.astype(BF16)
        for z in range(gg.shape[0]):
            tab_mixed[z] = dot(scaled, gg[z])
        tab_up[...] = dot(low.T.astype(BF16), cot[...])
        extra = dot(low.astype(BF16), up[...])
        assemble(parts, out, lambda v: (x[...].astype(F32) + v * r + extra).astype(BF16))


def input_kernel(
    count, scalars, gz, gi, wg, wi, gmap, gstep, glow, mw, sw, down, x, cot, scale, gain, out, parts
):
    j = pl.program_id(0)
    total = (
        dot_nt(gmap[...], mw[0]) + dot_nt(gstep[...], sw[0]) + dot_nt(glow[...], down[0])
    )
    for k in range(wg.shape[1]):
        slot = scalars[1 + k]
        total = total + dot_nt(gz[slot], wg[0, k]) + dot_nt(gi[slot], wi[0, k])
    parts[j ^ scalars[0]] = total

    @pl.when(j == count - 1)
    def _():
        q = scale[:, 0:1]
        xf = x[...].astype(F32)

        def finish(v):
            weighted = v * gain[...]
            mean = jnp.mean(xf * weighted, axis=-1, keepdims=True)
            return q * weighted - xf * (q * q * q * mean) + cot[...].astype(F32)

        assemble(parts, out, finish)


def whole(shape):
    return pl.BlockSpec(shape, lambda *_: (0,) * len(shape))


def call(kernel, grid, in_specs, out_specs, out_shape, scratch, flops, traffic, prefetch=1):
    return pl.pallas_call(
        kernel,
        grid_spec=pltpu.PrefetchScalarGridSpec(
            num_scalar_prefetch=prefetch,
            grid=grid,
            in_specs=in_specs,
            out_specs=out_specs,
            scratch_shapes=scratch,
        ),
        out_shape=out_shape,
        compiler_params=pltpu.CompilerParams(
            dimension_semantics=("arbitrary",) * len(grid), vmem_limit_bytes=56 * 2**20
        ),
        cost_estimate=pl.CostEstimate(
            flops=int(flops), bytes_accessed=int(traffic), transcendentals=0
        ),
    )


def shape(dims, kind):
    return jax.ShapeDtypeStruct(dims, kind)


def gather_rows(block, ndp, nz):
    rows, columns = block.shape
    everything = lax.all_gather(block, ("dp", "tensor")).reshape(ndp, nz, rows, columns)
    if rows % 64:
        everything = jnp.swapaxes(everything, 0, 1).reshape(1, nz, ndp * rows, columns)
    return everything


def shards(
    layer_in,
    cotangent,
    segment_ids,
    adapter_ids,
    norm_gain,
    inner_weight,
    map_weight,
    step_weight,
    conv_inner_weight,
    conv_inner_bias,
    conv_map_weight,
    conv_map_bias,
    step_bias,
    decay_log,
    skip_gain,
    gate_gain,
    out_weight,
    adapter_down,
    adapter_inner,
    adapter_map,
    adapter_step,
    adapter_mixed,
    adapter_up,
):
    ndp, nz = lax.axis_size("dp"), lax.axis_size("tensor")
    z = lax.axis_index("tensor")
    x, cot = layer_in[0], cotangent[0]
    tokens, width = x.shape
    rows_here = inner_weight.shape[0]
    part = gate_gain.shape[0]
    inner = part * nz
    heads_here = step_bias.shape[0]
    heads = heads_here * nz
    adapters, _, rank = adapter_down.shape
    n2 = map_weight.shape[1]
    n = n2 // 2
    count = inner // COLS
    chunks = tokens // CHUNK
    seq = segment_ids.shape[1]
    up_one = [(i, i + 1) for i in range(nz - 1)]
    down_one = [(i + 1, i) for i in range(nz - 1)]

    halo = lax.ppermute(x[tokens - HALO :], "tensor", up_one)
    x_ext = jnp.concatenate([halo, x], axis=0)
    w_inner = gather_rows(inner_weight[:, 1], ndp, nz)
    pick = adapter_ids[0]
    astep_here = adapter_step[pick]
    thin = jnp.concatenate([step_weight, astep_here], axis=0)
    thin = lax.all_gather(thin, "tensor", axis=1, tiled=True)
    small = jnp.concatenate([map_weight, thin[:rows_here]], axis=1)
    small = lax.all_gather(small, "dp", axis=0, tiled=True)
    map_full, step_full = small[:, :n2], small[:, n2:]
    astep = thin[rows_here:]
    packed = jnp.concatenate(
        [
            conv_inner_weight,
            conv_inner_bias[None],
            gate_gain[None],
            jnp.pad(
                jnp.concatenate([step_bias, decay_log, skip_gain])[None],
                ((0, 0), (0, part - 3 * heads_here)),
            ),
        ],
        axis=0,
    )
    packed = lax.all_gather(packed, "tensor")
    wide_rows = jnp.swapaxes(packed[:, :6], 0, 1).reshape(6, inner)
    conv_w, conv_b, gain = wide_rows[:4], wide_rows[4:5], wide_rows[5:6]
    thin_rows = packed[:, 6, : 3 * heads_here].reshape(nz, 3, heads_here)
    thin_rows = jnp.swapaxes(thin_rows, 0, 1).reshape(3, heads)
    sbias, dlog = thin_rows[0:1], thin_rows[1:2]
    skip = jnp.repeat(thin_rows[2], inner // heads)[None]
    tables = jnp.concatenate(
        [adapter_inner[pick].reshape(2 * rank, part), adapter_mixed[pick].T], axis=0
    )
    tables = lax.all_gather(tables, "tensor")
    tables = jnp.swapaxes(tables, 0, 1).reshape(3 * rank, inner)
    both = tables[: 2 * rank].reshape(rank, 2, inner)
    agate, ainner, amixed = both[:, 0], both[:, 1], tables[2 * rank :]
    down, amap, up = adapter_down[pick], adapter_map[pick], adapter_up[pick]
    w_gate = gather_rows(inner_weight[:, 0], ndp, nz)
    w_out = gather_rows(out_weight.T, ndp, nz)
    groups, _, group_rows, _ = w_inner.shape
    scalars = jnp.array([0] + list(range(nz)) + [part // COLS], jnp.int32)

    segment = segment_ids[0]
    padded = jnp.pad(segment, (HALO, HALO), constant_values=-1)
    near = lax.dynamic_slice(padded, (z * tokens,), (tokens + 2 * HALO,))
    own = near[HALO : HALO + tokens]
    blocks = own.reshape(chunks, CHUNK)
    before = jnp.concatenate([near[HALO - 1 : HALO], blocks[:-1, -1]])
    columns = [near[HALO - k : HALO - k + tokens] == own for k in (1, 2, 3)]
    columns += [
        (blocks == before[:, None]).reshape(tokens),
        (blocks == blocks[:, -1:]).reshape(tokens),
        own == near[HALO - 1],
        own == own[tokens - 1],
        own,
    ]
    columns += [near[HALO + k : HALO + k + tokens] == own for k in (1, 2, 3)]
    cols = jnp.stack([c.astype(F32) for c in columns], axis=1)
    rows = jnp.broadcast_to(own.astype(F32)[None], (8, tokens))

    ext = tokens + HALO
    nq = 3 * heads
    nrm, scale, low, maps, pre_map, quant, step, sig = call(
        lambda sc, *refs: front_kernel(heads, groups, *refs),
        (1,),
        [
            whole((ext, width)), whole((1, width)), whole((width, rank)), whole((width, n2)),
            whole((width, heads)), whole((rank, n2)), whole((rank, heads)), whole((4, n2)),
            whole((1, n2)), whole((1, heads)), whole((1, heads)), whole(cols.shape),
        ],
        [
            whole((groups, ext, width // groups)), whole((tokens, 128)), whole((ext, rank)),
            whole((tokens, n2)), whole((tokens, n2)), whole((6, tokens, nq)),
            whole((tokens, heads)), whole((tokens, heads)),
        ],
        [
            shape((groups, ext, width // groups), BF16), shape((tokens, 128), F32),
            shape((ext, rank), BF16), shape((tokens, n2), BF16), shape((tokens, n2), F32),
            shape((6, tokens, nq), BF16), shape((tokens, heads), F32), shape((tokens, heads), F32),
        ],
        [pltpu.VMEM((ext, n2), F32)],
        2 * ext * width * (n2 + heads + rank), 8e6,
    )(
        scalars, x_ext, norm_gain[None], down, map_full, step_full, amap, astep,
        conv_map_weight, conv_map_bias[None], sbias, dlog, cols,
    )

    def block_of(j, sc):
        return sc[1 + j // sc[5]] * sc[5] + lax.rem(j, sc[5])

    def by_col(height):
        return pl.BlockSpec((height, COLS), lambda j, sc: (0, block_of(j, sc)))

    def by_weight(w):
        return pl.BlockSpec(
            (w.shape[0], 1, w.shape[2], COLS), lambda j, sc: (0, j // sc[5], 0, lax.rem(j, sc[5]))
        )

    def wide_out(kind=BF16, height=tokens):
        return shape((height, inner), kind)

    values, pre, y_local, s_local = call(
        functools.partial(values_kernel, heads, 1),
        (count,),
        [
            whole(nrm.shape), whole(low.shape), by_col(rank), by_col(4), by_col(1), whole(maps.shape),
            pl.BlockSpec((4, tokens, nq), lambda j, sc: (0, 0, 0)),
            whole(cols.shape), whole(rows.shape), by_weight(w_inner),
        ],
        [by_col(tokens), by_col(tokens), by_col(tokens), by_col(n)],
        [wide_out(), wide_out(), wide_out(), wide_out(BF16, n)],
        [
            pltpu.VMEM((chunks, CHUNK, CHUNK), F32), pltpu.VMEM((chunks, n, CHUNK), BF16),
            pltpu.VMEM((ext, COLS), F32),
        ],
        2 * ext * width * inner * 2, 25e6,
    )(scalars, nrm, low, ainner, conv_w, conv_b, maps, quant, cols, rows, w_inner)

    ent_last = quant[4, tokens - 1].reshape(3, heads).astype(F32).sum(0)
    through = jnp.repeat(ent_last, inner // heads)[None]
    hops = min(nz - 1, 1 + (DOC_MOST - 2) // tokens)

    def carry(local, pairs):
        got = lax.ppermute(local, "tensor", pairs)
        total = got
        for _ in range(hops - 1):
            got = lax.ppermute((got.astype(F32) * through).astype(BF16), "tensor", pairs)
            total = (total.astype(F32) + got.astype(F32)).astype(BF16)
        return total

    s_in = carry(s_local, up_one)

    gate, y_all, gg, r_gate = call(
        functools.partial(gate_kernel, heads, 1, count),
        (count,),
        [
            whole(nrm.shape), whole(low.shape), by_col(rank), whole(maps.shape),
            pl.BlockSpec((1, tokens, nq), lambda j, sc: (4, 0, 0)),
            by_col(tokens), by_col(tokens), by_col(n), by_col(1), by_col(1), by_weight(w_gate),
        ],
        [by_col(tokens), by_col(tokens), by_col(tokens), whole((tokens, 128))],
        [wide_out(), wide_out(), wide_out(), shape((tokens, 128), F32)],
        [pltpu.VMEM((tokens, 1), F32)],
        2 * ext * width * inner, 25e6,
    )(scalars, nrm, low, agate, maps, quant, y_local, values, s_in, skip, gain, w_gate)

    def first(j, sc):
        return jnp.minimum(j, count - 1)

    def second(j, sc):
        return jnp.maximum(j - count, 0)

    def by_col_in(height, phase):
        return pl.BlockSpec((height, COLS), lambda j, sc: (0, block_of(phase(j, sc), sc)))

    gy, gz, gml, g_local = call(
        functools.partial(gated_kernel, heads, 1, count),
        (2 * count,),
        [
            whole(cot.shape), whole(up.shape), by_col_in(rank, first), by_col_in(tokens, first),
            by_col_in(tokens, second), by_col_in(tokens, second), by_col_in(1, second),
            whole((tokens, 128)), pl.BlockSpec((1, tokens, nq), lambda j, sc: (4, 0, 0)),
            whole(maps.shape),
            pl.BlockSpec(
                (w_out.shape[0], 1, w_out.shape[2], COLS),
                lambda j, sc: (0, first(j, sc) // sc[5], 0, lax.rem(first(j, sc), sc[5])),
            ),
        ],
        [
            by_col_in(tokens, second), by_col_in(tokens, second), whole((tokens, rank)),
            by_col_in(n, second),
        ],
        [wide_out(), wide_out(), shape((tokens, rank), F32), wide_out(BF16, n)],
        [
            pltpu.VMEM((count, tokens, COLS), F32), pltpu.VMEM((tokens, 1), F32),
            pltpu.VMEM((groups, tokens, width // groups), BF16), pltpu.VMEM((n, tokens), BF16),
        ],
        2 * tokens * width * inner, 25e6,
    )(scalars, cot, up, amixed, gg, gate, y_all, gain, r_gate, quant, maps, w_out)

    g_in = carry(g_local, down_one)

    dx, gmaps, r_local = call(
        functools.partial(backward_kernel, heads, count),
        (count,),
        [
            by_col(tokens), by_col(tokens), by_col(n), whole(maps.shape),
            pl.BlockSpec((4, tokens, nq), lambda j, sc: (0, 0, 0)), whole(cols.shape), whole(rows.shape),
        ],
        [by_col(tokens), whole((tokens, n2)), whole((tokens, 128))],
        [wide_out(), shape((tokens, n2), F32), shape((tokens, 128), F32)],
        [
            pltpu.VMEM((chunks, CHUNK, CHUNK), F32), pltpu.VMEM((chunks, CHUNK, CHUNK), F32),
            pltpu.VMEM((chunks, CHUNK, CHUNK), F32), pltpu.VMEM((tokens, n), F32),
            pltpu.VMEM((tokens, n), F32), pltpu.VMEM((tokens, 128), F32),
            pltpu.VMEM((heads, tokens), F32), pltpu.VMEM((tokens, 128), F32),
            pltpu.VMEM((tokens, 128), F32), pltpu.VMEM((8 * chunks, 128), F32),
            pltpu.VMEM((chunks, n, CHUNK), BF16), pltpu.VMEM((chunks, n, CHUNK), BF16),
        ],
        2 * tokens * width * inner * 3, 15e6,
    )(scalars, values, gy, s_in, maps, quant, cols, rows)

    quant_late = jnp.stack([quant[1], quant[4], quant[5]])
    c_all, cmap, gstep = call(
        functools.partial(finish_kernel, heads, count),
        (count,),
        [
            by_col(tokens), by_col(tokens), by_col(tokens), by_col(tokens), by_col(n), by_col(n),
            whole(maps.shape), whole(quant_late.shape), by_col(1), whole(gmaps.shape),
            whole(r_local.shape), whole(sig.shape), whole(dlog.shape), whole(pre_map.shape),
        ],
        [by_col(tokens), whole((tokens, n2)), whole((tokens, heads))],
        [wide_out(), shape((tokens, n2), BF16), shape((tokens, heads), BF16)],
        [
            pltpu.VMEM((tokens, 128), F32), pltpu.VMEM((tokens, 128), F32),
            pltpu.VMEM((tokens, n), F32), pltpu.VMEM((8, 128), F32),
        ],
        2 * tokens * width * inner // 2, 20e6,
    )(scalars, values, dx, gy, pre, g_in, s_in, maps, quant_late, skip, gmaps, r_local, sig, dlog, pre_map)

    c_halo = lax.ppermute(
        jnp.concatenate([c_all[:HALO], cmap[:HALO]], axis=1), "tensor", down_one
    )
    gi, gmap, glow, tab_gate, tab_inner, tab_map, tab_step, tab_down = call(
        lambda sc, *refs: tables_kernel(count, groups, *refs),
        (count,),
        [
            by_col(tokens), by_col(HALO), whole(cmap.shape), whole((HALO, n2)), by_col(tokens),
            by_col(4), whole((4, n2)), by_col(rank), by_col(rank), whole(amap.shape),
            whole(astep.shape), whole(gstep.shape), whole(low.shape), whole(nrm.shape),
            whole(cols.shape),
        ],
        [
            by_col(tokens), whole((tokens, n2)), whole((tokens, rank)), by_col(rank), by_col(rank),
            whole((rank, n2)), whole((rank, heads)), whole((groups, rank, width // groups)),
        ],
        [
            wide_out(), shape((tokens, n2), BF16), shape((tokens, rank), BF16),
            wide_out(F32, rank), wide_out(F32, rank), shape((rank, n2), F32),
            shape((rank, heads), F32), shape((groups, rank, width // groups), F32),
        ],
        [
            pltpu.VMEM((ext, COLS), F32), pltpu.VMEM((tokens, rank), F32),
            pltpu.VMEM((rank, tokens), BF16),
        ],
        2 * tokens * width * inner // 4, 10e6,
    )(
        scalars, c_all, c_halo[:, :inner], cmap, c_halo[:, inner:], gz, conv_w, conv_map_weight,
        agate, ainner, amap, astep, gstep, low, nrm, cols,
    )
    tab_down = jnp.swapaxes(tab_down, 0, 1).reshape(rank, width)

    def by_part(a):
        return jnp.swapaxes(a.reshape(a.shape[0], nz, part), 0, 1)

    def by_group(w):
        return pl.BlockSpec((1,) + w.shape[1:], lambda j, sc: (j,) + (0,) * (len(w.shape) - 1))

    gg_parts = by_part(gg)
    am_parts = by_part(amixed)
    layer_out, tab_up, tab_mixed = call(
        functools.partial(out_kernel, groups),
        (groups,),
        [
            whole(x.shape), whole(gg_parts.shape), by_group(w_out), whole(am_parts.shape),
            whole(up.shape), whole(r_gate.shape), whole(gml.shape), whole(cot.shape),
        ],
        [whole(x.shape), whole(up.shape), whole(am_parts.shape)],
        [shape(x.shape, BF16), shape(up.shape, F32), shape(am_parts.shape, F32)],
        [pltpu.VMEM((groups, tokens, width // groups), F32)],
        2 * tokens * width * inner, 20e6,
    )(scalars, x, gg_parts, w_out, am_parts, up, r_gate, gml, cot)

    gz_parts, gi_parts = by_part(gz), by_part(gi)
    mw_rows = map_full.reshape(groups, group_rows, n2)
    sw_rows = step_full.reshape(groups, group_rows, heads)
    down_rows = down.reshape(groups, group_rows, rank)
    input_grad = call(
        functools.partial(input_kernel, groups),
        (groups,),
        [
            whole(gz_parts.shape), whole(gi_parts.shape), by_group(w_gate), by_group(w_inner),
            whole(gmap.shape), whole(gstep.shape), whole(glow.shape), by_group(mw_rows),
            by_group(sw_rows), by_group(down_rows), whole(x.shape), whole(cot.shape),
            whole(scale.shape), whole((1, width)),
        ],
        whole(x.shape),
        shape(x.shape, F32),
        [pltpu.VMEM((groups, tokens, width // groups), F32)],
        2 * tokens * width * inner * 2, 25e6,
    )(
        scalars, gz_parts, gi_parts, w_gate, w_inner, gmap, gstep, glow, mw_rows, sw_rows, down_rows,
        x, cot, scale, norm_gain[None],
    )

    def fold(per_sequence):
        picked = lax.all_gather(pick, "dp")
        hot = (picked[:, None] == jnp.arange(adapters)[None, :]).astype(F32)
        return jnp.einsum("sa,s...->a...", hot, per_sequence, precision=EXACT)

    shared = jnp.concatenate([tab_down, tab_up, tab_map], axis=1)
    shared = lax.all_gather(lax.psum(shared, "tensor"), "dp")
    shared = fold(shared)
    grad_down = jnp.swapaxes(shared[:, :, :width], 1, 2)
    grad_up = shared[:, :, width : 2 * width]
    grad_map = shared[:, :, 2 * width :]
    heads_pack = jnp.concatenate(
        [
            by_part(tab_gate), by_part(tab_inner), tab_mixed,
            jnp.swapaxes(tab_step.reshape(rank, nz, heads_here), 0, 1),
        ],
        axis=2,
    )
    mine = lax.psum_scatter(heads_pack, "tensor", scatter_dimension=0)
    mine = fold(lax.all_gather(mine, "dp"))
    grad_inner = mine[:, :, : 2 * part].reshape(adapters, rank, 2, part)
    grad_mixed = jnp.swapaxes(mine[:, :, 2 * part : 3 * part], 1, 2)
    grad_step = mine[:, :, 3 * part :]
    return (
        layer_out[None], input_grad[None], grad_down, grad_inner, grad_map, grad_step, grad_mixed, grad_up
    )


def solution(mesh):
    return jax.shard_map(
        shards,
        mesh=mesh,
        in_specs=(
            P("dp", "tensor", None),
            P("dp", "tensor", None),
            P("dp", None),
            P("dp"),
            P(),
            P("dp", None, "tensor"),
            P("dp", None),
            P("dp", "tensor"),
            P(None, "tensor"),
            P("tensor"),
            P(),
            P(),
            P("tensor"),
            P("tensor"),
            P("tensor"),
            P("tensor"),
            P("tensor", "dp"),
            P(),
            P(None, None, None, "tensor"),
            P(),
            P(None, None, "tensor"),
            P(None, "tensor", None),
            P(),
        ),
        out_specs=(
            P("dp", "tensor", None),
            P("dp", "tensor", None),
            P(),
            P(None, None, None, "tensor"),
            P(),
            P(None, None, "tensor"),
            P(None, "tensor", None),
            P(),
        ),
        check_vma=False,
    )
```

```python
import functools

import jax
import jax.numpy as jnp
from jax import lax
from jax.experimental import pallas as pl
from jax.experimental.pallas import tpu as pltpu
from jax.sharding import PartitionSpec as P

EPSILON = 1e-05
HALO = 16
CHUNK = 128
SUB = 256
DOC_MOST = 800
LOG2E = 1.4426950408889634
F32 = jnp.float32
BF16 = jnp.bfloat16
EXACT = lax.Precision.HIGHEST


def dot(a, b, precision=None):
    return lax.dot_general(
        a, b, (((1,), (0,)), ((), ())), precision=precision, preferred_element_type=F32
    )


def dot_nt(a, b, precision=None):
    return lax.dot_general(
        a, b, (((1,), (1,)), ((), ())), precision=precision, preferred_element_type=F32
    )


def sigmoid(v):
    return 0.5 * jnp.tanh(0.5 * v) + 0.5


def split3(v):
    hi = v.astype(BF16)
    rest = v - hi.astype(F32)
    mid = rest.astype(BF16)
    lo = (rest - mid.astype(F32)).astype(BF16)
    return jnp.concatenate([hi, mid, lo], axis=1)


def spread_matrix(heads, cols, base, width):
    k = lax.broadcasted_iota(jnp.int32, (3 * heads, cols), 0)
    k = jnp.where(k >= 2 * heads, k - 2 * heads, jnp.where(k >= heads, k - heads, k))
    l = lax.broadcasted_iota(jnp.int32, (3 * heads, cols), 1)
    return jnp.where(k == base + l // width, 1.0, 0.0).astype(BF16)


def row_matrix(heads, rows, base):
    k = lax.broadcasted_iota(jnp.int32, (rows, 3 * heads), 1)
    k = jnp.where(k >= 2 * heads, k - 2 * heads, jnp.where(k >= heads, k - heads, k))
    i = lax.broadcasted_iota(jnp.int32, (rows, 3 * heads), 0)
    return jnp.where(k == base + i, 1.0, 0.0).astype(BF16)


def gather_matrix(cols, base, width):
    l = lax.broadcasted_iota(jnp.int32, (cols, 128), 0)
    lane = lax.broadcasted_iota(jnp.int32, (cols, 128), 1)
    return jnp.where(lane == base + l // width, 1.0, 0.0).astype(BF16)


def two_heads(v, lane_low):
    return jnp.concatenate(
        [jnp.where(lane_low, v, 0.0), jnp.where(lane_low, 0.0, v)], axis=0
    ).astype(BF16)


def triangle(strict_lower=False, upper=False):
    r = lax.broadcasted_iota(jnp.int32, (CHUNK, CHUNK), 0)
    c = lax.broadcasted_iota(jnp.int32, (CHUNK, CHUNK), 1)
    keep = (r <= c) if upper else ((r > c) if strict_lower else (r >= c))
    return jnp.where(keep, 1.0, 0.0)


def conv_forward(buffer, tokens, weight, bias, cols):
    result = bias + weight[0:1] * buffer[HALO : HALO + tokens, :]
    for lag in range(1, 4):
        moved = buffer[HALO - lag : HALO - lag + tokens, :]
        result = result + weight[lag : lag + 1] * (moved * cols[:, lag - 1 : lag])
    return result


def fetch(plan, refs, buffer, sems, slot, k, wait=False):
    for at, entries in enumerate(plan):

        @pl.when(k == at)
        def _(entries=entries):
            for index, (which, lead, source, rows, place) in enumerate(entries):
                copy = pltpu.make_async_copy(
                    refs[which].at[lead, pl.ds(source, rows)],
                    buffer.at[slot, pl.ds(place, rows)],
                    sems.at[slot, index],
                )
                copy.wait() if wait else copy.start()


def pieces_of(plan):
    return 1 + max(entry[0] for entries in plan for entry in entries)


def stream(plan, refs, buffer, sems, j, first, last, k):
    slot = lax.rem(j, 2)

    @pl.when(j == first)
    def _():
        fetch(plan, refs, buffer, sems, slot, k)

    @pl.when(j + 1 < last)
    def _():
        fetch(plan, refs, buffer, sems, 1 - slot, k + 1)

    fetch(plan, refs, buffer, sems, slot, k, wait=True)
    return slot


def reorder(parts, source, shift, inverse=False):
    groups, _, width = parts.shape
    for g in range(groups):
        parts[g ^ shift] = source[:, g * width : (g + 1) * width]
    return jnp.concatenate([parts[g] for g in range(groups)], axis=1)


def lanes_of(i):
    return pl.ds(pl.multiple_of(i * SUB, SUB), SUB)


def chunk_rows(c):
    return slice(c * CHUNK, (c + 1) * CHUNK)


def allowed_mask(cols, rows, c, transposed=False):
    r = lax.broadcasted_iota(jnp.int32, (CHUNK, CHUNK), 0)
    l = lax.broadcasted_iota(jnp.int32, (CHUNK, CHUNK), 1)
    same = cols[chunk_rows(c), 7:8] == rows[0:1, chunk_rows(c)]
    return same & ((r <= l) if transposed else (r >= l))


def added(refs, lanes):
    total = refs[0][:, lanes].astype(F32)
    for ref in refs[1:]:
        total = total + ref[:, lanes].astype(F32)
    return total


def transpose(v):
    return v.astype(F32).T.astype(BF16)


def front_kernel(
    n_small, scalars, x, halo, gain, down, amap, astep, cmw, cmb, sbias, dlog, cols, *rest
):
    small_refs, rest = rest[:n_small], rest[n_small:]
    nrm, scale, low, low_out, maps, pre_map, quant, sig_out, small, buffer, parts = rest
    tokens, n2 = maps.shape
    heads = sig_out.shape[1]
    lead, half, _ = small_refs[0].shape
    columns = small.shape[1]
    for g in range(lead):
        for b in range(n_small):
            at = (g * n_small + b) * 2 * half
            small[at : at + half] = small_refs[b][g, :, :columns]
            small[at + half : at + 2 * half] = small_refs[b][g, :, columns:]
    before = jnp.concatenate([halo[:HALO], halo[HALO:]], axis=1).astype(F32)
    before = jnp.where(scalars[1] > 0, before, 0.0)
    xf = jnp.concatenate([before, x[...].astype(F32)], axis=0)
    q = lax.rsqrt(jnp.mean(xf * xf, axis=-1, keepdims=True) + EPSILON)
    normed = (xf * q * gain[...]).astype(BF16)
    scale[...] = jnp.broadcast_to(q[HALO:], scale.shape)
    adapter_low = dot(normed, down[...])
    low_out[...] = adapter_low[HALO:]
    adapter_low = adapter_low.astype(BF16)
    low[...] = adapter_low
    ordered = reorder(parts, normed, scalars[0])
    nrm[...] = ordered
    buffer[...] = dot(ordered, small[:, :n2]) + dot(adapter_low, amap[...])
    pre = conv_forward(buffer, tokens, cmw[...], cmb[...], cols[...])
    pre_map[...] = pre
    maps[...] = (pre * sigmoid(pre)).astype(BF16)
    raw = dot(ordered[HALO:], small[:, n2 : n2 + heads]) + sbias[...]
    raw = raw + dot(adapter_low[HALO:], astep[...])
    step = jnp.maximum(raw, 0.0) + jnp.log(1.0 + jnp.exp(-jnp.abs(raw)))
    sig_out[...] = sigmoid(raw)
    rate = -jnp.exp(dlog[...])
    drop = step * rate * LOG2E
    lower = triangle()
    sums = []
    for c in range(tokens // CHUNK):
        sums.append(dot(lower, drop[c * CHUNK : (c + 1) * CHUNK], precision=EXACT))
    base = jnp.zeros_like(sums[0][0:1])
    bases = []
    for c in range(tokens // CHUNK):
        bases.append(base)
        base = base + sums[c][CHUNK - 1 : CHUNK]
    column = cols[...]
    cum = jnp.concatenate(sums, axis=0)
    whole = jnp.concatenate([s + b for s, b in zip(sums, bases)], axis=0)
    left = jnp.concatenate([s[CHUNK - 1 : CHUNK] - s for s in sums], axis=0)
    quant[0] = split3(cum)
    quant[1] = split3(step)
    quant[2] = split3(jnp.exp2(cum) * column[:, 3:4])
    quant[3] = split3(jnp.exp2(left) * column[:, 4:5])
    quant[4] = split3(jnp.exp2(whole) * column[:, 5:6])
    quant[5] = split3(jnp.exp2(base - whole) * column[:, 6:7])


def values_kernel(
    heads, plan, first, count, scalars, nrm, low, aw, cw, cb, maps, quant, cols, rows, *rest
):
    n_w = pieces_of(plan)
    w_refs, rest = rest[:n_w], rest[-10:]
    values, pre_out, y_out, s_out, masked, in_t, buffer, wide_buffer, wbuf, sems = rest
    j = pl.program_id(0)
    slot = stream(plan, w_refs, wbuf, sems, j, 0, count, j + first)
    tokens = maps.shape[0]
    chunks = tokens // CHUNK
    n = maps.shape[1] // 2

    @pl.when(j == 0)
    def _():
        for c in range(chunks):
            b = maps[chunk_rows(c), :n]
            scores = dot_nt(maps[chunk_rows(c), n:], b)
            masked[c] = jnp.where(allowed_mask(cols, rows, c), scores, 0.0)
            in_t[c] = transpose(b)
        for lag in range(3):
            wide_buffer[lag] = jnp.broadcast_to(cols[:, lag : lag + 1], wide_buffer.shape[1:])

    buffer[...] = dot(nrm[...], wbuf[slot]) + dot(low[...], aw[...])
    subs = buffer.shape[1] // SUB
    lane_low = lax.broadcasted_iota(jnp.int32, (CHUNK, 128), 1) < 64

    def body(i, carry):
        lanes = lanes_of(i)
        base = ((j + first) * subs + i) * (SUB // 64)
        weight = cw[:, lanes]
        pre = cb[:, lanes] + weight[0:1] * buffer[HALO : HALO + tokens, lanes]
        for lag in range(1, 4):
            keep = jnp.concatenate([wide_buffer[lag - 1]] * 2, axis=1)
            moved = buffer[HALO - lag : HALO - lag + tokens, lanes]
            pre = pre + weight[lag : lag + 1] * (moved * keep)
        pre_out[:, lanes] = pre.astype(BF16)
        v = (pre * sigmoid(pre)).astype(BF16)
        values[:, lanes] = v
        wide = spread_matrix(heads, SUB, base, 64)
        v = v.astype(F32)
        vp = dot(quant[1], wide) * v
        row = dot_nt(row_matrix(heads, 8, base), quant[0])
        pair_wide = [spread_matrix(heads, 2 * CHUNK, base + 2 * p, CHUNK) for p in range(2)]
        state = None
        for c in range(chunks):
            rs = chunk_rows(c)
            cum_c = quant[0, rs]
            mask2 = jnp.concatenate([masked[c], masked[c]], axis=1)
            inside = []
            for p in range(2):
                r2 = jnp.concatenate(
                    [row[2 * p : 2 * p + 1, rs], row[2 * p + 1 : 2 * p + 2, rs]], axis=1
                )
                decay = jnp.exp2(jnp.minimum(dot(cum_c, pair_wide[p]) - r2, 0.0))
                vbd = two_heads(vp[rs, p * 128 : (p + 1) * 128], lane_low)
                inside.append(dot((decay * mask2).astype(BF16), vbd))
            y = jnp.concatenate(inside, axis=1)
            enter = dot(quant[2, rs], wide)
            if c > 0:
                y = y + enter * dot(maps[rs, n:], state.astype(BF16))
            y_out[rs, lanes] = y.astype(y_out.dtype)
            end = dot(quant[3, rs], wide)
            fresh = dot(in_t[c], (end * vp[rs]).astype(BF16))
            state = fresh if c == 0 else state * enter[CHUNK - 1 : CHUNK] + fresh
        s_out[:, lanes] = state.astype(s_out.dtype)
        return carry

    lax.fori_loop(0, subs, body, 0)


def gate_kernel(plan, count, scalars, nrm, low, aw, *rest):
    n_w = pieces_of(plan)
    w_refs, (gate_out, wbuf, sems) = rest[:n_w], rest[n_w:]
    j = pl.program_id(0)
    slot = stream(plan, w_refs, wbuf, sems, j, 0, count, j)
    gate = dot(nrm[HALO:], wbuf[slot]) + dot(low[HALO:], aw[...])
    gate_out[...] = gate.astype(BF16)


def gated_kernel(
    heads, plan, count, n_s, scalars, cot, up, amixed, gate, y_in, values, skip, gain, quant, maps, *rest
):
    n_w = pieces_of(plan)
    states, w_refs, rest = rest[:n_s], rest[n_s : n_s + n_w], rest[n_s + n_w :]
    gg_out, r_out, gy_out, gz_out, g_out, mlow_out, tab_up, tab_mixed, *rest = rest
    grad, ys, ggs, squares, inner, parts, cot_x, out_t, gml, low, scaled, wbuf, sems = rest
    j = pl.program_id(0)
    n = maps.shape[1] // 2
    part = gate.shape[1]
    subs = part // SUB

    @pl.when(j == 0)
    def _():
        gml[...] = dot_nt(cot[...], up[...])
        low[...] = jnp.zeros_like(low)
        inner[...] = jnp.zeros_like(inner)
        squares[...] = jnp.zeros_like(squares)
        cot_x[...] = reorder(parts, cot, scalars[0])
        out_t[...] = transpose(maps[:, n:])

    @pl.when(j < count)
    def _():
        slot = stream(plan, w_refs, wbuf, sems, j, 0, count, j)
        grad[j] = dot(cot_x[...], wbuf[slot]) + dot(gml[...].astype(BF16), amixed[...])

        def body(i, carry):
            lanes = lanes_of(i)
            wide = spread_matrix(heads, SUB, (j * subs + i) * (SUB // 64), 64)
            g = gate[:, lanes].astype(F32)
            state = added(states, lanes).astype(BF16)
            entering = dot(quant[0], wide) * dot(maps[:, n:], state)
            y = y_in[:, lanes].astype(F32) + entering
            y = y + skip[:, lanes] * values[:, lanes].astype(F32)
            ys[j, :, lanes] = y
            gated = y * (g * sigmoid(g))
            scaled_up = (gated * gain[:, lanes]).astype(BF16)
            ggs[j, :, lanes] = scaled_up
            gg_out[:, lanes] = scaled_up
            square = gated * gated
            squares[...] += square[:, :128] + square[:, 128:]
            term = scaled_up.astype(F32) * grad[j, :, lanes]
            inner[...] += term[:, :128] + term[:, 128:]
            return carry

        lax.fori_loop(0, subs, body, 0)
        low[...] += dot_nt(ggs[j], amixed[...])

    @pl.when(j >= count)
    def _():
        k = j - count
        size = count * part
        r = lax.rsqrt(jnp.sum(squares[...], axis=-1, keepdims=True) / size + EPSILON)
        cube = r * r * r * (jnp.sum(inner[...], axis=-1, keepdims=True) / size)

        @pl.when(k == 0)
        def _():
            r_out[...] = jnp.broadcast_to(r, r_out.shape)
            scaled[...] = transpose(gml[...] * r)
            mixed_low = low[...] * r
            mlow_out[...] = mixed_low.astype(BF16)
            tab_up[...] = dot(transpose(mixed_low), cot[...])

        tab_mixed[...] = dot(scaled[...], ggs[k])

        def body(i, carry):
            lanes = lanes_of(i)
            g = gate[:, lanes].astype(F32)
            y = ys[k, :, lanes]
            s = sigmoid(g)
            act = g * s
            grad_gated = (grad[k, :, lanes] * gain[:, lanes]) * r - y * act * cube
            gy = grad_gated * act
            gy_out[:, lanes] = gy.astype(BF16)
            gz_out[:, lanes] = (grad_gated * y * (s * (1.0 + g * (1.0 - s)))).astype(BF16)
            enter = dot(quant[0], spread_matrix(heads, SUB, (k * subs + i) * (SUB // 64), 64))
            g_out[:, lanes] = dot(out_t[...], (enter * gy).astype(BF16)).astype(g_out.dtype)
            return carry

        lax.fori_loop(0, subs, body, 0)


def backward_kernel(
    heads, count, n_s, scalars, values, gy_in, maps, quant, cols, rows, *rest
):
    s_refs, rest = rest[:n_s], rest[n_s:]
    dx_out, gmaps_out, r_out, masked, allowed, mixed, grad_b, grad_c, *rest = rest
    col_p, row_p, carry_a, carry_b, ends, in_b, out_b = rest
    j = pl.program_id(0)
    tokens = maps.shape[0]
    chunks = tokens // CHUNK
    n = maps.shape[1] // 2
    subs = values.shape[1] // SUB

    @pl.when(j == 0)
    def _():
        for c in range(chunks):
            rs = chunk_rows(c)
            ok = allowed_mask(cols, rows, c, transposed=True)
            scores = dot_nt(maps[rs, :n], maps[rs, n:])
            masked[c] = jnp.where(ok, scores, 0.0)
            allowed[c] = jnp.where(ok, 1.0, 0.0)
            in_b[c] = transpose(maps[rs, :n])
            out_b[c] = transpose(maps[rs, n:])
        for ref in (mixed, grad_b, grad_c, col_p, row_p, carry_a, carry_b, ends):
            ref[...] = jnp.zeros_like(ref)

    lane_low = lax.broadcasted_iota(jnp.int32, (CHUNK, 128), 1) < 64
    sub = lax.broadcasted_iota(jnp.int32, (heads, CHUNK), 0)

    def body(i, carry):
        lanes = lanes_of(i)
        base = (j * subs + i) * (SUB // 64)
        wide = spread_matrix(heads, SUB, base, 64)
        vp = dot(quant[1], wide) * values[:, lanes].astype(F32)
        row = dot_nt(row_matrix(heads, 8, base), quant[0])
        pair_wide = [spread_matrix(heads, 2 * CHUNK, base + 2 * p, CHUNK) for p in range(2)]
        pair_sum = [gather_matrix(2 * CHUNK, base + 2 * p, CHUNK) for p in range(2)]
        head_sum = gather_matrix(SUB, base, 64)
        enters, lefts, states = [], [], []
        state = added(s_refs, lanes)
        for c in range(chunks):
            rs = chunk_rows(c)
            enters.append(dot(quant[2, rs], wide))
            lefts.append(dot(quant[3, rs], wide))
            states.append(state)
            if c < chunks - 1:
                fresh = dot(in_b[c], (lefts[c] * vp[rs]).astype(BF16))
                state = state * enters[c][CHUNK - 1 : CHUNK] + fresh
        adjoint = None
        for c in range(chunks - 1, -1, -1):
            rs = chunk_rows(c)
            cum_c = quant[0, rs]
            gy = gy_in[rs, lanes].astype(F32)
            mask2 = jnp.concatenate([masked[c], masked[c]], axis=1)
            dx = []
            for p in range(2):
                pair = slice(p * 128, (p + 1) * 128)
                r2 = jnp.concatenate(
                    [row[2 * p : 2 * p + 1, rs], row[2 * p + 1 : 2 * p + 2, rs]], axis=1
                )
                decay = jnp.exp2(jnp.minimum(r2 - dot(cum_c, pair_wide[p]), 0.0))
                gbd = two_heads(gy[:, pair], lane_low)
                dx.append(dot((decay * mask2).astype(BF16), gbd))
                part = decay * dot_nt(vp[rs, pair].astype(BF16), gbd)
                mixed[c] += part[:, :CHUNK] + part[:, CHUNK:]
                weighed = (part * mask2).astype(BF16)
                col_p[rs] += dot(weighed, pair_sum[p])
                for q in range(2):
                    pick = jnp.where(sub == base + 2 * p + q, 1.0, 0.0).astype(BF16)
                    row_p[:, rs] += dot(pick, weighed[:, q * CHUNK : (q + 1) * CHUNK])
            dx = jnp.concatenate(dx, axis=1)
            entering = enters[c] * gy
            carried = entering * dot(maps[rs, n:], states[c].astype(BF16))
            carry_a[rs] += dot(carried.astype(BF16), head_sum)
            entering = entering.astype(BF16)
            grad_c[rs] += dot_nt(entering, states[c].astype(BF16))
            last = enters[c][CHUNK - 1 : CHUNK]
            if adjoint is not None:
                adj = adjoint.astype(BF16)
                leaving = lefts[c] * dot(maps[rs, :n], adj)
                dx = dx + leaving
                carry_b[rs] += dot((vp[rs] * leaving).astype(BF16), head_sum)
                grad_b[rs] += dot_nt((lefts[c] * vp[rs]).astype(BF16), adj)
                through = jnp.sum(adjoint * states[c], axis=0, keepdims=True) * last
                ends[c * 8 : c * 8 + 8] += dot(
                    jnp.broadcast_to(through, (8, SUB)), head_sum.astype(F32), precision=EXACT
                )
            dx_out[rs, lanes] = dx.astype(dx_out.dtype)
            if c > 0:
                fresh = dot(out_b[c], entering)
                adjoint = fresh if adjoint is None else adjoint * last + fresh
        return carry

    lax.fori_loop(0, subs, body, 0)

    @pl.when(j == count - 1)
    def _():
        suffix = triangle(upper=True)
        prefix = triangle(strict_lower=True)
        for c in range(chunks):
            rs = chunk_rows(c)
            w = mixed[c] * allowed[c]
            gb = grad_b[rs] + dot(w.astype(BF16), maps[rs, n:])
            gc = grad_c[rs] + dot(w.T.astype(BF16), maps[rs, :n])
            gmaps_out[rs] = jnp.concatenate([gb, gc], axis=1)
            rowsum = jnp.concatenate(
                [row_p[:, rs].T, jnp.zeros((CHUNK, 128 - heads), F32)], axis=1
            )
            first = rowsum - col_p[rs] + carry_a[rs]
            r_out[rs] = (
                dot(suffix, first, precision=EXACT)
                + dot(prefix, carry_b[rs], precision=EXACT)
                + ends[c * 8 : c * 8 + 1]
            )


def finish_kernel(
    heads, count, n_s, scalars, values, dx_in, gy_in, pre, maps, quant_step, quant_enter, quant_left,
    skip, gmaps, r_in, sig, dlog, pre_map, *rest
):
    s_refs, g_refs, rest = rest[:n_s], rest[n_s : 2 * n_s], rest[2 * n_s :]
    c_out, cmap_out, gstep_out, col_g, carry_b, grad_b, ends = rest
    j = pl.program_id(0)
    tokens = maps.shape[0]
    n = maps.shape[1] // 2
    subs = values.shape[1] // SUB

    @pl.when(j == 0)
    def _():
        for ref in (col_g, carry_b, grad_b, ends):
            ref[...] = jnp.zeros_like(ref)

    def body(i, carry):
        lanes = lanes_of(i)
        base = (j * subs + i) * (SUB // 64)
        wide = spread_matrix(heads, SUB, base, 64)
        head_sum = gather_matrix(SUB, base, 64)
        v = values[:, lanes].astype(F32)
        step = dot(quant_step[0], wide)
        left = dot(quant_left[0], wide)
        vp = step * v
        adjoint = added(g_refs, lanes)
        both = adjoint * added(s_refs, lanes)
        adjoint = adjoint.astype(BF16)
        more = left * dot(maps[:, :n], adjoint)
        dx = dx_in[:, lanes].astype(F32) + more
        carry_b[...] += dot((vp * more).astype(BF16), head_sum)
        col_g[...] += dot((v * dx).astype(BF16), head_sum)
        grad_b[...] += dot_nt((left * vp).astype(BF16), adjoint)
        last = dot(quant_enter[0, tokens - 16 :], wide)[15:16]
        through = jnp.sum(both, axis=0, keepdims=True) * last
        ends[...] += dot(jnp.broadcast_to(through, (8, SUB)), head_sum.astype(F32), precision=EXACT)
        dv = step * dx + skip[:, lanes] * gy_in[:, lanes].astype(F32)
        pre_f = pre[:, lanes].astype(F32)
        s = sigmoid(pre_f)
        c_out[:, lanes] = (dv * (s * (1.0 + pre_f * (1.0 - s)))).astype(BF16)
        return carry

    lax.fori_loop(0, subs, body, 0)

    @pl.when(j == count - 1)
    def _():
        prefix = triangle(strict_lower=True)
        run = ends[0:1]
        rate = -jnp.exp(dlog[...])
        for c in range(tokens // CHUNK):
            rs = chunk_rows(c)
            total = r_in[rs] + dot(prefix, carry_b[rs], precision=EXACT) + run
            run = run + jnp.sum(carry_b[rs], axis=0, keepdims=True)
            raw = (col_g[rs][:, :heads] + rate * total[:, :heads]) * sig[rs]
            gstep_out[rs] = raw.astype(BF16)
        gb = gmaps[:, :n] + grad_b[...]
        g = jnp.concatenate([gb, gmaps[:, n:]], axis=1)
        pm = pre_map[...]
        sm = sigmoid(pm)
        cmap_out[...] = (g * (sm * (1.0 + pm * (1.0 - sm)))).astype(cmap_out.dtype)


def conv_backward(buffer, tokens, weight, cols):
    result = weight[0:1] * buffer[0:tokens, :]
    for lag in range(1, 4):
        result = result + weight[lag : lag + 1] * (
            buffer[lag : lag + tokens, :] * cols[:, 7 + lag : 8 + lag]
        )
    return result


def tables_kernel(
    count, scalars, c_in, c_halo, cmap, cmap_halo, glow_in, cw, cmw, ainner, amap, astep, gstep, low, low_f, nrm, cols,
    gi_out, gmap_out, glow_out, tab_inner, tab_map, tab_step, tab_down, buffer, glow, low_t, parts,
):
    j = pl.program_id(0)
    tokens = gi_out.shape[0]
    subs = gi_out.shape[1] // SUB

    @pl.when(j == 0)
    def _():
        low_t[...] = transpose(low[HALO:])
        buffer[:tokens] = cmap[...].astype(F32)
        buffer[tokens:] = cmap_halo[...].astype(F32)
        gmap = conv_backward(buffer, tokens, cmw[...], cols[...])
        exact_low = low_f[...].T
        tab_map[...] = dot(exact_low, gmap, precision=EXACT)
        tab_step[...] = dot(exact_low, gstep[...].astype(F32), precision=EXACT)
        gmap = gmap.astype(BF16)
        gmap_out[...] = gmap
        glow[...] = glow_in[...] + dot_nt(gmap, amap[...]) + dot_nt(gstep[...], astep[...])

    def body(i, carry):
        lanes = lanes_of(i)
        buffer[:tokens] = c_in[:, lanes].astype(F32)
        buffer[tokens:] = c_halo[:, lanes].astype(F32)
        gi_out[:, lanes] = conv_backward(buffer, tokens, cw[:, lanes], cols[...]).astype(BF16)
        return carry

    lax.fori_loop(0, subs, body, 0)
    glow[...] += dot_nt(gi_out[...], ainner[...])
    tab_inner[...] = dot(low_t[...], gi_out[...])

    @pl.when(j == count - 1)
    def _():
        glow_out[...] = glow[...].astype(BF16)
        down = dot(transpose(glow[...]), nrm[HALO:])
        tab_down[...] = reorder(parts, down, scalars[0])


def out_kernel(plan, count, scalars, x, gg, up, r_in, mlow, *rest):
    n_w = pieces_of(plan)
    w_refs = rest[:n_w]
    out, total, parts, wbuf, sems = rest[n_w:]
    j = pl.program_id(0)
    slot = stream(plan, w_refs, wbuf, sems, j, 0, count, j)
    term = dot_nt(gg[...], wbuf[slot])

    @pl.when(j == 0)
    def _():
        total[...] = term

    @pl.when(j > 0)
    def _():
        total[...] += term

    @pl.when(j == count - 1)
    def _():
        branch = reorder(parts, total, scalars[0]) * r_in[:, 0:1]
        out[...] = (x[...].astype(F32) + branch + dot(mlow[...], up[...])).astype(BF16)


def gate_rows_kernel(plan, count, scalars, gz, agate, low, *rest):
    n_w = pieces_of(plan)
    w_refs = rest[:n_w]
    total, glow, tab_gate, low_t, wbuf, sems = rest[n_w:]
    j = pl.program_id(0)
    slot = stream(plan, w_refs, wbuf, sems, j, 0, count, j)

    @pl.when(j == 0)
    def _():
        low_t[...] = transpose(low[HALO:])

    term = dot_nt(gz[...], wbuf[slot])
    thin = dot_nt(gz[...], agate[...])
    tab_gate[...] = dot(low_t[...], gz[...])

    @pl.when(j == 0)
    def _():
        total[...] = term
        glow[...] = thin

    @pl.when(j > 0)
    def _():
        total[...] += term
        glow[...] += thin


def input_kernel(
    plan, count, scalars, start, gi, gmap, gstep, glow, small, down, x, cot, scale, gain, *rest
):
    n_w = pieces_of(plan)
    w_refs = rest[:n_w]
    out, total, parts, wbuf, sems = rest[n_w:]
    j = pl.program_id(0)
    slot = stream(plan, w_refs, wbuf, sems, j, 0, count, j)

    @pl.when(j == 0)
    def _():
        n2, heads = gmap.shape[1], gstep.shape[1]
        total[...] = (
            start[...]
            + dot_nt(gmap[...], small[:, :n2])
            + dot_nt(gstep[...], small[:, n2 : n2 + heads])
        )

    total[...] += dot_nt(gi[...], wbuf[slot])

    @pl.when(j == count - 1)
    def _():
        q = scale[:, 0:1]
        xf = x[...].astype(F32)
        normed_grad = reorder(parts, total, scalars[0]) + dot_nt(glow[...], down[...])
        weighted = normed_grad * gain[...]
        mean = jnp.mean(xf * weighted, axis=-1, keepdims=True)
        out[...] = q * weighted - xf * (q * q * q * mean) + cot[...].astype(F32)


def whole(shape):
    return pl.BlockSpec(shape, lambda *_: (0,) * len(shape))


def call(kernel, steps, in_specs, out_specs, out_shape, scratch, micros, aliases=None):
    return pl.pallas_call(
        kernel,
        grid_spec=pltpu.PrefetchScalarGridSpec(
            num_scalar_prefetch=1,
            grid=(steps,),
            in_specs=in_specs,
            out_specs=out_specs,
            scratch_shapes=scratch,
        ),
        out_shape=out_shape,
        input_output_aliases=aliases or {},
        compiler_params=pltpu.CompilerParams(
            dimension_semantics=("arbitrary",), vmem_limit_bytes=56 * 2**20
        ),
        cost_estimate=pl.CostEstimate(
            flops=int(micros * 1.1e9), bytes_accessed=int(micros * 1e6), transcendentals=0
        ),
    )


def shape(dims, kind):
    return jax.ShapeDtypeStruct(dims, kind)


def xor(v, m, ndp):
    return lax.ppermute(v, "dp", [(i, i ^ m) for i in range(ndp)])


def around(v, k, nz):
    return lax.ppermute(v, "tensor", [(i, (i + k) % nz) for i in range(nz)])


def all_slots(v, nz):
    return [v] + [around(v, k, nz) for k in range(1, nz)]


def after(v, *others):
    return lax.optimization_barrier((v, others))[0]


def split_rows(v):
    high = lax.optimization_barrier(v.astype(BF16))
    rest = v - high.astype(F32)
    middle = lax.optimization_barrier(rest.astype(BF16))
    return jnp.concatenate([high, middle, (rest - middle.astype(F32)).astype(BF16)], axis=0)


def joined_rows(v):
    high, middle, low = jnp.split(v.astype(F32), 3, axis=0)
    return high + middle + low


def shards(
    layer_in,
    cotangent,
    segment_ids,
    adapter_ids,
    norm_gain,
    inner_weight,
    map_weight,
    step_weight,
    conv_inner_weight,
    conv_inner_bias,
    conv_map_weight,
    conv_map_bias,
    step_bias,
    decay_log,
    skip_gain,
    gate_gain,
    out_weight,
    adapter_down,
    adapter_inner,
    adapter_map,
    adapter_step,
    adapter_mixed,
    adapter_up,
):
    ndp, nz = lax.axis_size("dp"), lax.axis_size("tensor")
    z = lax.axis_index("tensor")
    x, cot = layer_in[0], cotangent[0]
    tokens, width = x.shape
    rows_here = inner_weight.shape[0]
    part = gate_gain.shape[0]
    inner = part * nz
    heads_here = step_bias.shape[0]
    heads = heads_here * nz
    adapters, _, rank = adapter_down.shape
    n2 = map_weight.shape[1]
    n = n2 // 2
    chunks = tokens // CHUNK
    ext = tokens + HALO
    nq = 3 * heads
    up_one = [(i, i + 1) for i in range(nz - 1)]
    down_one = [(i + 1, i) for i in range(nz - 1)]
    chip_plan = ndp == 8 and nz == 4 and rows_here % 64 == 0

    pick = adapter_ids[0]
    tail = x[tokens - HALO :]
    thin_rows = jnp.concatenate([step_bias, decay_log, skip_gain])[None]
    packed = jnp.concatenate(
        [
            conv_inner_weight,
            conv_inner_bias[None],
            gate_gain[None],
            jnp.pad(thin_rows, ((0, 0), (0, part - 3 * heads_here))),
        ],
        axis=0,
    )
    thin = jnp.concatenate([step_weight.T, adapter_step[pick].T], axis=1)
    tables = jnp.concatenate(
        [adapter_inner[pick].reshape(2 * rank, part), adapter_mixed[pick].T], axis=0
    )
    first_block, gate_block, out_block = inner_weight[:, 1], inner_weight[:, 0], out_weight.T

    if chip_plan:
        groups = ndp
        scalars = jnp.stack([lax.axis_index("dp") % 2, z]).astype(jnp.int32)
        chips = ndp // 2
        small_rows = rows_here // 2
        rest_rows = (nz - 1) * rows_here
        same_core = [[2 * g + core for g in range(chips)] for core in (0, 1)]

        def plan_of(which):
            def entries(first, low):
                return tuple(
                    (first + b, g, low, rows_here, (2 * g + b) * rows_here)
                    for g in range(chips)
                    for b in (0, 1)
                )

            return (entries(0, which * rows_here),) + tuple(
                entries(2, k * rows_here) for k in range(nz - 1)
            )

        plan_in, plan_gate, plan_out = plan_of(0), plan_of(1), plan_of(2)

        def spread(v):
            return lax.all_gather(v, "dp", axis_index_groups=same_core)

        def both(v):
            return [v, xor(v, 1, ndp)]

        wide_thin = jnp.pad(thin, ((0, 0), (0, part - thin.shape[1])))
        tail = jnp.concatenate(jnp.split(tail, 2, axis=1), axis=0)
        lead = jnp.concatenate([first_block, tail, split_rows(packed), wide_thin], axis=0)
        lead = jnp.pad(lead, ((0, -lead.shape[0] % 16), (0, 0)))
        own_block = jnp.concatenate([first_block, gate_block, out_block], axis=0)
        owns = spread(own_block)
        z1 = all_slots(lead, nz)
        others = jnp.concatenate([gate_block, out_block, tables], axis=0)
        z2 = all_slots(after(others, z1), nz)
        low_at = rows_here + 2 * HALO
        halo = z1[1]
        halo_spec = pl.BlockSpec((2 * HALO, part), lambda j, sc: (rows_here // (2 * HALO), 0))
        at = low_at + 3 * packed.shape[0]
        packed = [joined_rows(v[low_at:at]) for v in z1]
        thin = jnp.concatenate([v[at : at + heads_here, : thin.shape[1]] for v in z1], axis=0).T
        small = jnp.concatenate([map_weight, thin[:rows_here]], axis=1)
        small = jnp.pad(small, ((0, 0), (0, part // 2 - small.shape[1])))
        small = jnp.concatenate([small[:small_rows], small[small_rows:]], axis=1)
        s1 = jnp.concatenate([v[:rows_here] for v in z1[1:]] + [small], axis=0)
        rest1 = spread(after(s1, owns))
        s2 = jnp.concatenate([v[:rows_here] for v in z2[1:]], axis=0)
        rest2 = spread(after(s2, rest1))
        s3 = jnp.concatenate([v[rows_here : 2 * rows_here] for v in z2[1:]], axis=0)
        rest3 = spread(after(s3, rest1))
        tables = [v[2 * rows_here :] for v in z2]
        small_spec = pl.BlockSpec(
            (chips, small_rows, part), lambda j, sc: (0, rest_rows // small_rows, 0)
        )
    else:
        groups = 1
        scalars = jnp.stack([jnp.zeros_like(z), z]).astype(jnp.int32)
        plan_in = tuple(((0, 0, k * width, width, 0),) for k in range(nz))
        plan_gate = plan_out = plan_in
        tail = jnp.concatenate(jnp.split(tail, 2, axis=1), axis=0)
        halo = lax.ppermute(tail, "tensor", up_one)
        halo_spec = pl.BlockSpec((2 * HALO, part), lambda j, sc: (0, 0))

        def plain(block):
            block = lax.all_gather(block, "dp", axis=0, tiled=True)
            return [jnp.concatenate(all_slots(block, nz), axis=0)[None]]

        w_inner, w_gate, w_out = plain(first_block), plain(gate_block), plain(out_block)
        packed, tables = all_slots(packed, nz), all_slots(tables, nz)
        thin = jnp.concatenate(all_slots(thin, nz), axis=0).T
        small = jnp.concatenate([map_weight, thin[:rows_here]], axis=1)
        small = jnp.pad(small, ((0, 0), (0, part // 2 - small.shape[1])))
        small = lax.all_gather(small, "dp", axis=0, tiled=True)
        small = [jnp.concatenate(jnp.split(small, 2, axis=0), axis=1)[None]]
        small_spec = pl.BlockSpec((1, width // 2, part), lambda j, sc: (0, 0, 0))
    group_rows = width // groups

    astep = thin[rows_here : rows_here + rank]
    wide_rows = jnp.concatenate([v[:6] for v in packed], axis=1)
    conv_w, conv_b, gain = wide_rows[:4], wide_rows[4:5], wide_rows[5:6]
    thin_rows = jnp.stack([v[6, : 3 * heads_here].reshape(3, heads_here) for v in packed], axis=1)
    thin_rows = thin_rows.reshape(3, heads)
    sbias, dlog = thin_rows[0:1], thin_rows[1:2]
    skip = jnp.repeat(thin_rows[2], inner // heads)[None]
    tables = jnp.concatenate(tables, axis=1)
    two = tables[: 2 * rank].reshape(rank, 2, inner)
    agate, ainner, amixed = two[:, 0], two[:, 1], tables[2 * rank :]
    down, amap, up = adapter_down[pick], adapter_map[pick], adapter_up[pick]

    segment = segment_ids[0]
    padded = jnp.pad(segment, (HALO, HALO), constant_values=-1)
    near = lax.dynamic_slice(padded, (z * tokens,), (tokens + 2 * HALO,))
    own = near[HALO : HALO + tokens]
    by_chunk = own.reshape(chunks, CHUNK)
    before = jnp.concatenate([near[HALO - 1 : HALO], by_chunk[:-1, -1]])
    columns = [near[HALO - k : HALO - k + tokens] == own for k in (1, 2, 3)]
    columns += [
        (by_chunk == before[:, None]).reshape(tokens),
        (by_chunk == by_chunk[:, -1:]).reshape(tokens),
        own == near[HALO - 1],
        own == own[tokens - 1],
        own,
    ]
    columns += [near[HALO + k : HALO + k + tokens] == own for k in (1, 2, 3)]
    cols = jnp.stack([c.astype(F32) for c in columns], axis=1)
    rows = jnp.broadcast_to(own.astype(F32)[None], (8, tokens))

    if chip_plan:
        ready = (cols, rows, conv_w, conv_b, gain, skip, sbias, dlog, astep, ainner, amap, down)
        owns, rest1 = after((owns, rest1), ready)
        owns, rest1 = both(owns), both(rest1)
        w_inner = owns + rest1
        small = rest1
    n_w = len(w_inner)

    def by_slot(height, first=0):
        return pl.BlockSpec((height, part), lambda j, sc: (0, j + first))

    def turned(height, by):
        return pl.BlockSpec((height, part), lambda j, sc: (0, lax.rem(j + by + 2 * nz, nz)))

    def quantity(*which):
        if len(which) == 1:
            return pl.BlockSpec((1, tokens, nq), lambda j, sc: (which[0], 0, 0))
        return pl.BlockSpec((len(which), tokens, nq), lambda j, sc: (0, 0, 0))

    anywhere = pl.BlockSpec(memory_space=pl.ANY)

    def wide_out(kind=BF16, height=tokens):
        return shape((height, inner), kind)

    def weight_scratch():
        return [
            pltpu.VMEM((2, width, part), BF16),
            pltpu.SemaphoreType.DMA((2, max(len(entries) for entries in plan_in + plan_out))),
        ]

    parts_scratch = pltpu.VMEM((groups, tokens, group_rows), F32)

    columns = part // 2
    nrm, scale, low, low_f, maps, pre_map, quant, sig, small_full = call(
        functools.partial(front_kernel, len(small)),
        1,
        [
            whole(x.shape), halo_spec, whole((1, width)), whole((width, rank)), whole((rank, n2)),
            whole((rank, heads)), whole((4, n2)), whole((1, n2)), whole((1, heads)),
            whole((1, heads)), whole(cols.shape),
        ]
        + [small_spec] * len(small),
        [
            whole((ext, width)), whole((tokens, 128)), whole((ext, rank)), whole((tokens, rank)),
            whole((tokens, n2)), whole((tokens, n2)), whole((6, tokens, nq)), whole((tokens, heads)),
            whole((width, columns)),
        ],
        [
            shape((ext, width), BF16), shape((tokens, 128), F32), shape((ext, rank), BF16),
            shape((tokens, rank), F32), shape((tokens, n2), BF16), shape((tokens, n2), F32),
            shape((6, tokens, nq), BF16), shape((tokens, heads), F32), shape((width, columns), BF16),
        ],
        [pltpu.VMEM((ext, n2), F32), pltpu.VMEM((groups, ext, group_rows), BF16)],
        8,
    )(
        scalars, x, halo, norm_gain[None], down, amap, astep, conv_map_weight, conv_map_bias[None],
        sbias, dlog, cols, *small,
    )

    results = []
    half = nz
    for first in range(0, nz, half):
        base_args = [scalars, nrm, low, ainner, conv_w, conv_b, maps, quant, cols, rows, *w_inner]
        results = call(
            functools.partial(values_kernel, heads, plan_in, first, half),
            half,
            [
                whole(nrm.shape), whole(low.shape), by_slot(rank, first), by_slot(4, first),
                by_slot(1, first), whole(maps.shape), quantity(0, 1, 2, 3), whole(cols.shape),
                whole(rows.shape),
            ]
            + [anywhere] * (n_w + len(results)),
            [by_slot(tokens, first)] * 3 + [by_slot(n, first)],
            [wide_out(), wide_out(), wide_out(), wide_out(BF16, n)],
            [
                pltpu.VMEM((chunks, CHUNK, CHUNK), F32), pltpu.VMEM((chunks, n, CHUNK), BF16),
                pltpu.VMEM((ext, part), F32), pltpu.VMEM((3, tokens, 128), F32),
            ]
            + weight_scratch(),
            15,
            {len(base_args) + i: i for i in range(len(results))},
        )(*base_args, *results)
    values, pre, y_local, s_local = results

    ent_last = quant[4, tokens - 1].reshape(3, heads).astype(F32).sum(0)
    through = jnp.repeat(ent_last, inner // heads)[None]
    hops = min(nz - 1, 1 + (DOC_MOST - 2) // tokens)

    def carry(local, pairs, turn):
        got = [lax.ppermute(local, "tensor", pairs)]
        for hop in range(1, hops):
            passed = got[-1].astype(F32) * jnp.roll(through, -turn * hop * part, axis=1)
            got.append(lax.ppermute(passed.astype(BF16), "tensor", pairs))
        return got

    s_in = carry(s_local, up_one, 1)
    from_left = [turned(n, -1 - hop) for hop in range(hops)]
    from_right = [turned(n, 1 + hop) for hop in range(hops)]

    if chip_plan:
        w_gate = owns + both(after(rest2, values))
    gate = call(
        functools.partial(gate_kernel, plan_gate, nz),
        nz,
        [whole(nrm.shape), whole(low.shape), by_slot(rank)] + [anywhere] * n_w,
        by_slot(tokens),
        wide_out(),
        weight_scratch(),
        10,
    )(scalars, after(nrm, s_local), low, agate, *w_gate)
    if chip_plan:
        w_out = owns + both(after(rest3, s_in[-1], gate))

    def slot_in(height, phase, by=0):
        def index(j, sc):
            at = (jnp.minimum(j, nz - 1), jnp.maximum(j - nz, 0), lax.rem(j, nz))[phase]
            return (0, lax.rem(at + by + 2 * nz, nz))

        return pl.BlockSpec((height, part), index)

    gg, r_gate, gy, gz, g_local, mixed_low, tab_up, tab_mixed = call(
        functools.partial(gated_kernel, heads, plan_out, nz, hops),
        2 * nz,
        [
            whole(cot.shape), whole(up.shape), slot_in(rank, 0), slot_in(tokens, 2),
            slot_in(tokens, 0), slot_in(tokens, 0), slot_in(1, 0), slot_in(1, 2), quantity(4),
            whole(maps.shape),
        ]
        + [slot_in(n, 0, -1 - hop) for hop in range(hops)]
        + [anywhere] * n_w,
        [
            slot_in(tokens, 0), whole((tokens, 128)), slot_in(tokens, 1), slot_in(tokens, 1),
            slot_in(n, 1), whole((tokens, rank)), whole(up.shape), slot_in(rank, 1),
        ],
        [
            wide_out(), shape((tokens, 128), F32), wide_out(), wide_out(), wide_out(BF16, n),
            shape((tokens, rank), BF16), shape(up.shape, F32), wide_out(F32, rank),
        ],
        [
            pltpu.VMEM((nz, tokens, part), F32), pltpu.VMEM((nz, tokens, part), F32),
            pltpu.VMEM((nz, tokens, part), BF16), pltpu.VMEM((tokens, 128), F32),
            pltpu.VMEM((tokens, 128), F32), pltpu.VMEM((groups, tokens, group_rows), BF16),
            pltpu.VMEM((tokens, width), BF16), pltpu.VMEM((n, tokens), BF16),
            pltpu.VMEM((tokens, rank), F32), pltpu.VMEM((tokens, rank), F32),
            pltpu.VMEM((rank, tokens), BF16),
        ]
        + weight_scratch(),
        26,
    )(
        scalars, cot, up, amixed, gate, y_local, values, skip, gain, quant, maps, *s_in, *w_out,
    )

    g_in = carry(g_local, down_one, -1)
    start, glow_gate, tab_gate = call(
        functools.partial(gate_rows_kernel, plan_gate, nz),
        nz,
        [by_slot(tokens), by_slot(rank), whole(low.shape)] + [anywhere] * n_w,
        [whole((tokens, width)), whole((tokens, rank)), by_slot(rank)],
        [shape((tokens, width), F32), shape((tokens, rank), F32), wide_out(F32, rank)],
        [pltpu.VMEM((rank, tokens), BF16)] + weight_scratch(),
        11,
    )(scalars, gz, agate, low, *w_gate)
    gy = after(gy, g_in[0], start)

    dx, gmaps, r_local = call(
        functools.partial(backward_kernel, heads, nz, hops),
        nz,
        [
            by_slot(tokens), by_slot(tokens), whole(maps.shape), quantity(0, 1, 2, 3),
            whole(cols.shape), whole(rows.shape),
        ]
        + from_left,
        [by_slot(tokens), whole((tokens, n2)), whole((tokens, 128))],
        [wide_out(), shape((tokens, n2), F32), shape((tokens, 128), F32)],
        [
            pltpu.VMEM((chunks, CHUNK, CHUNK), F32), pltpu.VMEM((chunks, CHUNK, CHUNK), F32),
            pltpu.VMEM((chunks, CHUNK, CHUNK), F32), pltpu.VMEM((tokens, n), F32),
            pltpu.VMEM((tokens, n), F32), pltpu.VMEM((tokens, 128), F32),
            pltpu.VMEM((heads, tokens), F32), pltpu.VMEM((tokens, 128), F32),
            pltpu.VMEM((tokens, 128), F32), pltpu.VMEM((8 * chunks, 128), F32),
            pltpu.VMEM((chunks, n, CHUNK), BF16), pltpu.VMEM((chunks, n, CHUNK), BF16),
        ],
        32,
    )(scalars, values, gy, maps, quant, cols, rows, *s_in)

    c_all, cmap, gstep = call(
        functools.partial(finish_kernel, heads, nz, hops),
        nz,
        [
            by_slot(tokens), by_slot(tokens), by_slot(tokens), by_slot(tokens), whole(maps.shape),
            quantity(1), quantity(4), quantity(5), by_slot(1), whole(gmaps.shape),
            whole(r_local.shape), whole(sig.shape), whole(dlog.shape), whole(pre_map.shape),
        ]
        + from_left
        + from_right,
        [by_slot(tokens), whole((tokens, n2)), whole((tokens, heads))],
        [wide_out(), shape((tokens, n2), F32), shape((tokens, heads), BF16)],
        [
            pltpu.VMEM((tokens, 128), F32), pltpu.VMEM((tokens, 128), F32),
            pltpu.VMEM((tokens, n), F32), pltpu.VMEM((8, 128), F32),
        ],
        12,
    )(
        scalars, values, dx, gy, pre, maps, quant, quant, quant, skip, gmaps, r_local, sig, dlog, pre_map,
        *s_in, *g_in,
    )

    c_halo = lax.ppermute(
        jnp.concatenate([c_all[:HALO], cmap[:HALO].astype(BF16)], axis=1), "tensor", down_one
    )
    gi, gmap, glow, tab_inner, tab_map, tab_step, tab_down = call(
        functools.partial(tables_kernel, nz),
        nz,
        [
            by_slot(tokens), turned(HALO, 1), whole(cmap.shape), whole((HALO, n2)),
            whole((tokens, rank)), by_slot(4), whole((4, n2)), by_slot(rank), whole(amap.shape),
            whole(astep.shape), whole(gstep.shape), whole(low.shape), whole(low_f.shape),
            whole(nrm.shape), whole(cols.shape),
        ],
        [
            by_slot(tokens), whole((tokens, n2)), whole((tokens, rank)), by_slot(rank),
            whole((rank, n2)), whole((rank, heads)), whole((rank, width)),
        ],
        [
            wide_out(), shape((tokens, n2), BF16), shape((tokens, rank), BF16),
            wide_out(F32, rank), shape((rank, n2), F32),
            shape((rank, heads), F32), shape((rank, width), F32),
        ],
        [
            pltpu.VMEM((ext, SUB), F32), pltpu.VMEM((tokens, rank), F32),
            pltpu.VMEM((rank, tokens), BF16), pltpu.VMEM((groups, rank, group_rows), F32),
        ],
        10,
    )(
        scalars, c_all, c_halo[:, :inner], cmap, c_halo[:, inner:], glow_gate, conv_w,
        conv_map_weight, ainner, amap, astep, gstep, low, low_f, nrm, cols,
    )

    input_grad = call(
        functools.partial(input_kernel, plan_in, nz),
        nz,
        [
            whole((tokens, width)), by_slot(tokens), whole(gmap.shape), whole(gstep.shape),
            whole(glow.shape), whole(small_full.shape), whole(down.shape),
            whole(x.shape), whole(cot.shape), whole(scale.shape), whole((1, width)),
        ]
        + [anywhere] * n_w,
        whole(x.shape),
        shape(x.shape, F32),
        [pltpu.VMEM((tokens, width), F32), parts_scratch] + weight_scratch(),
        14,
    )(
        scalars, start, gi, gmap, gstep, glow, small_full, down, x, cot, scale,
        norm_gain[None], *w_inner,
    )

    shared = jnp.concatenate([tab_down, tab_up, tab_map], axis=1)

    def slot_pack(k):
        at = slice(k * part, (k + 1) * part)
        steps = tab_step[:, k * heads_here : (k + 1) * heads_here]
        pack = [tab_gate[:, at], tab_inner[:, at], tab_mixed[:, at], shared, steps]
        return jnp.concatenate(pack, axis=1)

    total = slot_pack(0)
    for k in range(1, nz):
        total = total + around(slot_pack(k).astype(BF16), -k, nz).astype(F32)
    layer_out = call(
        functools.partial(out_kernel, plan_out, nz),
        nz,
        [
            whole(x.shape), by_slot(tokens), whole(up.shape), whole(r_gate.shape),
            whole((tokens, rank)),
        ]
        + [anywhere] * n_w,
        whole(x.shape),
        shape(x.shape, BF16),
        [pltpu.VMEM((tokens, width), F32), parts_scratch] + weight_scratch(),
        12,
    )(scalars, x, after(gg, total), up, r_gate, mixed_low, *w_out)

    picked = jnp.broadcast_to(pick.astype(F32), (rank, 1))
    total = jnp.concatenate([total, picked], axis=1).astype(BF16)
    if chip_plan:
        every = jnp.stack([total] + [xor(total, m, ndp) for m in range(1, ndp)])
    else:
        every = lax.all_gather(total, "dp")
    every = every.astype(F32)
    hot = (every[:, 0, -1][:, None] == jnp.arange(adapters)[None, :].astype(F32)).astype(F32)
    summed = jnp.einsum("sa,src->arc", hot, every, precision=EXACT)
    grad_inner = summed[:, :, : 2 * part].reshape(adapters, rank, 2, part)
    grad_mixed = jnp.swapaxes(summed[:, :, 2 * part : 3 * part], 1, 2)
    at = 3 * part
    grad_down = jnp.swapaxes(summed[:, :, at : at + width], 1, 2)
    grad_up = summed[:, :, at + width : at + 2 * width]
    at = at + 2 * width
    grad_map = summed[:, :, at : at + n2]
    grad_step = summed[:, :, at + n2 : at + n2 + heads_here]
    return (
        layer_out[None], input_grad[None], grad_down, grad_inner, grad_map, grad_step, grad_mixed, grad_up
    )


def solution(mesh):
    return jax.shard_map(
        shards,
        mesh=mesh,
        in_specs=(
            P("dp", "tensor", None),
            P("dp", "tensor", None),
            P("dp", None),
            P("dp"),
            P(),
            P("dp", None, "tensor"),
            P("dp", None),
            P("dp", "tensor"),
            P(None, "tensor"),
            P("tensor"),
            P(),
            P(),
            P("tensor"),
            P("tensor"),
            P("tensor"),
            P("tensor"),
            P("tensor", "dp"),
            P(),
            P(None, None, None, "tensor"),
            P(),
            P(None, None, "tensor"),
            P(None, "tensor", None),
            P(),
        ),
        out_specs=(
            P("dp", "tensor", None),
            P("dp", "tensor", None),
            P(),
            P(None, None, None, "tensor"),
            P(),
            P(None, None, "tensor"),
            P(None, "tensor", None),
            P(),
        ),
        check_vma=False,
    )
```

```python
import functools

import jax
import jax.numpy as jnp
from jax import lax
from jax.experimental import pallas as pl
from jax.experimental.pallas import tpu as pltpu
from jax.sharding import PartitionSpec as P

EPSILON = 1e-05
HALO = 16
CHUNK = 128
SUB = 256
DOC_MOST = 800
LOG2E = 1.4426950408889634
F32 = jnp.float32
BF16 = jnp.bfloat16
EXACT = lax.Precision.HIGHEST


def dot(a, b, precision=None):
    return lax.dot_general(
        a, b, (((1,), (0,)), ((), ())), precision=precision, preferred_element_type=F32
    )


def dot_nt(a, b, precision=None):
    return lax.dot_general(
        a, b, (((1,), (1,)), ((), ())), precision=precision, preferred_element_type=F32
    )


def sigmoid(v):
    return 0.5 * jnp.tanh(0.5 * v) + 0.5


def split3(v):
    hi = v.astype(BF16)
    rest = v - hi.astype(F32)
    mid = rest.astype(BF16)
    lo = (rest - mid.astype(F32)).astype(BF16)
    return jnp.concatenate([hi, mid, lo], axis=1)


def spread_matrix(heads, cols, base, width):
    k = lax.broadcasted_iota(jnp.int32, (3 * heads, cols), 0)
    k = jnp.where(k >= 2 * heads, k - 2 * heads, jnp.where(k >= heads, k - heads, k))
    l = lax.broadcasted_iota(jnp.int32, (3 * heads, cols), 1)
    return jnp.where(k == base + l // width, 1.0, 0.0).astype(BF16)


def row_matrix(heads, rows, base):
    k = lax.broadcasted_iota(jnp.int32, (rows, 3 * heads), 1)
    k = jnp.where(k >= 2 * heads, k - 2 * heads, jnp.where(k >= heads, k - heads, k))
    i = lax.broadcasted_iota(jnp.int32, (rows, 3 * heads), 0)
    return jnp.where(k == base + i, 1.0, 0.0).astype(BF16)


def row_picks(groups, width, kind=BF16):
    row = lax.broadcasted_iota(jnp.int32, (8, groups * width), 0)
    lane = lax.broadcasted_iota(jnp.int32, (8, groups * width), 1)
    return jnp.where(row == lane // width, 1.0, 0.0).astype(kind)


def head_rows(ref, heads, each, lanes=None, only=None):
    blocks, _, columns = ref.shape
    flat = ref[...].reshape(blocks * 8, columns)
    if lanes is not None:
        flat = jnp.concatenate([flat[:, at : at + CHUNK] for at in lanes], axis=1)
    head = lax.broadcasted_iota(jnp.int32, (heads, blocks * 8), 0)
    row = lax.broadcasted_iota(jnp.int32, (heads, blocks * 8), 1)
    inside = lax.rem(head, each)
    if only is None:
        pick = row == head // each * 8 + inside
    else:
        pick = (row == head // each * 8) & (inside == only)
    return dot(jnp.where(pick, 1.0, 0.0), flat, precision=EXACT)


def two_heads(v, lane_low):
    return jnp.concatenate(
        [jnp.where(lane_low, v, 0.0), jnp.where(lane_low, 0.0, v)], axis=0
    ).astype(BF16)


def triangle(strict_upper=False):
    r = lax.broadcasted_iota(jnp.int32, (CHUNK, CHUNK), 0)
    c = lax.broadcasted_iota(jnp.int32, (CHUNK, CHUNK), 1)
    keep = (r < c) if strict_upper else (r >= c)
    return jnp.where(keep, 1.0, 0.0)


def conv_forward(buffer, tokens, weight, bias, cols):
    result = bias + weight[0:1] * buffer[HALO : HALO + tokens, :]
    for lag in range(1, 4):
        moved = buffer[HALO - lag : HALO - lag + tokens, :]
        result = result + weight[lag : lag + 1] * (moved * cols[:, lag - 1 : lag])
    return result


def fetch(plan, refs, buffer, sems, slot, k, wait=False):
    for at, entries in enumerate(plan):

        @pl.when(k == at)
        def _(entries=entries):
            for index, (which, lead, source, rows, place) in enumerate(entries):
                copy = pltpu.make_async_copy(
                    refs[which].at[lead, pl.ds(source, rows)],
                    buffer.at[slot, pl.ds(place, rows)],
                    sems.at[slot, index],
                )
                copy.wait() if wait else copy.start()


def pieces_of(plan):
    return 1 + max(entry[0] for entries in plan for entry in entries)


def stream(plan, refs, buffer, sems, j, first, last, k):
    slot = lax.rem(j, 2)

    @pl.when(j == first)
    def _():
        fetch(plan, refs, buffer, sems, slot, k)

    @pl.when(j + 1 < last)
    def _():
        fetch(plan, refs, buffer, sems, 1 - slot, k + 1)

    fetch(plan, refs, buffer, sems, slot, k, wait=True)
    return slot


def reorder(parts, source, shift, inverse=False):
    groups, _, width = parts.shape
    for g in range(groups):
        parts[g ^ shift] = source[:, g * width : (g + 1) * width]
    return jnp.concatenate([parts[g] for g in range(groups)], axis=1)


def lanes_of(i):
    return pl.ds(pl.multiple_of(i * SUB, SUB), SUB)


def chunk_rows(c):
    return slice(c * CHUNK, (c + 1) * CHUNK)


def allowed_mask(cols, rows, c, transposed=False):
    r = lax.broadcasted_iota(jnp.int32, (CHUNK, CHUNK), 0)
    l = lax.broadcasted_iota(jnp.int32, (CHUNK, CHUNK), 1)
    same = cols[chunk_rows(c), 7:8] == rows[0:1, chunk_rows(c)]
    return same & ((r <= l) if transposed else (r >= l))


def added(refs, lanes):
    total = refs[0][:, lanes].astype(F32)
    for ref in refs[1:]:
        total = total + ref[:, lanes].astype(F32)
    return total


def transpose(v):
    return v.astype(F32).T.astype(BF16)


def front_kernel(
    n_small, scalars, x, halo, gain, down, amap, astep, cmw, cmb, sbias, dlog, cols, *rest
):
    small_refs, rest = rest[:n_small], rest[n_small:]
    nrm, scale, low, low_out, maps, pre_map, quant, sig_out, small, buffer, parts = rest
    tokens, n2 = maps.shape
    heads = sig_out.shape[1]
    lead, half, _ = small_refs[0].shape
    columns = small.shape[1]
    for g in range(lead):
        for b in range(n_small):
            at = (g * n_small + b) * 2 * half
            small[at : at + half] = small_refs[b][g, :, :columns]
            small[at + half : at + 2 * half] = small_refs[b][g, :, columns:]
    before = jnp.concatenate([halo[:HALO], halo[HALO:]], axis=1).astype(F32)
    before = jnp.where(scalars[1] > 0, before, 0.0)
    xf = jnp.concatenate([before, x[...].astype(F32)], axis=0)
    q = lax.rsqrt(jnp.mean(xf * xf, axis=-1, keepdims=True) + EPSILON)
    normed = (xf * q * gain[...]).astype(BF16)
    scale[...] = jnp.broadcast_to(q[HALO:], scale.shape)
    adapter_low = dot(normed, down[...])
    low_out[...] = adapter_low[HALO:]
    adapter_low = adapter_low.astype(BF16)
    low[...] = adapter_low
    ordered = reorder(parts, normed, scalars[0])
    nrm[...] = ordered
    buffer[...] = dot(ordered, small[:, :n2]) + dot(adapter_low, amap[...])
    pre = conv_forward(buffer, tokens, cmw[...], cmb[...], cols[...])
    pre_map[...] = pre
    maps[...] = (pre * sigmoid(pre)).astype(BF16)
    raw = dot(ordered[HALO:], small[:, n2 : n2 + heads]) + sbias[...]
    raw = raw + dot(adapter_low[HALO:], astep[...])
    step = jnp.maximum(raw, 0.0) + jnp.log(1.0 + jnp.exp(-jnp.abs(raw)))
    sig_out[...] = sigmoid(raw)
    rate = -jnp.exp(dlog[...])
    drop = step * rate * LOG2E
    lower = triangle()
    sums = []
    for c in range(tokens // CHUNK):
        sums.append(dot(lower, drop[c * CHUNK : (c + 1) * CHUNK], precision=EXACT))
    base = jnp.zeros_like(sums[0][0:1])
    bases = []
    for c in range(tokens // CHUNK):
        bases.append(base)
        base = base + sums[c][CHUNK - 1 : CHUNK]
    column = cols[...]
    cum = jnp.concatenate(sums, axis=0)
    whole = jnp.concatenate([s + b for s, b in zip(sums, bases)], axis=0)
    left = jnp.concatenate([s[CHUNK - 1 : CHUNK] - s for s in sums], axis=0)
    quant[0] = split3(cum)
    quant[1] = split3(step)
    quant[2] = split3(jnp.exp2(cum) * column[:, 3:4])
    quant[3] = split3(jnp.exp2(left) * column[:, 4:5])
    quant[4] = split3(jnp.exp2(whole) * column[:, 5:6])
    quant[5] = split3(jnp.exp2(base - whole) * column[:, 6:7])


def values_kernel(
    heads, plan, first, count, scalars, nrm, low, aw, cw, cb, maps, quant, cols, rows, *rest
):
    n_w = pieces_of(plan)
    w_refs, rest = rest[:n_w], rest[-10:]
    values, pre_out, y_out, s_out, masked, in_t, buffer, wide_buffer, wbuf, sems = rest
    j = pl.program_id(0)
    slot = stream(plan, w_refs, wbuf, sems, j, 0, count, j + first)
    tokens = maps.shape[0]
    chunks = tokens // CHUNK
    n = maps.shape[1] // 2

    @pl.when(j == 0)
    def _():
        for c in range(chunks):
            b = maps[chunk_rows(c), :n]
            scores = dot_nt(maps[chunk_rows(c), n:], b)
            masked[c] = jnp.where(allowed_mask(cols, rows, c), scores, 0.0)
            in_t[c] = transpose(b)
        for lag in range(3):
            wide_buffer[lag] = jnp.broadcast_to(cols[:, lag : lag + 1], wide_buffer.shape[1:])

    buffer[...] = dot(nrm[...], wbuf[slot]) + dot(low[...], aw[...])
    subs = buffer.shape[1] // SUB
    lane_low = lax.broadcasted_iota(jnp.int32, (CHUNK, 128), 1) < 64

    def body(i, carry):
        lanes = lanes_of(i)
        base = ((j + first) * subs + i) * (SUB // 64)
        weight = cw[:, lanes]
        pre = cb[:, lanes] + weight[0:1] * buffer[HALO : HALO + tokens, lanes]
        for lag in range(1, 4):
            keep = jnp.concatenate([wide_buffer[lag - 1]] * 2, axis=1)
            moved = buffer[HALO - lag : HALO - lag + tokens, lanes]
            pre = pre + weight[lag : lag + 1] * (moved * keep)
        pre_out[:, lanes] = pre.astype(BF16)
        v = (pre * sigmoid(pre)).astype(BF16)
        values[:, lanes] = v
        wide = spread_matrix(heads, SUB, base, 64)
        v = v.astype(F32)
        vp = dot(quant[1], wide) * v
        row = dot_nt(row_matrix(heads, 8, base), quant[0])
        pair_wide = [spread_matrix(heads, 2 * CHUNK, base + 2 * p, CHUNK) for p in range(2)]
        state = None
        for c in range(chunks):
            rs = chunk_rows(c)
            cum_c = quant[0, rs]
            mask2 = jnp.concatenate([masked[c], masked[c]], axis=1)
            inside = []
            for p in range(2):
                r2 = jnp.concatenate(
                    [row[2 * p : 2 * p + 1, rs], row[2 * p + 1 : 2 * p + 2, rs]], axis=1
                )
                decay = jnp.exp2(jnp.minimum(dot(cum_c, pair_wide[p]) - r2, 0.0))
                vbd = two_heads(vp[rs, p * 128 : (p + 1) * 128], lane_low)
                inside.append(dot((decay * mask2).astype(BF16), vbd))
            y = jnp.concatenate(inside, axis=1)
            enter = dot(quant[2, rs], wide)
            if c > 0:
                y = y + enter * dot(maps[rs, n:], state.astype(BF16))
            y_out[rs, lanes] = y.astype(y_out.dtype)
            end = dot(quant[3, rs], wide)
            fresh = dot(in_t[c], (end * vp[rs]).astype(BF16))
            state = fresh if c == 0 else state * enter[CHUNK - 1 : CHUNK] + fresh
        s_out[:, lanes] = state.astype(s_out.dtype)
        return carry

    lax.fori_loop(0, subs, body, 0)


def gate_kernel(plan, count, scalars, nrm, low, aw, *rest):
    n_w = pieces_of(plan)
    w_refs, (gate_out, wbuf, sems) = rest[:n_w], rest[n_w:]
    j = pl.program_id(0)
    slot = stream(plan, w_refs, wbuf, sems, j, 0, count, j)
    gate = dot(nrm[HALO:], wbuf[slot]) + dot(low[HALO:], aw[...])
    gate_out[...] = gate.astype(BF16)


def gated_kernel(
    heads, plan, count, n_s, scalars, cot, up, amixed, gate, y_in, values, skip, gain, quant, maps, *rest
):
    n_w = pieces_of(plan)
    states, w_refs, rest = rest[:n_s], rest[n_s : n_s + n_w], rest[n_s + n_w :]
    gg_out, r_out, gy_out, gz_out, g_out, mlow_out, tab_up, tab_mixed, *rest = rest
    grad, ys, ggs, squares, inner, parts, cot_x, out_t, gml, low, scaled, wbuf, sems = rest
    j = pl.program_id(0)
    n = maps.shape[1] // 2
    part = gate.shape[1]
    subs = part // SUB

    @pl.when(j == 0)
    def _():
        gml[...] = dot_nt(cot[...], up[...])
        low[...] = jnp.zeros_like(low)
        inner[...] = jnp.zeros_like(inner)
        squares[...] = jnp.zeros_like(squares)
        cot_x[...] = reorder(parts, cot, scalars[0])
        out_t[...] = transpose(maps[:, n:])

    @pl.when(j < count)
    def _():
        slot = stream(plan, w_refs, wbuf, sems, j, 0, count, j)
        grad[j] = dot(cot_x[...], wbuf[slot]) + dot(gml[...].astype(BF16), amixed[...])

        def body(i, carry):
            lanes = lanes_of(i)
            wide = spread_matrix(heads, SUB, (j * subs + i) * (SUB // 64), 64)
            g = gate[:, lanes].astype(F32)
            state = added(states, lanes).astype(BF16)
            entering = dot(quant[0], wide) * dot(maps[:, n:], state)
            y = y_in[:, lanes].astype(F32) + entering
            y = y + skip[:, lanes] * values[:, lanes].astype(F32)
            ys[j, :, lanes] = y
            gated = y * (g * sigmoid(g))
            scaled_up = (gated * gain[:, lanes]).astype(BF16)
            ggs[j, :, lanes] = scaled_up
            gg_out[:, lanes] = scaled_up
            square = gated * gated
            squares[...] += square[:, :128] + square[:, 128:]
            term = scaled_up.astype(F32) * grad[j, :, lanes]
            inner[...] += term[:, :128] + term[:, 128:]
            return carry

        lax.fori_loop(0, subs, body, 0)
        low[...] += dot_nt(ggs[j], amixed[...])

    @pl.when(j >= count)
    def _():
        k = j - count
        size = count * part
        r = lax.rsqrt(jnp.sum(squares[...], axis=-1, keepdims=True) / size + EPSILON)
        cube = r * r * r * (jnp.sum(inner[...], axis=-1, keepdims=True) / size)

        @pl.when(k == 0)
        def _():
            r_out[...] = jnp.broadcast_to(r, r_out.shape)
            scaled[...] = transpose(gml[...] * r)
            mixed_low = low[...] * r
            mlow_out[...] = mixed_low.astype(BF16)
            tab_up[...] = dot(transpose(mixed_low), cot[...])

        tab_mixed[...] = dot(scaled[...], ggs[k])

        def body(i, carry):
            lanes = lanes_of(i)
            g = gate[:, lanes].astype(F32)
            y = ys[k, :, lanes]
            s = sigmoid(g)
            act = g * s
            grad_gated = (grad[k, :, lanes] * gain[:, lanes]) * r - y * act * cube
            gy = grad_gated * act
            gy_out[:, lanes] = gy.astype(BF16)
            gz_out[:, lanes] = (grad_gated * y * (s * (1.0 + g * (1.0 - s)))).astype(BF16)
            enter = dot(quant[0], spread_matrix(heads, SUB, (k * subs + i) * (SUB // 64), 64))
            g_out[:, lanes] = dot(out_t[...], (enter * gy).astype(BF16)).astype(g_out.dtype)
            return carry

        lax.fori_loop(0, subs, body, 0)


def backward_kernel(
    heads, count, n_s, scalars, values, gy_in, maps, quant, cols, rows, *rest
):
    s_refs, rest = rest[:n_s], rest[n_s:]
    dx_out, gmaps_out, r_out, masked, allowed, mixed, grad_b, grad_c, *rest = rest
    col_p, row_p, carry_a, carry_b, ends, in_b, out_b = rest
    j = pl.program_id(0)
    tokens = maps.shape[0]
    chunks = tokens // CHUNK
    n = maps.shape[1] // 2
    subs = values.shape[1] // SUB

    @pl.when(j == 0)
    def _():
        for c in range(chunks):
            rs = chunk_rows(c)
            ok = allowed_mask(cols, rows, c, transposed=True)
            scores = dot_nt(maps[rs, :n], maps[rs, n:])
            masked[c] = jnp.where(ok, scores, 0.0)
            allowed[c] = jnp.where(ok, 1.0, 0.0)
            in_b[c] = transpose(maps[rs, :n])
            out_b[c] = transpose(maps[rs, n:])
        for ref in (mixed, grad_b, grad_c, carry_b, ends):
            ref[...] = jnp.zeros_like(ref)

    lane_low = lax.broadcasted_iota(jnp.int32, (CHUNK, 128), 1) < 64
    ones = jnp.ones((8, CHUNK), BF16)
    by_pair = row_picks(2, CHUNK)
    by_head = row_picks(SUB // 64, 64)
    by_head_f = row_picks(SUB // 64, 64, F32)

    def body(i, carry):
        lanes = lanes_of(i)
        block = j * subs + i
        base = block * (SUB // 64)
        wide = spread_matrix(heads, SUB, base, 64)
        vp = dot(quant[1], wide) * values[:, lanes].astype(F32)
        row = dot_nt(row_matrix(heads, 8, base), quant[0])
        pair_wide = [spread_matrix(heads, 2 * CHUNK, base + 2 * p, CHUNK) for p in range(2)]
        enters, lefts, states = [], [], []
        state = added(s_refs, lanes)
        for c in range(chunks):
            rs = chunk_rows(c)
            enters.append(dot(quant[2, rs], wide))
            lefts.append(dot(quant[3, rs], wide))
            states.append(state)
            if c < chunks - 1:
                fresh = dot(in_b[c], (lefts[c] * vp[rs]).astype(BF16))
                state = state * enters[c][CHUNK - 1 : CHUNK] + fresh
        adjoint = None
        for c in range(chunks - 1, -1, -1):
            rs = chunk_rows(c)
            cum_c = quant[0, rs]
            gy = gy_in[rs, lanes].astype(F32)
            mask2 = jnp.concatenate([masked[c], masked[c]], axis=1)
            dx = []
            for p in range(2):
                pair = slice(p * 128, (p + 1) * 128)
                r2 = jnp.concatenate(
                    [row[2 * p : 2 * p + 1, rs], row[2 * p + 1 : 2 * p + 2, rs]], axis=1
                )
                decay = jnp.exp2(jnp.minimum(r2 - dot(cum_c, pair_wide[p]), 0.0))
                gbd = two_heads(gy[:, pair], lane_low)
                dx.append(dot((decay * mask2).astype(BF16), gbd))
                part = decay * dot_nt(vp[rs, pair].astype(BF16), gbd)
                mixed[c] += part[:, :CHUNK] + part[:, CHUNK:]
                weighed = (part * mask2).astype(BF16)
                col_p[block * 2 + p, :, rs] = dot_nt(by_pair, weighed)
                row_p[block * 2 + p, :, 2 * c * CHUNK : 2 * (c + 1) * CHUNK] = dot(ones, weighed)
            dx = jnp.concatenate(dx, axis=1)
            entering = enters[c] * gy
            carried = entering * dot(maps[rs, n:], states[c].astype(BF16))
            carry_a[block, :, rs] = dot_nt(by_head, carried.astype(BF16))
            entering = entering.astype(BF16)
            grad_c[rs] += dot_nt(entering, states[c].astype(BF16))
            last = enters[c][CHUNK - 1 : CHUNK]
            if adjoint is not None:
                adj = adjoint.astype(BF16)
                leaving = lefts[c] * dot(maps[rs, :n], adj)
                dx = dx + leaving
                carry_b[block, :, rs] = dot_nt(by_head, (vp[rs] * leaving).astype(BF16))
                grad_b[rs] += dot_nt((lefts[c] * vp[rs]).astype(BF16), adj)
                through = jnp.sum(adjoint * states[c], axis=0, keepdims=True) * last
                through = jnp.sum(by_head_f * through, axis=1, keepdims=True)
                ends[block, :, rs] = jnp.broadcast_to(through, (8, CHUNK))
            dx_out[rs, lanes] = dx.astype(dx_out.dtype)
            if c > 0:
                fresh = dot(out_b[c], entering)
                adjoint = fresh if adjoint is None else adjoint * last + fresh
        return carry

    lax.fori_loop(0, subs, body, 0)

    @pl.when(j == count - 1)
    def _():
        suffix, prefix = triangle(), triangle(strict_upper=True)
        plain = head_rows(carry_a, heads, SUB // 64) - head_rows(col_p, heads, 2)
        for q in range(2):
            lanes = [(2 * c + q) * CHUNK for c in range(chunks)]
            plain = plain + head_rows(row_p, heads, 2, lanes, q)
        left = head_rows(carry_b, heads, SUB // 64)
        sums = head_rows(ends, heads, SUB // 64)
        for c in range(chunks):
            rs = chunk_rows(c)
            w = mixed[c] * allowed[c]
            gb = grad_b[rs] + dot(w.astype(BF16), maps[rs, n:])
            gc = grad_c[rs] + dot(w.T.astype(BF16), maps[rs, :n])
            gmaps_out[rs] = jnp.concatenate([gb, gc], axis=1)
            r_out[:, rs] = (
                dot(plain[:, rs], suffix, precision=EXACT)
                + dot(left[:, rs], prefix, precision=EXACT)
                + sums[:, rs]
            )


def finish_kernel(
    heads, count, n_s, scalars, values, dx_in, gy_in, pre, maps, quant_step, quant_enter, quant_left,
    skip, gmaps, r_in, sig, dlog, pre_map, *rest
):
    s_refs, g_refs, rest = rest[:n_s], rest[n_s : 2 * n_s], rest[2 * n_s :]
    c_out, cmap_out, gstep_out, col_g, carry_b, grad_b, ends = rest
    j = pl.program_id(0)
    tokens = maps.shape[0]
    n = maps.shape[1] // 2
    subs = values.shape[1] // SUB

    @pl.when(j == 0)
    def _():
        grad_b[...] = jnp.zeros_like(grad_b)

    by_head = row_picks(SUB // 64, 64)
    by_head_f = row_picks(SUB // 64, 64, F32)

    def body(i, carry):
        lanes = lanes_of(i)
        base = (j * subs + i) * (SUB // 64)
        wide = spread_matrix(heads, SUB, base, 64)
        block = j * subs + i
        v = values[:, lanes].astype(F32)
        step = dot(quant_step[0], wide)
        left = dot(quant_left[0], wide)
        vp = step * v
        adjoint = added(g_refs, lanes)
        both = adjoint * added(s_refs, lanes)
        adjoint = adjoint.astype(BF16)
        more = left * dot(maps[:, :n], adjoint)
        dx = dx_in[:, lanes].astype(F32) + more
        carry_b[block] = dot_nt(by_head, (vp * more).astype(BF16))
        col_g[block] = dot_nt(by_head, (v * dx).astype(BF16))
        grad_b[...] += dot_nt((left * vp).astype(BF16), adjoint)
        last = dot(quant_enter[0, tokens - 16 :], wide)[15:16]
        through = jnp.sum(both, axis=0, keepdims=True) * last
        through = jnp.sum(by_head_f * through, axis=1, keepdims=True)
        ends[block] = jnp.broadcast_to(through, (8, CHUNK))
        dv = step * dx + skip[:, lanes] * gy_in[:, lanes].astype(F32)
        pre_f = pre[:, lanes].astype(F32)
        s = sigmoid(pre_f)
        c_out[:, lanes] = (dv * (s * (1.0 + pre_f * (1.0 - s)))).astype(BF16)
        return carry

    lax.fori_loop(0, subs, body, 0)

    @pl.when(j == count - 1)
    def _():
        prefix = triangle(strict_upper=True)
        run = head_rows(ends, heads, SUB // 64)
        left = head_rows(carry_b, heads, SUB // 64)
        grads = head_rows(col_g, heads, SUB // 64)
        rate = -jnp.exp(dlog[...]).T
        for c in range(tokens // CHUNK):
            rs = chunk_rows(c)
            total = r_in[:, rs] + dot(left[:, rs], prefix, precision=EXACT) + run
            run = run + jnp.sum(left[:, rs], axis=1, keepdims=True)
            raw = grads[:, rs] + rate * total
            gstep_out[rs] = (raw.T * sig[rs]).astype(BF16)
        gb = gmaps[:, :n] + grad_b[...]
        g = jnp.concatenate([gb, gmaps[:, n:]], axis=1)
        pm = pre_map[...]
        sm = sigmoid(pm)
        cmap_out[...] = (g * (sm * (1.0 + pm * (1.0 - sm)))).astype(cmap_out.dtype)


def conv_backward(buffer, tokens, weight, cols):
    result = weight[0:1] * buffer[0:tokens, :]
    for lag in range(1, 4):
        result = result + weight[lag : lag + 1] * (
            buffer[lag : lag + tokens, :] * cols[:, 7 + lag : 8 + lag]
        )
    return result


def tables_kernel(
    count, heads_here, scalars, c_in, c_halo, cmap, cmap_halo, glow_in, tab_gate, tab_mixed, tab_up, cw, cmw, ainner,
    amap, astep, gstep, low, low_f, nrm, cols, gi_out, gmap_out, glow_out, *rest
):
    packs, (buffer, glow, low_t, parts) = rest[:count], rest[count:]
    j = pl.program_id(0)
    tokens = gi_out.shape[0]
    subs = gi_out.shape[1] // SUB

    @pl.when(j == 0)
    def _():
        low_t[...] = transpose(low[HALO:])
        buffer[:tokens] = cmap[...].astype(F32)
        buffer[tokens:] = cmap_halo[...].astype(F32)
        gmap = conv_backward(buffer, tokens, cmw[...], cols[...])
        exact_low = low_f[...].T
        tab_map = dot(exact_low, gmap, precision=EXACT)
        tab_step = dot(exact_low, gstep[...].astype(F32), precision=EXACT)
        rank = tab_map.shape[0]
        lane = lax.broadcasted_iota(jnp.int32, (rank, 128), 1)
        last = packs[0].shape[1] - 128
        for k, pack in enumerate(packs):
            steps = tab_step[:, k * heads_here : (k + 1) * heads_here]
            steps = jnp.concatenate([steps, jnp.zeros((rank, 128 - heads_here), F32)], axis=1)
            if k == 0:
                steps = jnp.where(lane == heads_here, scalars[3].astype(F32), steps)
            pack[:, last:] = steps.astype(BF16)
            pack[:, last - tab_map.shape[1] : last] = tab_map.astype(BF16)
        gmap = gmap.astype(BF16)
        gmap_out[...] = gmap
        glow[...] = glow_in[...] + dot_nt(gmap, amap[...]) + dot_nt(gstep[...], astep[...])

    def body(i, carry):
        lanes = lanes_of(i)
        buffer[:tokens] = c_in[:, lanes].astype(F32)
        buffer[tokens:] = c_halo[:, lanes].astype(F32)
        gi_out[:, lanes] = conv_backward(buffer, tokens, cw[:, lanes], cols[...]).astype(BF16)
        return carry

    lax.fori_loop(0, subs, body, 0)
    glow[...] += dot_nt(gi_out[...], ainner[...])
    tab_inner = dot(low_t[...], gi_out[...])
    part = gi_out.shape[1]
    for k, pack in enumerate(packs):

        @pl.when(j == k)
        def _(pack=pack):
            pack[:, :part] = tab_gate[...].astype(BF16)
            pack[:, part : 2 * part] = tab_inner.astype(BF16)
            pack[:, 2 * part : 3 * part] = tab_mixed[...].astype(BF16)

    @pl.when(j == count - 1)
    def _():
        glow_out[...] = glow[...].astype(BF16)
        down = dot(transpose(glow[...]), nrm[HALO:])
        down = reorder(parts, down, scalars[0]).astype(BF16)
        width = down.shape[1]
        for pack in packs:
            pack[:, 3 * part : 3 * part + width] = down
            pack[:, 3 * part + width : 3 * part + 2 * width] = tab_up[...].astype(BF16)


def out_kernel(plan, count, scalars, x, gg, up, r_in, mlow, *rest):
    n_w = pieces_of(plan)
    w_refs = rest[:n_w]
    out, total, parts, wbuf, sems = rest[n_w:]
    j = pl.program_id(0)
    slot = stream(plan, w_refs, wbuf, sems, j, 0, count, j)
    term = dot_nt(gg[...], wbuf[slot])

    @pl.when(j == 0)
    def _():
        total[...] = term

    @pl.when(j > 0)
    def _():
        total[...] += term

    @pl.when(j == count - 1)
    def _():
        branch = reorder(parts, total, scalars[0]) * r_in[:, 0:1]
        out[...] = (x[...].astype(F32) + branch + dot(mlow[...], up[...])).astype(BF16)


def gate_rows_kernel(plan, count, scalars, gz, agate, low, *rest):
    n_w = pieces_of(plan)
    w_refs = rest[:n_w]
    total, glow, tab_gate, low_t, wbuf, sems = rest[n_w:]
    j = pl.program_id(0)
    slot = stream(plan, w_refs, wbuf, sems, j, 0, count, j)

    @pl.when(j == 0)
    def _():
        low_t[...] = transpose(low[HALO:])

    term = dot_nt(gz[...], wbuf[slot])
    thin = dot_nt(gz[...], agate[...])
    tab_gate[...] = dot(low_t[...], gz[...])

    @pl.when(j == 0)
    def _():
        total[...] = term
        glow[...] = thin

    @pl.when(j > 0)
    def _():
        total[...] += term
        glow[...] += thin


def input_kernel(
    plan, count, scalars, start, gi, gmap, gstep, glow, small, down, x, cot, scale, gain, *rest
):
    n_w = pieces_of(plan)
    w_refs = rest[:n_w]
    out, total, parts, wbuf, sems = rest[n_w:]
    j = pl.program_id(0)
    slot = stream(plan, w_refs, wbuf, sems, j, 0, count, j)

    @pl.when(j == 0)
    def _():
        n2, heads = gmap.shape[1], gstep.shape[1]
        total[...] = (
            start[...]
            + dot_nt(gmap[...], small[:, :n2])
            + dot_nt(gstep[...], small[:, n2 : n2 + heads])
        )

    total[...] += dot_nt(gi[...], wbuf[slot])

    @pl.when(j == count - 1)
    def _():
        q = scale[:, 0:1]
        xf = x[...].astype(F32)
        normed_grad = reorder(parts, total, scalars[0]) + dot_nt(glow[...], down[...])
        weighted = normed_grad * gain[...]
        mean = jnp.mean(xf * weighted, axis=-1, keepdims=True)
        out[...] = q * weighted - xf * (q * q * q * mean) + cot[...].astype(F32)


def whole(shape):
    return pl.BlockSpec(shape, lambda *_: (0,) * len(shape))


def call(kernel, steps, in_specs, out_specs, out_shape, scratch, micros, aliases=None):
    return pl.pallas_call(
        kernel,
        grid_spec=pltpu.PrefetchScalarGridSpec(
            num_scalar_prefetch=1,
            grid=(steps,),
            in_specs=in_specs,
            out_specs=out_specs,
            scratch_shapes=scratch,
        ),
        out_shape=out_shape,
        input_output_aliases=aliases or {},
        compiler_params=pltpu.CompilerParams(
            dimension_semantics=("arbitrary",), vmem_limit_bytes=56 * 2**20
        ),
        cost_estimate=pl.CostEstimate(
            flops=int(micros * 1.1e9), bytes_accessed=int(micros * 1e6), transcendentals=0
        ),
    )


def shape(dims, kind):
    return jax.ShapeDtypeStruct(dims, kind)


def xor(v, m, ndp):
    return lax.ppermute(v, "dp", [(i, i ^ m) for i in range(ndp)])


def around(v, k, nz):
    return lax.ppermute(v, "tensor", [(i, (i + k) % nz) for i in range(nz)])


def all_slots(v, nz):
    return [v] + [around(v, k, nz) for k in range(1, nz)]


def after(v, *others):
    return lax.optimization_barrier((v, others))[0]


def split_rows(v):
    high = lax.optimization_barrier(v.astype(BF16))
    rest = v - high.astype(F32)
    middle = lax.optimization_barrier(rest.astype(BF16))
    return jnp.concatenate([high, middle, (rest - middle.astype(F32)).astype(BF16)], axis=0)


def joined_rows(v):
    high, middle, low = jnp.split(v.astype(F32), 3, axis=0)
    return high + middle + low


def shards(
    layer_in,
    cotangent,
    segment_ids,
    adapter_ids,
    norm_gain,
    inner_weight,
    map_weight,
    step_weight,
    conv_inner_weight,
    conv_inner_bias,
    conv_map_weight,
    conv_map_bias,
    step_bias,
    decay_log,
    skip_gain,
    gate_gain,
    out_weight,
    adapter_down,
    adapter_inner,
    adapter_map,
    adapter_step,
    adapter_mixed,
    adapter_up,
):
    ndp, nz = lax.axis_size("dp"), lax.axis_size("tensor")
    z = lax.axis_index("tensor")
    x, cot = layer_in[0], cotangent[0]
    tokens, width = x.shape
    rows_here = inner_weight.shape[0]
    part = gate_gain.shape[0]
    inner = part * nz
    heads_here = step_bias.shape[0]
    heads = heads_here * nz
    adapters, _, rank = adapter_down.shape
    n2 = map_weight.shape[1]
    n = n2 // 2
    chunks = tokens // CHUNK
    ext = tokens + HALO
    nq = 3 * heads
    up_one = [(i, i + 1) for i in range(nz - 1)]
    down_one = [(i + 1, i) for i in range(nz - 1)]
    chip_plan = ndp == 8 and nz == 4 and rows_here % 64 == 0

    pick = adapter_ids[0]
    tail = x[tokens - HALO :]
    thin_rows = jnp.concatenate([step_bias, decay_log, skip_gain])[None]
    packed = jnp.concatenate(
        [
            conv_inner_weight,
            conv_inner_bias[None],
            gate_gain[None],
            jnp.pad(thin_rows, ((0, 0), (0, part - 3 * heads_here))),
        ],
        axis=0,
    )
    thin = jnp.concatenate([step_weight.T, adapter_step[pick].T], axis=1)
    tables = jnp.concatenate(
        [adapter_inner[pick].reshape(2 * rank, part), adapter_mixed[pick].T], axis=0
    )
    first_block, gate_block, out_block = inner_weight[:, 1], inner_weight[:, 0], out_weight.T

    if chip_plan:
        groups = ndp
        scalars = jnp.stack([lax.axis_index("dp") % 2, z, z, pick]).astype(jnp.int32)
        chips = ndp // 2
        small_rows = rows_here // 2
        rest_rows = (nz - 1) * rows_here
        same_core = [[2 * g + core for g in range(chips)] for core in (0, 1)]

        def plan_of(which):
            def entries(first, low):
                return tuple(
                    (first + b, g, low, rows_here, (2 * g + b) * rows_here)
                    for g in range(chips)
                    for b in (0, 1)
                )

            return (entries(0, which * rows_here),) + tuple(
                entries(2, k * rows_here) for k in range(nz - 1)
            )

        plan_in, plan_gate, plan_out = plan_of(0), plan_of(1), plan_of(2)

        def spread(v):
            return lax.all_gather(v, "dp", axis_index_groups=same_core)

        def both(v):
            return [v, xor(v, 1, ndp)]

        wide_thin = jnp.pad(thin, ((0, 0), (0, part - thin.shape[1])))
        tail = jnp.concatenate(jnp.split(tail, 2, axis=1), axis=0)
        lead = jnp.concatenate([first_block, tail, split_rows(packed), wide_thin], axis=0)
        lead = jnp.pad(lead, ((0, -lead.shape[0] % 16), (0, 0)))
        own_block = jnp.concatenate([first_block, gate_block, out_block], axis=0)
        owns = spread(own_block)
        z1 = all_slots(lead, nz)
        others = jnp.concatenate([gate_block, out_block, tables], axis=0)
        z2 = all_slots(after(others, z1), nz)
        low_at = rows_here + 2 * HALO
        halo = z1[1]
        halo_spec = pl.BlockSpec((2 * HALO, part), lambda j, sc: (rows_here // (2 * HALO), 0))
        at = low_at + 3 * packed.shape[0]
        packed = [joined_rows(v[low_at:at]) for v in z1]
        thin = jnp.concatenate([v[at : at + heads_here, : thin.shape[1]] for v in z1], axis=0).T
        small = jnp.concatenate([map_weight, thin[:rows_here]], axis=1)
        small = jnp.pad(small, ((0, 0), (0, part // 2 - small.shape[1])))
        small = jnp.concatenate([small[:small_rows], small[small_rows:]], axis=1)
        s1 = jnp.concatenate([v[:rows_here] for v in z1[1:]] + [small], axis=0)
        rest1 = spread(after(s1, owns))
        s2 = jnp.concatenate([v[:rows_here] for v in z2[1:]], axis=0)
        rest2 = spread(after(s2, rest1))
        s3 = jnp.concatenate([v[rows_here : 2 * rows_here] for v in z2[1:]], axis=0)
        rest3 = spread(after(s3, rest1))
        tables = [v[2 * rows_here :] for v in z2]
        small_spec = pl.BlockSpec(
            (chips, small_rows, part), lambda j, sc: (0, rest_rows // small_rows, 0)
        )
    else:
        groups = 1
        scalars = jnp.stack([jnp.zeros_like(z), z, z, pick]).astype(jnp.int32)
        plan_in = tuple(((0, 0, k * width, width, 0),) for k in range(nz))
        plan_gate = plan_out = plan_in
        tail = jnp.concatenate(jnp.split(tail, 2, axis=1), axis=0)
        halo = lax.ppermute(tail, "tensor", up_one)
        halo_spec = pl.BlockSpec((2 * HALO, part), lambda j, sc: (0, 0))

        def plain(block):
            block = lax.all_gather(block, "dp", axis=0, tiled=True)
            return [jnp.concatenate(all_slots(block, nz), axis=0)[None]]

        w_inner, w_gate, w_out = plain(first_block), plain(gate_block), plain(out_block)
        packed, tables = all_slots(packed, nz), all_slots(tables, nz)
        thin = jnp.concatenate(all_slots(thin, nz), axis=0).T
        small = jnp.concatenate([map_weight, thin[:rows_here]], axis=1)
        small = jnp.pad(small, ((0, 0), (0, part // 2 - small.shape[1])))
        small = lax.all_gather(small, "dp", axis=0, tiled=True)
        small = [jnp.concatenate(jnp.split(small, 2, axis=0), axis=1)[None]]
        small_spec = pl.BlockSpec((1, width // 2, part), lambda j, sc: (0, 0, 0))
    group_rows = width // groups

    astep = thin[rows_here : rows_here + rank]
    wide_rows = jnp.concatenate([v[:6] for v in packed], axis=1)
    conv_w, conv_b, gain = wide_rows[:4], wide_rows[4:5], wide_rows[5:6]
    thin_rows = jnp.stack([v[6, : 3 * heads_here].reshape(3, heads_here) for v in packed], axis=1)
    thin_rows = thin_rows.reshape(3, heads)
    sbias, dlog = thin_rows[0:1], thin_rows[1:2]
    skip = jnp.repeat(thin_rows[2], inner // heads)[None]
    tables = jnp.concatenate(tables, axis=1)
    two = tables[: 2 * rank].reshape(rank, 2, inner)
    agate, ainner, amixed = two[:, 0], two[:, 1], tables[2 * rank :]
    down, amap, up = adapter_down[pick], adapter_map[pick], adapter_up[pick]

    segment = segment_ids[0]
    padded = jnp.pad(segment, (HALO, HALO), constant_values=-1)
    near = lax.dynamic_slice(padded, (z * tokens,), (tokens + 2 * HALO,))
    own = near[HALO : HALO + tokens]
    by_chunk = own.reshape(chunks, CHUNK)
    before = jnp.concatenate([near[HALO - 1 : HALO], by_chunk[:-1, -1]])
    columns = [near[HALO - k : HALO - k + tokens] == own for k in (1, 2, 3)]
    columns += [
        (by_chunk == before[:, None]).reshape(tokens),
        (by_chunk == by_chunk[:, -1:]).reshape(tokens),
        own == near[HALO - 1],
        own == own[tokens - 1],
        own,
    ]
    columns += [near[HALO + k : HALO + k + tokens] == own for k in (1, 2, 3)]
    cols = jnp.stack([c.astype(F32) for c in columns], axis=1)
    rows = jnp.broadcast_to(own.astype(F32)[None], (8, tokens))

    if chip_plan:
        ready = (cols, rows, conv_w, conv_b, gain, skip, sbias, dlog, astep, ainner, amap, down)
        owns, rest1 = after((owns, rest1), ready)
        owns, rest1 = both(owns), both(rest1)
        w_inner = owns + rest1
        small = rest1
    n_w = len(w_inner)

    def by_slot(height, first=0):
        return pl.BlockSpec((height, part), lambda j, sc: (0, j + first))

    def turned(height, by):
        return pl.BlockSpec((height, part), lambda j, sc: (0, lax.rem(j + by + 2 * nz, nz)))

    def quantity(*which):
        if len(which) == 1:
            return pl.BlockSpec((1, tokens, nq), lambda j, sc: (which[0], 0, 0))
        return pl.BlockSpec((len(which), tokens, nq), lambda j, sc: (0, 0, 0))

    anywhere = pl.BlockSpec(memory_space=pl.ANY)

    def wide_out(kind=BF16, height=tokens):
        return shape((height, inner), kind)

    def weight_scratch():
        return [
            pltpu.VMEM((2, width, part), BF16),
            pltpu.SemaphoreType.DMA((2, max(len(entries) for entries in plan_in + plan_out))),
        ]

    parts_scratch = pltpu.VMEM((groups, tokens, group_rows), F32)

    columns = part // 2
    nrm, scale, low, low_f, maps, pre_map, quant, sig, small_full = call(
        functools.partial(front_kernel, len(small)),
        1,
        [
            whole(x.shape), halo_spec, whole((1, width)), whole((width, rank)), whole((rank, n2)),
            whole((rank, heads)), whole((4, n2)), whole((1, n2)), whole((1, heads)),
            whole((1, heads)), whole(cols.shape),
        ]
        + [small_spec] * len(small),
        [
            whole((ext, width)), whole((tokens, 128)), whole((ext, rank)), whole((tokens, rank)),
            whole((tokens, n2)), whole((tokens, n2)), whole((6, tokens, nq)), whole((tokens, heads)),
            whole((width, columns)),
        ],
        [
            shape((ext, width), BF16), shape((tokens, 128), F32), shape((ext, rank), BF16),
            shape((tokens, rank), F32), shape((tokens, n2), BF16), shape((tokens, n2), F32),
            shape((6, tokens, nq), BF16), shape((tokens, heads), F32), shape((width, columns), BF16),
        ],
        [pltpu.VMEM((ext, n2), F32), pltpu.VMEM((groups, ext, group_rows), BF16)],
        8,
    )(
        scalars, x, halo, norm_gain[None], down, amap, astep, conv_map_weight, conv_map_bias[None],
        sbias, dlog, cols, *small,
    )

    results = []
    half = nz
    for first in range(0, nz, half):
        base_args = [scalars, nrm, low, ainner, conv_w, conv_b, maps, quant, cols, rows, *w_inner]
        results = call(
            functools.partial(values_kernel, heads, plan_in, first, half),
            half,
            [
                whole(nrm.shape), whole(low.shape), by_slot(rank, first), by_slot(4, first),
                by_slot(1, first), whole(maps.shape), quantity(0, 1, 2, 3), whole(cols.shape),
                whole(rows.shape),
            ]
            + [anywhere] * (n_w + len(results)),
            [by_slot(tokens, first)] * 3 + [by_slot(n, first)],
            [wide_out(), wide_out(), wide_out(), wide_out(BF16, n)],
            [
                pltpu.VMEM((chunks, CHUNK, CHUNK), F32), pltpu.VMEM((chunks, n, CHUNK), BF16),
                pltpu.VMEM((ext, part), F32), pltpu.VMEM((3, tokens, 128), F32),
            ]
            + weight_scratch(),
            15,
            {len(base_args) + i: i for i in range(len(results))},
        )(*base_args, *results)
    values, pre, y_local, s_local = results

    ent_last = quant[4, tokens - 1].reshape(3, heads).astype(F32).sum(0)
    through = jnp.repeat(ent_last, inner // heads)[None]
    hops = min(nz - 1, 1 + (DOC_MOST - 2) // tokens)

    def carry(local, pairs, turn):
        got = [lax.ppermute(local, "tensor", pairs)]
        for hop in range(1, hops):
            passed = got[-1].astype(F32) * jnp.roll(through, -turn * hop * part, axis=1)
            got.append(lax.ppermute(passed.astype(BF16), "tensor", pairs))
        return got

    s_in = carry(s_local, up_one, 1)
    from_left = [turned(n, -1 - hop) for hop in range(hops)]
    from_right = [turned(n, 1 + hop) for hop in range(hops)]

    if chip_plan:
        w_gate = owns + both(after(rest2, values))
    gate = call(
        functools.partial(gate_kernel, plan_gate, nz),
        nz,
        [whole(nrm.shape), whole(low.shape), by_slot(rank)] + [anywhere] * n_w,
        by_slot(tokens),
        wide_out(),
        weight_scratch(),
        10,
    )(scalars, after(nrm, s_local), low, agate, *w_gate)
    if chip_plan:
        w_out = owns + both(after(rest3, s_in[-1], gate))

    def slot_in(height, phase, by=0):
        def index(j, sc):
            at = (jnp.minimum(j, nz - 1), jnp.maximum(j - nz, 0), lax.rem(j, nz))[phase]
            return (0, lax.rem(at + by + 2 * nz, nz))

        return pl.BlockSpec((height, part), index)

    gg, r_gate, gy, gz, g_local, mixed_low, tab_up, tab_mixed = call(
        functools.partial(gated_kernel, heads, plan_out, nz, hops),
        2 * nz,
        [
            whole(cot.shape), whole(up.shape), slot_in(rank, 0), slot_in(tokens, 2),
            slot_in(tokens, 0), slot_in(tokens, 0), slot_in(1, 0), slot_in(1, 2), quantity(4),
            whole(maps.shape),
        ]
        + [slot_in(n, 0, -1 - hop) for hop in range(hops)]
        + [anywhere] * n_w,
        [
            slot_in(tokens, 0), whole((tokens, 128)), slot_in(tokens, 1), slot_in(tokens, 1),
            slot_in(n, 1), whole((tokens, rank)), whole(up.shape), slot_in(rank, 1),
        ],
        [
            wide_out(), shape((tokens, 128), F32), wide_out(), wide_out(), wide_out(BF16, n),
            shape((tokens, rank), BF16), shape(up.shape, F32), wide_out(F32, rank),
        ],
        [
            pltpu.VMEM((nz, tokens, part), F32), pltpu.VMEM((nz, tokens, part), F32),
            pltpu.VMEM((nz, tokens, part), BF16), pltpu.VMEM((tokens, 128), F32),
            pltpu.VMEM((tokens, 128), F32), pltpu.VMEM((groups, tokens, group_rows), BF16),
            pltpu.VMEM((tokens, width), BF16), pltpu.VMEM((n, tokens), BF16),
            pltpu.VMEM((tokens, rank), F32), pltpu.VMEM((tokens, rank), F32),
            pltpu.VMEM((rank, tokens), BF16),
        ]
        + weight_scratch(),
        26,
    )(
        scalars, cot, up, amixed, gate, y_local, values, skip, gain, quant, maps, *s_in, *w_out,
    )

    g_in = carry(g_local, down_one, -1)
    start, glow_gate, tab_gate = call(
        functools.partial(gate_rows_kernel, plan_gate, nz),
        nz,
        [by_slot(tokens), by_slot(rank), whole(low.shape)] + [anywhere] * n_w,
        [whole((tokens, width)), whole((tokens, rank)), by_slot(rank)],
        [shape((tokens, width), F32), shape((tokens, rank), F32), wide_out(F32, rank)],
        [pltpu.VMEM((rank, tokens), BF16)] + weight_scratch(),
        11,
    )(scalars, gz, agate, low, *w_gate)
    gy = after(gy, g_in[0], start)

    dx, gmaps, r_local = call(
        functools.partial(backward_kernel, heads, nz, hops),
        nz,
        [
            by_slot(tokens), by_slot(tokens), whole(maps.shape), quantity(0, 1, 2, 3),
            whole(cols.shape), whole(rows.shape),
        ]
        + from_left,
        [by_slot(tokens), whole((tokens, n2)), whole((heads, tokens))],
        [wide_out(), shape((tokens, n2), F32), shape((heads, tokens), F32)],
        [
            pltpu.VMEM((chunks, CHUNK, CHUNK), F32), pltpu.VMEM((chunks, CHUNK, CHUNK), F32),
            pltpu.VMEM((chunks, CHUNK, CHUNK), F32), pltpu.VMEM((tokens, n), F32),
            pltpu.VMEM((tokens, n), F32), pltpu.VMEM((heads // 2, 8, tokens), F32),
            pltpu.VMEM((heads // 2, 8, 2 * tokens), F32), pltpu.VMEM((inner // SUB, 8, tokens), F32),
            pltpu.VMEM((inner // SUB, 8, tokens), F32), pltpu.VMEM((inner // SUB, 8, tokens), F32),
            pltpu.VMEM((chunks, n, CHUNK), BF16), pltpu.VMEM((chunks, n, CHUNK), BF16),
        ],
        32,
    )(scalars, values, gy, maps, quant, cols, rows, *s_in)

    c_all, cmap, gstep = call(
        functools.partial(finish_kernel, heads, nz, hops),
        nz,
        [
            by_slot(tokens), by_slot(tokens), by_slot(tokens), by_slot(tokens), whole(maps.shape),
            quantity(1), quantity(4), quantity(5), by_slot(1), whole(gmaps.shape),
            whole(r_local.shape), whole(sig.shape), whole(dlog.shape), whole(pre_map.shape),
        ]
        + from_left
        + from_right,
        [by_slot(tokens), whole((tokens, n2)), whole((tokens, heads))],
        [wide_out(), shape((tokens, n2), F32), shape((tokens, heads), BF16)],
        [
            pltpu.VMEM((inner // SUB, 8, tokens), F32), pltpu.VMEM((inner // SUB, 8, tokens), F32),
            pltpu.VMEM((tokens, n), F32), pltpu.VMEM((inner // SUB, 8, CHUNK), F32),
        ],
        12,
    )(
        scalars, values, dx, gy, pre, maps, quant, quant, quant, skip, gmaps, r_local, sig, dlog, pre_map,
        *s_in, *g_in,
    )

    c_halo = lax.ppermute(
        jnp.concatenate([c_all[:HALO], cmap[:HALO].astype(BF16)], axis=1), "tensor", down_one
    )
    total_width = 3 * part + 2 * width + n2 + 128
    gi, gmap, glow, *packs = call(
        functools.partial(tables_kernel, nz, heads_here),
        nz,
        [
            by_slot(tokens), turned(HALO, 1), whole(cmap.shape), whole((HALO, n2)),
            whole((tokens, rank)), by_slot(rank), by_slot(rank), whole(up.shape), by_slot(4),
            whole((4, n2)), by_slot(rank), whole(amap.shape),
            whole(astep.shape), whole(gstep.shape), whole(low.shape), whole(low_f.shape),
            whole(nrm.shape), whole(cols.shape),
        ],
        [
            by_slot(tokens), whole((tokens, n2)), whole((tokens, rank)),
            *[whole((rank, total_width))] * nz,
        ],
        [
            wide_out(), shape((tokens, n2), BF16), shape((tokens, rank), BF16),
            *[shape((rank, total_width), BF16)] * nz,
        ],
        [
            pltpu.VMEM((ext, SUB), F32), pltpu.VMEM((tokens, rank), F32),
            pltpu.VMEM((rank, tokens), BF16), pltpu.VMEM((groups, rank, group_rows), F32),
        ],
        10,
    )(
        scalars, c_all, c_halo[:, :inner], cmap, c_halo[:, inner:], glow_gate, tab_gate, tab_mixed, tab_up,
        conv_w, conv_map_weight, ainner, amap, astep, gstep, low, low_f, nrm, cols,
    )

    input_grad = call(
        functools.partial(input_kernel, plan_in, nz),
        nz,
        [
            whole((tokens, width)), by_slot(tokens), whole(gmap.shape), whole(gstep.shape),
            whole(glow.shape), whole(small_full.shape), whole(down.shape),
            whole(x.shape), whole(cot.shape), whole(scale.shape), whole((1, width)),
        ]
        + [anywhere] * n_w,
        whole(x.shape),
        shape(x.shape, F32),
        [pltpu.VMEM((tokens, width), F32), parts_scratch] + weight_scratch(),
        14,
    )(
        scalars, start, gi, gmap, gstep, glow, small_full, down, x, cot, scale,
        norm_gain[None], *w_inner,
    )

    total = packs[0].astype(F32)
    for k in range(1, nz):
        total = total + around(packs[k], -k, nz).astype(F32)
    total = total.astype(BF16)
    layer_out = call(
        functools.partial(out_kernel, plan_out, nz),
        nz,
        [
            whole(x.shape), by_slot(tokens), whole(up.shape), whole(r_gate.shape),
            whole((tokens, rank)),
        ]
        + [anywhere] * n_w,
        whole(x.shape),
        shape(x.shape, BF16),
        [pltpu.VMEM((tokens, width), F32), parts_scratch] + weight_scratch(),
        12,
    )(scalars, x, after(gg, total), up, r_gate, mixed_low, *w_out)

    if chip_plan:
        every = jnp.stack([total] + [xor(total, m, ndp) for m in (2, 4, 6)])
        every = jnp.concatenate([every, xor(every, 1, ndp)], axis=0)
    else:
        every = lax.all_gather(total, "dp")
    every = every.astype(F32)
    hot = (every[:, 0, total_width - 128 + heads_here][:, None] == jnp.arange(adapters)[None, :].astype(F32)).astype(F32)
    summed = jnp.einsum("sa,src->arc", hot, every, precision=EXACT)
    grad_inner = summed[:, :, : 2 * part].reshape(adapters, rank, 2, part)
    grad_mixed = jnp.swapaxes(summed[:, :, 2 * part : 3 * part], 1, 2)
    at = 3 * part
    grad_down = jnp.swapaxes(summed[:, :, at : at + width], 1, 2)
    grad_up = summed[:, :, at + width : at + 2 * width]
    at = at + 2 * width
    grad_map = summed[:, :, at : at + n2]
    grad_step = summed[:, :, at + n2 : at + n2 + heads_here]
    return (
        layer_out[None], input_grad[None], grad_down, grad_inner, grad_map, grad_step, grad_mixed, grad_up
    )


def solution(mesh):
    return jax.shard_map(
        shards,
        mesh=mesh,
        in_specs=(
            P("dp", "tensor", None),
            P("dp", "tensor", None),
            P("dp", None),
            P("dp"),
            P(),
            P("dp", None, "tensor"),
            P("dp", None),
            P("dp", "tensor"),
            P(None, "tensor"),
            P("tensor"),
            P(),
            P(),
            P("tensor"),
            P("tensor"),
            P("tensor"),
            P("tensor"),
            P("tensor", "dp"),
            P(),
            P(None, None, None, "tensor"),
            P(),
            P(None, None, "tensor"),
            P(None, "tensor", None),
            P(),
        ),
        out_specs=(
            P("dp", "tensor", None),
            P("dp", "tensor", None),
            P(),
            P(None, None, None, "tensor"),
            P(),
            P(None, None, "tensor"),
            P(None, "tensor", None),
            P(),
        ),
        check_vma=False,
    )
```

```python
import functools

import jax
import jax.numpy as jnp
from jax import lax
from jax.experimental import pallas as pl
from jax.experimental.pallas import tpu as pltpu
from jax.sharding import PartitionSpec as P

EPSILON = 1e-05
HALO = 16
CHUNK = 128
SUB = 256
DOC_MOST = 800
LOG2E = 1.4426950408889634
F32 = jnp.float32
BF16 = jnp.bfloat16
EXACT = lax.Precision.HIGHEST


def dot(a, b, precision=None):
    return lax.dot_general(
        a, b, (((1,), (0,)), ((), ())), precision=precision, preferred_element_type=F32
    )


def dot_nt(a, b, precision=None):
    return lax.dot_general(
        a, b, (((1,), (1,)), ((), ())), precision=precision, preferred_element_type=F32
    )


def sigmoid(v):
    return 0.5 * jnp.tanh(0.5 * v) + 0.5


def split3(v):
    hi = v.astype(BF16)
    rest = v - hi.astype(F32)
    mid = rest.astype(BF16)
    lo = (rest - mid.astype(F32)).astype(BF16)
    return jnp.concatenate([hi, mid, lo], axis=1)


def spread_matrix(heads, cols, base, width):
    k = lax.broadcasted_iota(jnp.int32, (3 * heads, cols), 0)
    k = jnp.where(k >= 2 * heads, k - 2 * heads, jnp.where(k >= heads, k - heads, k))
    l = lax.broadcasted_iota(jnp.int32, (3 * heads, cols), 1)
    return jnp.where(k == base + l // width, 1.0, 0.0).astype(BF16)


def row_matrix(heads, rows, base):
    k = lax.broadcasted_iota(jnp.int32, (rows, 3 * heads), 1)
    k = jnp.where(k >= 2 * heads, k - 2 * heads, jnp.where(k >= heads, k - heads, k))
    i = lax.broadcasted_iota(jnp.int32, (rows, 3 * heads), 0)
    return jnp.where(k == base + i, 1.0, 0.0).astype(BF16)


def row_picks(groups, width, kind=BF16):
    row = lax.broadcasted_iota(jnp.int32, (8, groups * width), 0)
    lane = lax.broadcasted_iota(jnp.int32, (8, groups * width), 1)
    return jnp.where(row == lane // width, 1.0, 0.0).astype(kind)


def head_rows(ref, heads, each, lanes=None, only=None):
    blocks, _, columns = ref.shape
    flat = ref[...].reshape(blocks * 8, columns)
    if lanes is not None:
        flat = jnp.concatenate([flat[:, at : at + CHUNK] for at in lanes], axis=1)
    head = lax.broadcasted_iota(jnp.int32, (heads, blocks * 8), 0)
    row = lax.broadcasted_iota(jnp.int32, (heads, blocks * 8), 1)
    inside = lax.rem(head, each)
    if only is None:
        pick = row == head // each * 8 + inside
    else:
        pick = (row == head // each * 8) & (inside == only)
    return dot(jnp.where(pick, 1.0, 0.0), flat, precision=EXACT)


def two_heads(v, lane_low):
    return jnp.concatenate(
        [jnp.where(lane_low, v, 0.0), jnp.where(lane_low, 0.0, v)], axis=0
    ).astype(BF16)


def triangle(strict_upper=False):
    r = lax.broadcasted_iota(jnp.int32, (CHUNK, CHUNK), 0)
    c = lax.broadcasted_iota(jnp.int32, (CHUNK, CHUNK), 1)
    keep = (r < c) if strict_upper else (r >= c)
    return jnp.where(keep, 1.0, 0.0)


def conv_forward(buffer, tokens, weight, bias, cols):
    result = bias + weight[0:1] * buffer[HALO : HALO + tokens, :]
    for lag in range(1, 4):
        moved = buffer[HALO - lag : HALO - lag + tokens, :]
        result = result + weight[lag : lag + 1] * (moved * cols[:, lag - 1 : lag])
    return result


def fetch(plan, scalars, refs, buffer, sems, slot, k, wait=False):
    for at, entries in enumerate(plan):

        @pl.when(k == at)
        def _(entries=entries):
            for index, (which, lead, source, rows, place) in enumerate(entries):
                place = pl.multiple_of((place ^ scalars[0]) * rows, rows)
                copy = pltpu.make_async_copy(
                    refs[which].at[lead, pl.ds(source, rows)],
                    buffer.at[slot, pl.ds(place, rows)],
                    sems.at[slot, index],
                )
                copy.wait() if wait else copy.start()


def pieces_of(plan):
    return 1 + max(entry[0] for entries in plan for entry in entries)


def stream(plan, scalars, refs, buffer, sems, j, first, last, k):
    slot = lax.rem(j, 2)

    @pl.when(j == first)
    def _():
        fetch(plan, scalars, refs, buffer, sems, slot, k)

    @pl.when(j + 1 < last)
    def _():
        fetch(plan, scalars, refs, buffer, sems, 1 - slot, k + 1)

    fetch(plan, scalars, refs, buffer, sems, slot, k, wait=True)
    return slot


def lanes_of(i):
    return pl.ds(pl.multiple_of(i * SUB, SUB), SUB)


def chunk_rows(c):
    return slice(c * CHUNK, (c + 1) * CHUNK)


def allowed_mask(cols, rows, c, transposed=False):
    r = lax.broadcasted_iota(jnp.int32, (CHUNK, CHUNK), 0)
    l = lax.broadcasted_iota(jnp.int32, (CHUNK, CHUNK), 1)
    same = cols[chunk_rows(c), 7:8] == rows[0:1, chunk_rows(c)]
    return same & ((r <= l) if transposed else (r >= l))


def added(refs, lanes):
    total = refs[0][:, lanes].astype(F32)
    for ref in refs[1:]:
        total = total + ref[:, lanes].astype(F32)
    return total


def transpose(v):
    return v.astype(F32).T.astype(BF16)


def front_kernel(
    n_small, scalars, x, halo, gain, down, amap, astep, cmw, cmb, sbias, dlog, cols, *rest
):
    small_refs, rest = rest[:n_small], rest[n_small:]
    nrm, scale, low, low_out, maps, pre_map, quant, sig_out, small, buffer = rest
    tokens, n2 = maps.shape
    heads = sig_out.shape[1]
    lead, half, _ = small_refs[0].shape
    columns = small.shape[1]
    for g in range(lead):
        for b in range(n_small):
            at = pl.multiple_of(((g * n_small + b) ^ scalars[0]) * 2 * half, 2 * half)
            small[pl.ds(at, half)] = small_refs[b][g, :, :columns]
            small[pl.ds(at + half, half)] = small_refs[b][g, :, columns:]
    before = jnp.concatenate([halo[:HALO], halo[HALO:]], axis=1).astype(F32)
    before = jnp.where(scalars[1] > 0, before, 0.0)
    xf = jnp.concatenate([before, x[...].astype(F32)], axis=0)
    q = lax.rsqrt(jnp.mean(xf * xf, axis=-1, keepdims=True) + EPSILON)
    normed = (xf * q * gain[...]).astype(BF16)
    scale[...] = jnp.broadcast_to(q[HALO:], scale.shape)
    adapter_low = dot(normed, down[...])
    low_out[...] = adapter_low[HALO:]
    adapter_low = adapter_low.astype(BF16)
    low[...] = adapter_low
    nrm[...] = normed
    buffer[...] = dot(normed, small[:, :n2]) + dot(adapter_low, amap[...])
    pre = conv_forward(buffer, tokens, cmw[...], cmb[...], cols[...])
    pre_map[...] = pre
    maps[...] = (pre * sigmoid(pre)).astype(BF16)
    raw = dot(normed[HALO:], small[:, n2 : n2 + heads]) + sbias[...]
    raw = raw + dot(adapter_low[HALO:], astep[...])
    step = jnp.maximum(raw, 0.0) + jnp.log(1.0 + jnp.exp(-jnp.abs(raw)))
    sig_out[...] = sigmoid(raw)
    rate = -jnp.exp(dlog[...])
    drop = step * rate * LOG2E
    lower = triangle()
    sums = []
    for c in range(tokens // CHUNK):
        sums.append(dot(lower, drop[c * CHUNK : (c + 1) * CHUNK], precision=EXACT))
    base = jnp.zeros_like(sums[0][0:1])
    bases = []
    for c in range(tokens // CHUNK):
        bases.append(base)
        base = base + sums[c][CHUNK - 1 : CHUNK]
    column = cols[...]
    cum = jnp.concatenate(sums, axis=0)
    whole = jnp.concatenate([s + b for s, b in zip(sums, bases)], axis=0)
    left = jnp.concatenate([s[CHUNK - 1 : CHUNK] - s for s in sums], axis=0)
    quant[0] = split3(cum)
    quant[1] = split3(step)
    quant[2] = split3(jnp.exp2(cum) * column[:, 3:4])
    quant[3] = split3(jnp.exp2(left) * column[:, 4:5])
    quant[4] = split3(jnp.exp2(whole) * column[:, 5:6])
    quant[5] = split3(jnp.exp2(base - whole) * column[:, 6:7])


def values_kernel(
    heads, plan, first, count, scalars, nrm, low, aw, cw, cb, maps, quant, cols, rows, *rest
):
    n_w = pieces_of(plan)
    w_refs, rest = rest[:n_w], rest[-10:]
    values, slope_out, y_out, s_out, masked, in_t, buffer, wide_buffer, wbuf, sems = rest
    j = pl.program_id(0)
    slot = stream(plan, scalars, w_refs, wbuf, sems, j, 0, count, j + first)
    tokens = maps.shape[0]
    chunks = tokens // CHUNK
    n = maps.shape[1] // 2

    @pl.when(j == 0)
    def _():
        for c in range(chunks):
            b = maps[chunk_rows(c), :n]
            scores = dot_nt(maps[chunk_rows(c), n:], b)
            masked[c] = jnp.where(allowed_mask(cols, rows, c), scores, 0.0)
            in_t[c] = transpose(b)
        for lag in range(3):
            wide_buffer[lag] = jnp.broadcast_to(cols[:, lag : lag + 1], wide_buffer.shape[1:])

    buffer[...] = dot(nrm[...], wbuf[slot]) + dot(low[...], aw[...])
    subs = buffer.shape[1] // SUB
    lane_low = lax.broadcasted_iota(jnp.int32, (CHUNK, 128), 1) < 64

    def body(i, carry):
        lanes = lanes_of(i)
        base = ((j + first) * subs + i) * (SUB // 64)
        weight = cw[:, lanes]
        pre = cb[:, lanes] + weight[0:1] * buffer[HALO : HALO + tokens, lanes]
        for lag in range(1, 4):
            keep = jnp.concatenate([wide_buffer[lag - 1]] * 2, axis=1)
            moved = buffer[HALO - lag : HALO - lag + tokens, lanes]
            pre = pre + weight[lag : lag + 1] * (moved * keep)
        s = sigmoid(pre)
        slope_out[:, lanes] = (s * (1.0 + pre * (1.0 - s))).astype(BF16)
        v = (pre * s).astype(BF16)
        values[:, lanes] = v
        wide = spread_matrix(heads, SUB, base, 64)
        v = v.astype(F32)
        vp = dot(quant[1], wide) * v
        row = dot_nt(row_matrix(heads, 8, base), quant[0])
        pair_wide = [spread_matrix(heads, 2 * CHUNK, base + 2 * p, CHUNK) for p in range(2)]
        state = None
        for c in range(chunks):
            rs = chunk_rows(c)
            cum_c = quant[0, rs]
            mask2 = jnp.concatenate([masked[c], masked[c]], axis=1)
            inside = []
            for p in range(2):
                r2 = jnp.concatenate(
                    [row[2 * p : 2 * p + 1, rs], row[2 * p + 1 : 2 * p + 2, rs]], axis=1
                )
                decay = jnp.exp2(jnp.minimum(dot(cum_c, pair_wide[p]) - r2, 0.0))
                vbd = two_heads(vp[rs, p * 128 : (p + 1) * 128], lane_low)
                inside.append(dot((decay * mask2).astype(BF16), vbd))
            y = jnp.concatenate(inside, axis=1)
            enter = dot(quant[2, rs], wide)
            if c > 0:
                y = y + enter * dot(maps[rs, n:], state.astype(BF16))
            y_out[rs, lanes] = y.astype(y_out.dtype)
            end = dot(quant[3, rs], wide)
            fresh = dot(in_t[c], (end * vp[rs]).astype(BF16))
            state = fresh if c == 0 else state * enter[CHUNK - 1 : CHUNK] + fresh
        s_out[:, lanes] = state.astype(s_out.dtype)
        return carry

    lax.fori_loop(0, subs, body, 0)


def gate_kernel(plan, count, scalars, nrm, low, aw, *rest):
    n_w = pieces_of(plan)
    w_refs, (act_out, slope_out, wbuf, sems) = rest[:n_w], rest[n_w:]
    j = pl.program_id(0)
    slot = stream(plan, scalars, w_refs, wbuf, sems, j, 0, count, j)

    def body(i, carry):
        lanes = lanes_of(i)
        gate = dot(nrm[HALO:], wbuf[slot, :, lanes]) + dot(low[HALO:], aw[:, lanes])
        s = sigmoid(gate)
        act_out[:, lanes] = (gate * s).astype(BF16)
        slope_out[:, lanes] = (s * (1.0 + gate * (1.0 - s))).astype(BF16)
        return carry

    lax.fori_loop(0, act_out.shape[1] // SUB, body, 0)


def gated_kernel(
    heads, plan, count, n_s, scalars, cot, up, amixed, act_in, act_slope, y_in, values, skip, gain, quant, maps, *rest
):
    n_w = pieces_of(plan)
    states, w_refs, rest = rest[:n_s], rest[n_s : n_s + n_w], rest[n_s + n_w :]
    gg_out, r_out, gy_out, gz_out, g_out, mlow_out, tab_up, tab_mixed, *rest = rest
    grad, ys, ggs, squares, inner, out_t, gml, low, scaled, wbuf, sems = rest
    j = pl.program_id(0)
    n = maps.shape[1] // 2
    part = act_in.shape[1]
    subs = part // SUB

    @pl.when(j == 0)
    def _():
        gml[...] = dot_nt(cot[...], up[...])
        low[...] = jnp.zeros_like(low)
        inner[...] = jnp.zeros_like(inner)
        squares[...] = jnp.zeros_like(squares)
        out_t[...] = transpose(maps[:, n:])

    @pl.when(j < count)
    def _():
        slot = stream(plan, scalars, w_refs, wbuf, sems, j, 0, count, j)
        thin = gml[...].astype(BF16)

        def body(i, carry):
            lanes = lanes_of(i)
            gradient = dot(cot[...], wbuf[slot, :, lanes]) + dot(thin, amixed[:, lanes])
            grad[j, :, lanes] = gradient
            wide = spread_matrix(heads, SUB, (j * subs + i) * (SUB // 64), 64)
            state = added(states, lanes).astype(BF16)
            entering = dot(quant[0], wide) * dot(maps[:, n:], state)
            y = y_in[:, lanes].astype(F32) + entering
            y = y + skip[:, lanes] * values[:, lanes].astype(F32)
            ys[j, :, lanes] = y
            gated = y * act_in[:, lanes].astype(F32)
            scaled_up = (gated * gain[:, lanes]).astype(BF16)
            ggs[j, :, lanes] = scaled_up
            gg_out[:, lanes] = scaled_up
            square = gated * gated
            squares[...] += square[:, :128] + square[:, 128:]
            term = scaled_up.astype(F32) * gradient
            inner[...] += term[:, :128] + term[:, 128:]
            return carry

        lax.fori_loop(0, subs, body, 0)
        low[...] += dot_nt(ggs[j], amixed[...])

    @pl.when(j >= count)
    def _():
        k = j - count
        size = count * part
        r = lax.rsqrt(jnp.sum(squares[...], axis=-1, keepdims=True) / size + EPSILON)
        cube = r * r * r * (jnp.sum(inner[...], axis=-1, keepdims=True) / size)

        @pl.when(k == 0)
        def _():
            r_out[...] = jnp.broadcast_to(r, r_out.shape)
            scaled[...] = transpose(gml[...] * r)
            mixed_low = low[...] * r
            mlow_out[...] = mixed_low.astype(BF16)
            tab_up[...] = dot(transpose(mixed_low), cot[...])

        tab_mixed[...] = dot(scaled[...], ggs[k])

        def body(i, carry):
            lanes = lanes_of(i)
            y = ys[k, :, lanes]
            act = act_in[:, lanes].astype(F32)
            grad_gated = (grad[k, :, lanes] * gain[:, lanes]) * r - y * act * cube
            gy = grad_gated * act
            gy_out[:, lanes] = gy.astype(BF16)
            gz_out[:, lanes] = (grad_gated * y * act_slope[:, lanes].astype(F32)).astype(BF16)
            enter = dot(quant[0], spread_matrix(heads, SUB, (k * subs + i) * (SUB // 64), 64))
            g_out[:, lanes] = dot(out_t[...], (enter * gy).astype(BF16)).astype(g_out.dtype)
            return carry

        lax.fori_loop(0, subs, body, 0)


def backward_kernel(
    heads, first, count, n_s, scalars, values, gy_in, maps, quant, cols, rows, *rest
):
    s_refs, rest = rest[:n_s], rest[-15:]
    dx_out, gmaps_out, r_out, masked, allowed, mixed, grad_b, grad_c, *rest = rest
    col_p, row_p, carry_a, carry_b, ends, in_b, out_b = rest
    j = pl.program_id(0)
    tokens = maps.shape[0]
    chunks = tokens // CHUNK
    n = maps.shape[1] // 2
    subs = values.shape[1] // SUB
    here = count * subs * (SUB // 64)

    @pl.when(j == 0)
    def _():
        for c in range(chunks):
            rs = chunk_rows(c)
            ok = allowed_mask(cols, rows, c, transposed=True)
            scores = dot_nt(maps[rs, :n], maps[rs, n:])
            masked[c] = jnp.where(ok, scores, 0.0)
            allowed[c] = jnp.where(ok, 1.0, 0.0)
            in_b[c] = transpose(maps[rs, :n])
            out_b[c] = transpose(maps[rs, n:])
        for ref in (mixed, grad_b, grad_c, carry_b, ends):
            ref[...] = jnp.zeros_like(ref)

    lane_low = lax.broadcasted_iota(jnp.int32, (CHUNK, 128), 1) < 64
    ones = jnp.ones((8, CHUNK), BF16)
    by_pair = row_picks(2, CHUNK)
    by_head = row_picks(SUB // 64, 64)
    by_head_f = row_picks(SUB // 64, 64, F32)

    def body(i, carry):
        lanes = lanes_of(i)
        block = j * subs + i
        base = (first * subs + block) * (SUB // 64)
        wide = spread_matrix(heads, SUB, base, 64)
        vp = dot(quant[1], wide) * values[:, lanes].astype(F32)
        row = dot_nt(row_matrix(heads, 8, base), quant[0])
        pair_wide = [spread_matrix(heads, 2 * CHUNK, base + 2 * p, CHUNK) for p in range(2)]
        enters, lefts, states = [], [], []
        state = added(s_refs, lanes)
        for c in range(chunks):
            rs = chunk_rows(c)
            enters.append(dot(quant[2, rs], wide))
            lefts.append(dot(quant[3, rs], wide))
            states.append(state)
            if c < chunks - 1:
                fresh = dot(in_b[c], (lefts[c] * vp[rs]).astype(BF16))
                state = state * enters[c][CHUNK - 1 : CHUNK] + fresh
        adjoint = None
        for c in range(chunks - 1, -1, -1):
            rs = chunk_rows(c)
            cum_c = quant[0, rs]
            gy = gy_in[rs, lanes].astype(F32)
            mask2 = jnp.concatenate([masked[c], masked[c]], axis=1)
            dx = []
            for p in range(2):
                pair = slice(p * 128, (p + 1) * 128)
                r2 = jnp.concatenate(
                    [row[2 * p : 2 * p + 1, rs], row[2 * p + 1 : 2 * p + 2, rs]], axis=1
                )
                decay = jnp.exp2(jnp.minimum(r2 - dot(cum_c, pair_wide[p]), 0.0))
                gbd = two_heads(gy[:, pair], lane_low)
                dx.append(dot((decay * mask2).astype(BF16), gbd))
                part = decay * dot_nt(vp[rs, pair].astype(BF16), gbd)
                mixed[c] += part[:, :CHUNK] + part[:, CHUNK:]
                weighed = (part * mask2).astype(BF16)
                col_p[block * 2 + p, :, rs] = dot_nt(by_pair, weighed)
                row_p[block * 2 + p, :, 2 * c * CHUNK : 2 * (c + 1) * CHUNK] = dot(ones, weighed)
            dx = jnp.concatenate(dx, axis=1)
            entering = enters[c] * gy
            carried = entering * dot(maps[rs, n:], states[c].astype(BF16))
            carry_a[block, :, rs] = dot_nt(by_head, carried.astype(BF16))
            entering = entering.astype(BF16)
            grad_c[rs] += dot_nt(entering, states[c].astype(BF16))
            last = enters[c][CHUNK - 1 : CHUNK]
            if adjoint is not None:
                adj = adjoint.astype(BF16)
                leaving = lefts[c] * dot(maps[rs, :n], adj)
                dx = dx + leaving
                carry_b[block, :, rs] = dot_nt(by_head, (vp[rs] * leaving).astype(BF16))
                grad_b[rs] += dot_nt((lefts[c] * vp[rs]).astype(BF16), adj)
                through = jnp.sum(adjoint * states[c], axis=0, keepdims=True) * last
                through = jnp.sum(by_head_f * through, axis=1, keepdims=True)
                ends[block, :, rs] = jnp.broadcast_to(through, (8, CHUNK))
            dx_out[rs, lanes] = dx.astype(dx_out.dtype)
            if c > 0:
                fresh = dot(out_b[c], entering)
                adjoint = fresh if adjoint is None else adjoint * last + fresh
        return carry

    lax.fori_loop(0, subs, body, 0)

    @pl.when(j == count - 1)
    def _():
        suffix, prefix = triangle(), triangle(strict_upper=True)
        plain = head_rows(carry_a, here, SUB // 64) - head_rows(col_p, here, 2)
        for q in range(2):
            lanes = [(2 * c + q) * CHUNK for c in range(chunks)]
            plain = plain + head_rows(row_p, here, 2, lanes, q)
        left = head_rows(carry_b, here, SUB // 64)
        sums = head_rows(ends, here, SUB // 64)
        for c in range(chunks):
            rs = chunk_rows(c)
            w = mixed[c] * allowed[c]
            gb = grad_b[rs] + dot(w.astype(BF16), maps[rs, n:])
            gc = grad_c[rs] + dot(w.T.astype(BF16), maps[rs, :n])
            gmaps_out[rs] = jnp.concatenate([gb, gc], axis=1)
            r_out[:, rs] = (
                dot(plain[:, rs], suffix, precision=EXACT)
                + dot(left[:, rs], prefix, precision=EXACT)
                + sums[:, rs]
            )


def finish_kernel(
    heads, count, n_s, n_r, scalars, values, dx_in, gy_in, slope, maps, quant_step, quant_enter, quant_left,
    skip, sig, dlog, pre_map, *rest
):
    gmap_refs, r_refs, rest = rest[:n_r], rest[n_r : 2 * n_r], rest[2 * n_r :]
    s_refs, g_refs, rest = rest[:n_s], rest[n_s : 2 * n_s], rest[2 * n_s :]
    c_out, cmap_out, gstep_out, col_g, carry_b, grad_b, ends = rest
    j = pl.program_id(0)
    tokens = maps.shape[0]
    n = maps.shape[1] // 2
    subs = values.shape[1] // SUB

    @pl.when(j == 0)
    def _():
        grad_b[...] = jnp.zeros_like(grad_b)

    by_head = row_picks(SUB // 64, 64)
    by_head_f = row_picks(SUB // 64, 64, F32)

    def body(i, carry):
        lanes = lanes_of(i)
        base = (j * subs + i) * (SUB // 64)
        wide = spread_matrix(heads, SUB, base, 64)
        block = j * subs + i
        v = values[:, lanes].astype(F32)
        step = dot(quant_step[0], wide)
        left = dot(quant_left[0], wide)
        vp = step * v
        adjoint = added(g_refs, lanes)
        both = adjoint * added(s_refs, lanes)
        adjoint = adjoint.astype(BF16)
        more = left * dot(maps[:, :n], adjoint)
        dx = dx_in[:, lanes].astype(F32) + more
        carry_b[block] = dot_nt(by_head, (vp * more).astype(BF16))
        col_g[block] = dot_nt(by_head, (v * dx).astype(BF16))
        grad_b[...] += dot_nt((left * vp).astype(BF16), adjoint)
        last = dot(quant_enter[0, tokens - 16 :], wide)[15:16]
        through = jnp.sum(both, axis=0, keepdims=True) * last
        through = jnp.sum(by_head_f * through, axis=1, keepdims=True)
        ends[block] = jnp.broadcast_to(through, (8, CHUNK))
        dv = step * dx + skip[:, lanes] * gy_in[:, lanes].astype(F32)
        c_out[:, lanes] = (dv * slope[:, lanes].astype(F32)).astype(BF16)
        return carry

    lax.fori_loop(0, subs, body, 0)

    @pl.when(j == count - 1)
    def _():
        prefix = triangle(strict_upper=True)
        run = head_rows(ends, heads, SUB // 64)
        left = head_rows(carry_b, heads, SUB // 64)
        grads = head_rows(col_g, heads, SUB // 64)
        rate = -jnp.exp(dlog[...]).T
        for c in range(tokens // CHUNK):
            rs = chunk_rows(c)
            total = jnp.concatenate([ref[:, rs] for ref in r_refs], axis=0)
            total = total + dot(left[:, rs], prefix, precision=EXACT) + run
            run = run + jnp.sum(left[:, rs], axis=1, keepdims=True)
            raw = grads[:, rs] + rate * total
            gstep_out[rs] = (raw.T * sig[rs]).astype(BF16)
        gmaps = gmap_refs[0][...]
        for ref in gmap_refs[1:]:
            gmaps = gmaps + ref[...]
        gb = gmaps[:, :n] + grad_b[...]
        g = jnp.concatenate([gb, gmaps[:, n:]], axis=1)
        pm = pre_map[...]
        sm = sigmoid(pm)
        cmap_out[...] = (g * (sm * (1.0 + pm * (1.0 - sm)))).astype(cmap_out.dtype)


def conv_backward(buffer, tokens, weight, cols):
    result = weight[0:1] * buffer[0:tokens, :]
    for lag in range(1, 4):
        result = result + weight[lag : lag + 1] * (
            buffer[lag : lag + tokens, :] * cols[:, 7 + lag : 8 + lag]
        )
    return result


def tables_kernel(
    count, heads_here, scalars, c_in, c_halo, cmap, cmap_halo, glow_in, tab_gate, tab_mixed, tab_up, cw, cmw, ainner,
    amap, astep, gstep, low, low_f, nrm, cols, gi_out, gmap_out, glow_out, *rest
):
    packs, (buffer, glow, low_t) = rest[:count], rest[count:]
    j = pl.program_id(0)
    tokens = gi_out.shape[0]
    subs = gi_out.shape[1] // SUB

    @pl.when(j == 0)
    def _():
        low_t[...] = transpose(low[HALO:])
        buffer[:tokens] = cmap[...].astype(F32)
        buffer[tokens:] = cmap_halo[...].astype(F32)
        gmap = conv_backward(buffer, tokens, cmw[...], cols[...])
        exact_low = low_f[...].T
        tab_map = dot(exact_low, gmap, precision=EXACT)
        tab_step = dot(exact_low, gstep[...].astype(F32), precision=EXACT)
        rank = tab_map.shape[0]
        lane = lax.broadcasted_iota(jnp.int32, (rank, 128), 1)
        last = packs[0].shape[1] - 128
        for k, pack in enumerate(packs):
            steps = tab_step[:, k * heads_here : (k + 1) * heads_here]
            steps = jnp.concatenate([steps, jnp.zeros((rank, 128 - heads_here), F32)], axis=1)
            if k == 0:
                steps = jnp.where(lane == heads_here, scalars[3].astype(F32), steps)
            pack[:, last:] = steps.astype(BF16)
            pack[:, last - tab_map.shape[1] : last] = tab_map.astype(BF16)
        gmap = gmap.astype(BF16)
        gmap_out[...] = gmap
        glow[...] = glow_in[...] + dot_nt(gmap, amap[...]) + dot_nt(gstep[...], astep[...])

    def body(i, carry):
        lanes = lanes_of(i)
        buffer[:tokens] = c_in[:, lanes].astype(F32)
        buffer[tokens:] = c_halo[:, lanes].astype(F32)
        gi_out[:, lanes] = conv_backward(buffer, tokens, cw[:, lanes], cols[...]).astype(BF16)
        return carry

    lax.fori_loop(0, subs, body, 0)
    glow[...] += dot_nt(gi_out[...], ainner[...])
    tab_inner = dot(low_t[...], gi_out[...])
    part = gi_out.shape[1]
    for k, pack in enumerate(packs):

        @pl.when(j == k)
        def _(pack=pack):
            pack[:, :part] = tab_gate[...].astype(BF16)
            pack[:, part : 2 * part] = tab_inner.astype(BF16)
            pack[:, 2 * part : 3 * part] = tab_mixed[...].astype(BF16)

    @pl.when(j == count - 1)
    def _():
        glow_out[...] = glow[...].astype(BF16)
        down = dot(transpose(glow[...]), nrm[HALO:])
        down = down.astype(BF16)
        width = down.shape[1]
        for pack in packs:
            pack[:, 3 * part : 3 * part + width] = down
            pack[:, 3 * part + width : 3 * part + 2 * width] = tab_up[...].astype(BF16)


def out_kernel(plan, count, scalars, x, gg, up, r_in, mlow, *rest):
    n_w = pieces_of(plan)
    w_refs = rest[:n_w]
    out, total, wbuf, sems = rest[n_w:]
    j = pl.program_id(0)
    slot = stream(plan, scalars, w_refs, wbuf, sems, j, 0, count, j)
    term = dot_nt(gg[...], wbuf[slot])

    @pl.when(j == 0)
    def _():
        total[...] = term

    @pl.when(j > 0)
    def _():
        total[...] += term

    @pl.when(j == count - 1)
    def _():
        branch = total[...] * r_in[:, 0:1]
        out[...] = (x[...].astype(F32) + branch + dot(mlow[...], up[...])).astype(BF16)


def gate_rows_kernel(plan, count, scalars, gz, agate, low, *rest):
    n_w = pieces_of(plan)
    w_refs = rest[:n_w]
    total, glow, tab_gate, low_t, wbuf, sems = rest[n_w:]
    j = pl.program_id(0)
    slot = stream(plan, scalars, w_refs, wbuf, sems, j, 0, count, j)

    @pl.when(j == 0)
    def _():
        low_t[...] = transpose(low[HALO:])

    term = dot_nt(gz[...], wbuf[slot])
    thin = dot_nt(gz[...], agate[...])
    tab_gate[...] = dot(low_t[...], gz[...])

    @pl.when(j == 0)
    def _():
        total[...] = term
        glow[...] = thin

    @pl.when(j > 0)
    def _():
        total[...] += term
        glow[...] += thin


def input_kernel(
    plan, count, scalars, start, gi, gmap, gstep, glow, small, down, x, cot, scale, gain, *rest
):
    n_w = pieces_of(plan)
    w_refs = rest[:n_w]
    out, total, wbuf, sems = rest[n_w:]
    j = pl.program_id(0)
    slot = stream(plan, scalars, w_refs, wbuf, sems, j, 0, count, j)

    @pl.when(j == 0)
    def _():
        n2, heads = gmap.shape[1], gstep.shape[1]
        total[...] = (
            start[...]
            + dot_nt(gmap[...], small[:, :n2])
            + dot_nt(gstep[...], small[:, n2 : n2 + heads])
        )

    total[...] += dot_nt(gi[...], wbuf[slot])

    @pl.when(j == count - 1)
    def _():
        q = scale[:, 0:1]
        xf = x[...].astype(F32)
        normed_grad = total[...] + dot_nt(glow[...], down[...])
        weighted = normed_grad * gain[...]
        mean = jnp.mean(xf * weighted, axis=-1, keepdims=True)
        out[...] = q * weighted - xf * (q * q * q * mean) + cot[...].astype(F32)


def whole(shape):
    return pl.BlockSpec(shape, lambda *_: (0,) * len(shape))


def call(kernel, steps, in_specs, out_specs, out_shape, scratch, micros, aliases=None):
    return pl.pallas_call(
        kernel,
        grid_spec=pltpu.PrefetchScalarGridSpec(
            num_scalar_prefetch=1,
            grid=(steps,),
            in_specs=in_specs,
            out_specs=out_specs,
            scratch_shapes=scratch,
        ),
        out_shape=out_shape,
        input_output_aliases=aliases or {},
        compiler_params=pltpu.CompilerParams(
            dimension_semantics=("arbitrary",), vmem_limit_bytes=56 * 2**20
        ),
        cost_estimate=pl.CostEstimate(
            flops=int(micros * 1.1e9), bytes_accessed=int(micros * 1e6), transcendentals=0
        ),
    )


def shape(dims, kind):
    return jax.ShapeDtypeStruct(dims, kind)


def xor(v, m, ndp):
    return lax.ppermute(v, "dp", [(i, i ^ m) for i in range(ndp)])


def around(v, k, nz):
    return lax.ppermute(v, "tensor", [(i, (i + k) % nz) for i in range(nz)])


def all_slots(v, nz):
    return [v] + [around(v, k, nz) for k in range(1, nz)]


def after(v, *others):
    return lax.optimization_barrier((v, others))[0]


def split_rows(v):
    high = lax.optimization_barrier(v.astype(BF16))
    rest = v - high.astype(F32)
    middle = lax.optimization_barrier(rest.astype(BF16))
    return jnp.concatenate([high, middle, (rest - middle.astype(F32)).astype(BF16)], axis=0)


def joined_rows(v):
    high, middle, low = jnp.split(v.astype(F32), 3, axis=0)
    return high + middle + low


def shards(
    layer_in,
    cotangent,
    segment_ids,
    adapter_ids,
    norm_gain,
    inner_weight,
    map_weight,
    step_weight,
    conv_inner_weight,
    conv_inner_bias,
    conv_map_weight,
    conv_map_bias,
    step_bias,
    decay_log,
    skip_gain,
    gate_gain,
    out_weight,
    adapter_down,
    adapter_inner,
    adapter_map,
    adapter_step,
    adapter_mixed,
    adapter_up,
):
    ndp, nz = lax.axis_size("dp"), lax.axis_size("tensor")
    z = lax.axis_index("tensor")
    x, cot = layer_in[0], cotangent[0]
    tokens, width = x.shape
    rows_here = inner_weight.shape[0]
    part = gate_gain.shape[0]
    inner = part * nz
    heads_here = step_bias.shape[0]
    heads = heads_here * nz
    adapters, _, rank = adapter_down.shape
    n2 = map_weight.shape[1]
    n = n2 // 2
    chunks = tokens // CHUNK
    ext = tokens + HALO
    nq = 3 * heads
    up_one = [(i, i + 1) for i in range(nz - 1)]
    down_one = [(i + 1, i) for i in range(nz - 1)]
    chip_plan = ndp == 8 and nz == 4 and rows_here % 64 == 0

    pick = adapter_ids[0]
    tail = x[tokens - HALO :]
    thin_rows = jnp.concatenate([step_bias, decay_log, skip_gain])[None]
    packed = jnp.concatenate(
        [
            conv_inner_weight,
            conv_inner_bias[None],
            gate_gain[None],
            jnp.pad(thin_rows, ((0, 0), (0, part - 3 * heads_here))),
        ],
        axis=0,
    )
    thin = jnp.concatenate([step_weight.T, adapter_step[pick].T], axis=1)
    tables = jnp.concatenate(
        [adapter_inner[pick].reshape(2 * rank, part), adapter_mixed[pick].T], axis=0
    )
    first_block, gate_block, out_block = inner_weight[:, 1], inner_weight[:, 0], out_weight.T

    if chip_plan:
        scalars = jnp.stack([lax.axis_index("dp") % 2, z, z, pick]).astype(jnp.int32)
        chips = ndp // 2
        small_rows = rows_here // 2
        rest_rows = (nz - 1) * rows_here
        same_core = [[2 * g + core for g in range(chips)] for core in (0, 1)]

        def plan_of(which):
            def entries(first, low):
                return tuple(
                    (first + b, g, low, rows_here, 2 * g + b)
                    for g in range(chips)
                    for b in (0, 1)
                )

            return (entries(0, which * rows_here),) + tuple(
                entries(2, k * rows_here) for k in range(nz - 1)
            )

        plan_in, plan_gate, plan_out = plan_of(0), plan_of(1), plan_of(2)

        def spread(v):
            return lax.all_gather(v, "dp", axis_index_groups=same_core)

        def both(v):
            return [v, xor(v, 1, ndp)]

        wide_thin = jnp.pad(thin, ((0, 0), (0, part - thin.shape[1])))
        tail = jnp.concatenate(jnp.split(tail, 2, axis=1), axis=0)
        lead = jnp.concatenate([first_block, tail, split_rows(packed), wide_thin], axis=0)
        lead = jnp.pad(lead, ((0, -lead.shape[0] % 16), (0, 0)))
        own_block = jnp.concatenate([first_block, gate_block, out_block], axis=0)
        owns = spread(own_block)
        z1 = all_slots(lead, nz)
        others = jnp.concatenate([gate_block, out_block, tables], axis=0)
        z2 = all_slots(after(others, z1), nz)
        low_at = rows_here + 2 * HALO
        halo = z1[1]
        halo_spec = pl.BlockSpec((2 * HALO, part), lambda j, sc: (rows_here // (2 * HALO), 0))
        at = low_at + 3 * packed.shape[0]
        packed = [joined_rows(v[low_at:at]) for v in z1]
        thin = jnp.concatenate([v[at : at + heads_here, : thin.shape[1]] for v in z1], axis=0).T
        small = jnp.concatenate([map_weight, thin[:rows_here]], axis=1)
        small = jnp.pad(small, ((0, 0), (0, part // 2 - small.shape[1])))
        small = jnp.concatenate([small[:small_rows], small[small_rows:]], axis=1)
        s1 = jnp.concatenate([v[:rows_here] for v in z1[1:]] + [small], axis=0)
        rest1 = spread(after(s1, owns))
        s2 = jnp.concatenate([v[:rows_here] for v in z2[1:]], axis=0)
        rest2 = spread(after(s2, rest1))
        s3 = jnp.concatenate([v[rows_here : 2 * rows_here] for v in z2[1:]], axis=0)
        rest3 = spread(after(s3, rest1))
        tables = [v[2 * rows_here :] for v in z2]
        small_spec = pl.BlockSpec(
            (chips, small_rows, part), lambda j, sc: (0, rest_rows // small_rows, 0)
        )
    else:
        scalars = jnp.stack([jnp.zeros_like(z), z, z, pick]).astype(jnp.int32)
        plan_in = tuple(((0, 0, k * width, width, 0),) for k in range(nz))
        plan_gate = plan_out = plan_in
        tail = jnp.concatenate(jnp.split(tail, 2, axis=1), axis=0)
        halo = lax.ppermute(tail, "tensor", up_one)
        halo_spec = pl.BlockSpec((2 * HALO, part), lambda j, sc: (0, 0))

        def plain(block):
            block = lax.all_gather(block, "dp", axis=0, tiled=True)
            return [jnp.concatenate(all_slots(block, nz), axis=0)[None]]

        w_inner, w_gate, w_out = plain(first_block), plain(gate_block), plain(out_block)
        packed, tables = all_slots(packed, nz), all_slots(tables, nz)
        thin = jnp.concatenate(all_slots(thin, nz), axis=0).T
        small = jnp.concatenate([map_weight, thin[:rows_here]], axis=1)
        small = jnp.pad(small, ((0, 0), (0, part // 2 - small.shape[1])))
        small = lax.all_gather(small, "dp", axis=0, tiled=True)
        small = [jnp.concatenate(jnp.split(small, 2, axis=0), axis=1)[None]]
        small_spec = pl.BlockSpec((1, width // 2, part), lambda j, sc: (0, 0, 0))
    astep = thin[rows_here : rows_here + rank]
    wide_rows = jnp.concatenate([v[:6] for v in packed], axis=1)
    conv_w, conv_b, gain = wide_rows[:4], wide_rows[4:5], wide_rows[5:6]
    thin_rows = jnp.stack([v[6, : 3 * heads_here].reshape(3, heads_here) for v in packed], axis=1)
    thin_rows = thin_rows.reshape(3, heads)
    sbias, dlog = thin_rows[0:1], thin_rows[1:2]
    skip = jnp.repeat(thin_rows[2], inner // heads)[None]
    tables = jnp.concatenate(tables, axis=1)
    two = tables[: 2 * rank].reshape(rank, 2, inner)
    agate, ainner, amixed = two[:, 0], two[:, 1], tables[2 * rank :]
    down, amap, up = adapter_down[pick], adapter_map[pick], adapter_up[pick]

    segment = segment_ids[0]
    padded = jnp.pad(segment, (HALO, HALO), constant_values=-1)
    near = lax.dynamic_slice(padded, (z * tokens,), (tokens + 2 * HALO,))
    own = near[HALO : HALO + tokens]
    by_chunk = own.reshape(chunks, CHUNK)
    before = jnp.concatenate([near[HALO - 1 : HALO], by_chunk[:-1, -1]])
    columns = [near[HALO - k : HALO - k + tokens] == own for k in (1, 2, 3)]
    columns += [
        (by_chunk == before[:, None]).reshape(tokens),
        (by_chunk == by_chunk[:, -1:]).reshape(tokens),
        own == near[HALO - 1],
        own == own[tokens - 1],
        own,
    ]
    columns += [near[HALO + k : HALO + k + tokens] == own for k in (1, 2, 3)]
    cols = jnp.stack([c.astype(F32) for c in columns], axis=1)
    rows = jnp.broadcast_to(own.astype(F32)[None], (8, tokens))

    if chip_plan:
        ready = (cols, rows, conv_w, conv_b, gain, skip, sbias, dlog, astep, ainner, amap, down)
        owns, rest1 = after((owns, rest1), ready)
        owns, rest1 = both(owns), both(rest1)
        w_inner = owns + rest1
        small = rest1
    n_w = len(w_inner)

    def by_slot(height, first=0):
        return pl.BlockSpec((height, part), lambda j, sc: (0, j + first))

    def turned(height, by):
        return pl.BlockSpec((height, part), lambda j, sc: (0, lax.rem(j + by + 2 * nz, nz)))

    def quantity(*which):
        if len(which) == 1:
            return pl.BlockSpec((1, tokens, nq), lambda j, sc: (which[0], 0, 0))
        return pl.BlockSpec((len(which), tokens, nq), lambda j, sc: (0, 0, 0))

    anywhere = pl.BlockSpec(memory_space=pl.ANY)

    def wide_out(kind=BF16, height=tokens):
        return shape((height, inner), kind)

    def weight_scratch():
        return [
            pltpu.VMEM((2, width, part), BF16),
            pltpu.SemaphoreType.DMA((2, max(len(entries) for entries in plan_in + plan_out))),
        ]


    columns = part // 2
    nrm, scale, low, low_f, maps, pre_map, quant, sig, small_full = call(
        functools.partial(front_kernel, len(small)),
        1,
        [
            whole(x.shape), halo_spec, whole((1, width)), whole((width, rank)), whole((rank, n2)),
            whole((rank, heads)), whole((4, n2)), whole((1, n2)), whole((1, heads)),
            whole((1, heads)), whole(cols.shape),
        ]
        + [small_spec] * len(small),
        [
            whole((ext, width)), whole((tokens, 128)), whole((ext, rank)), whole((tokens, rank)),
            whole((tokens, n2)), whole((tokens, n2)), whole((6, tokens, nq)), whole((tokens, heads)),
            whole((width, columns)),
        ],
        [
            shape((ext, width), BF16), shape((tokens, 128), F32), shape((ext, rank), BF16),
            shape((tokens, rank), F32), shape((tokens, n2), BF16), shape((tokens, n2), F32),
            shape((6, tokens, nq), BF16), shape((tokens, heads), F32), shape((width, columns), BF16),
        ],
        [pltpu.VMEM((ext, n2), F32)],
        8,
    )(
        scalars, x, halo, norm_gain[None], down, amap, astep, conv_map_weight, conv_map_bias[None],
        sbias, dlog, cols, *small,
    )

    results = []
    half = nz
    for first in range(0, nz, half):
        base_args = [scalars, nrm, low, ainner, conv_w, conv_b, maps, quant, cols, rows, *w_inner]
        results = call(
            functools.partial(values_kernel, heads, plan_in, first, half),
            half,
            [
                whole(nrm.shape), whole(low.shape), by_slot(rank, first), by_slot(4, first),
                by_slot(1, first), whole(maps.shape), quantity(0, 1, 2, 3), whole(cols.shape),
                whole(rows.shape),
            ]
            + [anywhere] * (n_w + len(results)),
            [by_slot(tokens, first)] * 3 + [by_slot(n, first)],
            [wide_out(), wide_out(), wide_out(), wide_out(BF16, n)],
            [
                pltpu.VMEM((chunks, CHUNK, CHUNK), F32), pltpu.VMEM((chunks, n, CHUNK), BF16),
                pltpu.VMEM((ext, part), F32), pltpu.VMEM((3, tokens, 128), F32),
            ]
            + weight_scratch(),
            15,
            {len(base_args) + i: i for i in range(len(results))},
        )(*base_args, *results)
    values, slope, y_local, s_local = results

    ent_last = quant[4, tokens - 1].reshape(3, heads).astype(F32).sum(0)
    through = jnp.repeat(ent_last, inner // heads)[None]
    hops = min(nz - 1, 1 + (DOC_MOST - 2) // tokens)

    def carry(local, pairs, turn):
        got = [lax.ppermute(local, "tensor", pairs)]
        for hop in range(1, hops):
            passed = got[-1].astype(F32) * jnp.roll(through, -turn * hop * part, axis=1)
            got.append(lax.ppermute(passed.astype(BF16), "tensor", pairs))
        return got

    s_in = carry(s_local, up_one, 1)
    from_left = [turned(n, -1 - hop) for hop in range(hops)]
    from_right = [turned(n, 1 + hop) for hop in range(hops)]

    if chip_plan:
        w_gate = owns + both(after(rest2, values))
    act, act_slope = call(
        functools.partial(gate_kernel, plan_gate, nz),
        nz,
        [whole(nrm.shape), whole(low.shape), by_slot(rank)] + [anywhere] * n_w,
        [by_slot(tokens), by_slot(tokens)],
        [wide_out(), wide_out()],
        weight_scratch(),
        10,
    )(scalars, after(nrm, s_local), low, agate, *w_gate)
    if chip_plan:
        w_out = owns + both(after(rest3, s_in[-1], act))

    def slot_in(height, phase, by=0):
        def index(j, sc):
            at = (jnp.minimum(j, nz - 1), jnp.maximum(j - nz, 0), lax.rem(j, nz))[phase]
            return (0, lax.rem(at + by + 2 * nz, nz))

        return pl.BlockSpec((height, part), index)

    gg, r_gate, gy, gz, g_local, mixed_low, tab_up, tab_mixed = call(
        functools.partial(gated_kernel, heads, plan_out, nz, hops),
        2 * nz,
        [
            whole(cot.shape), whole(up.shape), slot_in(rank, 0), slot_in(tokens, 2),
            slot_in(tokens, 1), slot_in(tokens, 0), slot_in(tokens, 0), slot_in(1, 0), slot_in(1, 2), quantity(4),
            whole(maps.shape),
        ]
        + [slot_in(n, 0, -1 - hop) for hop in range(hops)]
        + [anywhere] * n_w,
        [
            slot_in(tokens, 0), whole((tokens, 128)), slot_in(tokens, 1), slot_in(tokens, 1),
            slot_in(n, 1), whole((tokens, rank)), whole(up.shape), slot_in(rank, 1),
        ],
        [
            wide_out(), shape((tokens, 128), F32), wide_out(), wide_out(), wide_out(BF16, n),
            shape((tokens, rank), BF16), shape(up.shape, F32), wide_out(F32, rank),
        ],
        [
            pltpu.VMEM((nz, tokens, part), F32), pltpu.VMEM((nz, tokens, part), F32),
            pltpu.VMEM((nz, tokens, part), BF16), pltpu.VMEM((tokens, 128), F32),
            pltpu.VMEM((tokens, 128), F32), pltpu.VMEM((n, tokens), BF16),
            pltpu.VMEM((tokens, rank), F32), pltpu.VMEM((tokens, rank), F32),
            pltpu.VMEM((rank, tokens), BF16),
        ]
        + weight_scratch(),
        26,
    )(
        scalars, cot, up, amixed, act, act_slope, y_local, values, skip, gain, quant, maps, *s_in, *w_out,
    )

    g_in = carry(g_local, down_one, -1)
    dx, gmaps, r_local = [], [], []
    count = nz // 2 if nz % 2 == 0 else nz
    for first in range(0, nz, count):
        here = count * part // SUB
        heads_two = count * heads_here // 2
        args = [
            scalars, values, gy if first == 0 else after(gy, g_in[0]), maps, quant, cols, rows, *s_in
        ]
        dx, gmaps_part, r_part = call(
            functools.partial(backward_kernel, heads, first, count, hops),
            count,
            [
                by_slot(tokens, first), by_slot(tokens, first), whole(maps.shape),
                quantity(0, 1, 2, 3), whole(cols.shape), whole(rows.shape),
            ]
            + [turned(n, first - 1 - hop) for hop in range(hops)]
            + [anywhere] * (first > 0),
            [by_slot(tokens, first), whole((tokens, n2)), whole((2 * heads_two, tokens))],
            [wide_out(), shape((tokens, n2), F32), shape((2 * heads_two, tokens), F32)],
            [
                pltpu.VMEM((chunks, CHUNK, CHUNK), F32), pltpu.VMEM((chunks, CHUNK, CHUNK), F32),
                pltpu.VMEM((chunks, CHUNK, CHUNK), F32), pltpu.VMEM((tokens, n), F32),
                pltpu.VMEM((tokens, n), F32), pltpu.VMEM((heads_two, 8, tokens), F32),
                pltpu.VMEM((heads_two, 8, 2 * tokens), F32), pltpu.VMEM((here, 8, tokens), F32),
                pltpu.VMEM((here, 8, tokens), F32), pltpu.VMEM((here, 8, tokens), F32),
                pltpu.VMEM((chunks, n, CHUNK), BF16), pltpu.VMEM((chunks, n, CHUNK), BF16),
            ],
            18,
            {len(args): 0} if first > 0 else None,
        )(*args, *([dx] if first > 0 else []))
        gmaps.append(gmaps_part)
        r_local.append(r_part)

    c_all, cmap, gstep = call(
        functools.partial(finish_kernel, heads, nz, hops, len(gmaps)),
        nz,
        [
            by_slot(tokens), by_slot(tokens), by_slot(tokens), by_slot(tokens), whole(maps.shape),
            quantity(1), quantity(4), quantity(5), by_slot(1), whole(sig.shape), whole(dlog.shape),
            whole(pre_map.shape),
        ]
        + [whole(v.shape) for v in gmaps + r_local]
        + from_left
        + from_right,
        [by_slot(tokens), whole((tokens, n2)), whole((tokens, heads))],
        [wide_out(), shape((tokens, n2), F32), shape((tokens, heads), BF16)],
        [
            pltpu.VMEM((inner // SUB, 8, tokens), F32), pltpu.VMEM((inner // SUB, 8, tokens), F32),
            pltpu.VMEM((tokens, n), F32), pltpu.VMEM((inner // SUB, 8, CHUNK), F32),
        ],
        12,
    )(
        scalars, values, dx, gy, slope, maps, quant, quant, quant, skip, sig, dlog, pre_map, *gmaps,
        *r_local, *s_in, *g_in,
    )

    c_halo = lax.ppermute(
        jnp.concatenate([c_all[:HALO], cmap[:HALO].astype(BF16)], axis=1), "tensor", down_one
    )
    start, glow_gate, tab_gate = call(
        functools.partial(gate_rows_kernel, plan_gate, nz),
        nz,
        [by_slot(tokens), by_slot(rank), whole(low.shape)] + [anywhere] * n_w,
        [whole((tokens, width)), whole((tokens, rank)), by_slot(rank)],
        [shape((tokens, width), F32), shape((tokens, rank), F32), wide_out(F32, rank)],
        [pltpu.VMEM((rank, tokens), BF16)] + weight_scratch(),
        11,
    )(scalars, after(gz, c_all), agate, low, *w_gate)
    total_width = 3 * part + 2 * width + n2 + 128
    gi, gmap, glow, *packs = call(
        functools.partial(tables_kernel, nz, heads_here),
        nz,
        [
            by_slot(tokens), turned(HALO, 1), whole(cmap.shape), whole((HALO, n2)),
            whole((tokens, rank)), by_slot(rank), by_slot(rank), whole(up.shape), by_slot(4),
            whole((4, n2)), by_slot(rank), whole(amap.shape),
            whole(astep.shape), whole(gstep.shape), whole(low.shape), whole(low_f.shape),
            whole(nrm.shape), whole(cols.shape),
        ],
        [
            by_slot(tokens), whole((tokens, n2)), whole((tokens, rank)),
            *[whole((rank, total_width))] * nz,
        ],
        [
            wide_out(), shape((tokens, n2), BF16), shape((tokens, rank), BF16),
            *[shape((rank, total_width), BF16)] * nz,
        ],
        [
            pltpu.VMEM((ext, SUB), F32), pltpu.VMEM((tokens, rank), F32),
            pltpu.VMEM((rank, tokens), BF16),
        ],
        10,
    )(
        scalars, c_all, c_halo[:, :inner], cmap, c_halo[:, inner:], glow_gate, tab_gate, tab_mixed, tab_up,
        conv_w, conv_map_weight, ainner, amap, astep, gstep, low, low_f, nrm, cols,
    )

    input_grad = call(
        functools.partial(input_kernel, plan_in, nz),
        nz,
        [
            whole((tokens, width)), by_slot(tokens), whole(gmap.shape), whole(gstep.shape),
            whole(glow.shape), whole(small_full.shape), whole(down.shape),
            whole(x.shape), whole(cot.shape), whole(scale.shape), whole((1, width)),
        ]
        + [anywhere] * n_w,
        whole(x.shape),
        shape(x.shape, F32),
        [pltpu.VMEM((tokens, width), F32)] + weight_scratch(),
        14,
    )(
        scalars, start, gi, gmap, gstep, glow, small_full, down, x, cot, scale,
        norm_gain[None], *w_inner,
    )

    total = packs[0].astype(F32)
    for k in range(1, nz):
        total = total + around(packs[k], -k, nz).astype(F32)
    total = total.astype(BF16)
    layer_out = call(
        functools.partial(out_kernel, plan_out, nz),
        nz,
        [
            whole(x.shape), by_slot(tokens), whole(up.shape), whole(r_gate.shape),
            whole((tokens, rank)),
        ]
        + [anywhere] * n_w,
        whole(x.shape),
        shape(x.shape, BF16),
        [pltpu.VMEM((tokens, width), F32)] + weight_scratch(),
        12,
    )(scalars, x, after(gg, total), up, r_gate, mixed_low, *w_out)

    if chip_plan:
        every = jnp.stack([total] + [xor(total, m, ndp) for m in (2, 4, 6)])
        every = jnp.concatenate([every, xor(every, 1, ndp)], axis=0)
    else:
        every = lax.all_gather(total, "dp")
    every = every.astype(F32)
    hot = (every[:, 0, total_width - 128 + heads_here][:, None] == jnp.arange(adapters)[None, :].astype(F32)).astype(F32)
    summed = jnp.einsum("sa,src->arc", hot, every, precision=EXACT)
    grad_inner = summed[:, :, : 2 * part].reshape(adapters, rank, 2, part)
    grad_mixed = jnp.swapaxes(summed[:, :, 2 * part : 3 * part], 1, 2)
    at = 3 * part
    grad_down = jnp.swapaxes(summed[:, :, at : at + width], 1, 2)
    grad_up = summed[:, :, at + width : at + 2 * width]
    at = at + 2 * width
    grad_map = summed[:, :, at : at + n2]
    grad_step = summed[:, :, at + n2 : at + n2 + heads_here]
    return (
        layer_out[None], input_grad[None], grad_down, grad_inner, grad_map, grad_step, grad_mixed, grad_up
    )


def solution(mesh):
    return jax.shard_map(
        shards,
        mesh=mesh,
        in_specs=(
            P("dp", "tensor", None),
            P("dp", "tensor", None),
            P("dp", None),
            P("dp"),
            P(),
            P("dp", None, "tensor"),
            P("dp", None),
            P("dp", "tensor"),
            P(None, "tensor"),
            P("tensor"),
            P(),
            P(),
            P("tensor"),
            P("tensor"),
            P("tensor"),
            P("tensor"),
            P("tensor", "dp"),
            P(),
            P(None, None, None, "tensor"),
            P(),
            P(None, None, "tensor"),
            P(None, "tensor", None),
            P(),
        ),
        out_specs=(
            P("dp", "tensor", None),
            P("dp", "tensor", None),
            P(),
            P(None, None, None, "tensor"),
            P(),
            P(None, None, "tensor"),
            P(None, "tensor", None),
            P(),
        ),
        check_vma=False,
    )
```

```python
import functools

import jax
import jax.numpy as jnp
from jax import lax
from jax.experimental import pallas as pl
from jax.experimental.pallas import tpu as pltpu
from jax.sharding import PartitionSpec as P

EPSILON = 1e-05
HALO = 16
CHUNK = 128
SUB = 256
DOC_MOST = 800
LOG2E = 1.4426950408889634
F32 = jnp.float32
BF16 = jnp.bfloat16
EXACT = lax.Precision.HIGHEST


def dot(a, b, precision=None):
    return lax.dot_general(
        a, b, (((1,), (0,)), ((), ())), precision=precision, preferred_element_type=F32
    )


def dot_nt(a, b, precision=None):
    return lax.dot_general(
        a, b, (((1,), (1,)), ((), ())), precision=precision, preferred_element_type=F32
    )


def sigmoid(v):
    return 0.5 * jnp.tanh(0.5 * v) + 0.5


def split3(v):
    hi = v.astype(BF16)
    rest = v - hi.astype(F32)
    mid = rest.astype(BF16)
    lo = (rest - mid.astype(F32)).astype(BF16)
    return jnp.concatenate([hi, mid, lo], axis=1)


def spread_matrix(heads, cols, base, width):
    k = lax.broadcasted_iota(jnp.int32, (3 * heads, cols), 0)
    k = jnp.where(k >= 2 * heads, k - 2 * heads, jnp.where(k >= heads, k - heads, k))
    l = lax.broadcasted_iota(jnp.int32, (3 * heads, cols), 1)
    return jnp.where(k == base + l // width, 1.0, 0.0).astype(BF16)


def row_matrix(heads, rows, base):
    k = lax.broadcasted_iota(jnp.int32, (rows, 3 * heads), 1)
    k = jnp.where(k >= 2 * heads, k - 2 * heads, jnp.where(k >= heads, k - heads, k))
    i = lax.broadcasted_iota(jnp.int32, (rows, 3 * heads), 0)
    return jnp.where(k == base + i, 1.0, 0.0).astype(BF16)


def row_picks(groups, width, kind=BF16):
    row = lax.broadcasted_iota(jnp.int32, (8, groups * width), 0)
    lane = lax.broadcasted_iota(jnp.int32, (8, groups * width), 1)
    return jnp.where(row == lane // width, 1.0, 0.0).astype(kind)


def head_rows(ref, heads, each, lanes=None, only=None):
    blocks, _, columns = ref.shape
    flat = ref[...].reshape(blocks * 8, columns)
    if lanes is not None:
        flat = jnp.concatenate([flat[:, at : at + CHUNK] for at in lanes], axis=1)
    head = lax.broadcasted_iota(jnp.int32, (heads, blocks * 8), 0)
    row = lax.broadcasted_iota(jnp.int32, (heads, blocks * 8), 1)
    inside = lax.rem(head, each)
    if only is None:
        pick = row == head // each * 8 + inside
    else:
        pick = (row == head // each * 8) & (inside == only)
    return dot(jnp.where(pick, 1.0, 0.0), flat, precision=EXACT)


def two_heads(v, lane_low):
    return jnp.concatenate(
        [jnp.where(lane_low, v, 0.0), jnp.where(lane_low, 0.0, v)], axis=0
    ).astype(BF16)


def triangle(strict_upper=False):
    r = lax.broadcasted_iota(jnp.int32, (CHUNK, CHUNK), 0)
    c = lax.broadcasted_iota(jnp.int32, (CHUNK, CHUNK), 1)
    keep = (r < c) if strict_upper else (r >= c)
    return jnp.where(keep, 1.0, 0.0)


def conv_forward(buffer, tokens, weight, bias, cols):
    result = bias + weight[0:1] * buffer[HALO : HALO + tokens, :]
    for lag in range(1, 4):
        moved = buffer[HALO - lag : HALO - lag + tokens, :]
        result = result + weight[lag : lag + 1] * (moved * cols[:, lag - 1 : lag])
    return result


def fetch(plan, scalars, refs, buffer, sems, slot, k, wait=False):
    for at, entries in enumerate(plan):

        @pl.when(k == at)
        def _(entries=entries):
            for index, (which, lead, source, rows, place) in enumerate(entries):
                place = pl.multiple_of((place ^ scalars[0]) * rows, rows)
                copy = pltpu.make_async_copy(
                    refs[which].at[lead, pl.ds(source, rows)],
                    buffer.at[slot, pl.ds(place, rows)],
                    sems.at[slot, index],
                )
                copy.wait() if wait else copy.start()


def pieces_of(plan):
    return 1 + max(entry[0] for entries in plan for entry in entries)


def stream(plan, scalars, refs, buffer, sems, j, first, last, k):
    slot = lax.rem(j, 2)

    @pl.when(j == first)
    def _():
        fetch(plan, scalars, refs, buffer, sems, slot, k)

    @pl.when(j + 1 < last)
    def _():
        fetch(plan, scalars, refs, buffer, sems, 1 - slot, k + 1)

    fetch(plan, scalars, refs, buffer, sems, slot, k, wait=True)
    return slot


def lanes_of(i):
    return pl.ds(pl.multiple_of(i * SUB, SUB), SUB)


def chunk_rows(c):
    return slice(c * CHUNK, (c + 1) * CHUNK)


def allowed_mask(cols, rows, c, transposed=False):
    r = lax.broadcasted_iota(jnp.int32, (CHUNK, CHUNK), 0)
    l = lax.broadcasted_iota(jnp.int32, (CHUNK, CHUNK), 1)
    same = cols[chunk_rows(c), 7:8] == rows[0:1, chunk_rows(c)]
    return same & ((r <= l) if transposed else (r >= l))


def added(refs, lanes):
    total = refs[0][:, lanes].astype(F32)
    for ref in refs[1:]:
        total = total + ref[:, lanes].astype(F32)
    return total


def transpose(v):
    return v.astype(F32).T.astype(BF16)


def front_kernel(
    n_small, scalars, x, halo, gain, down, amap, astep, cmw, cmb, sbias, dlog, cols, *rest
):
    small_refs, rest = rest[:n_small], rest[n_small:]
    nrm, scale, low, low_out, maps, pre_map, quant, sig_out, small, buffer = rest
    tokens, n2 = maps.shape
    heads = sig_out.shape[1]
    lead, half, _ = small_refs[0].shape
    columns = small.shape[1]
    for g in range(lead):
        for b in range(n_small):
            at = pl.multiple_of(((g * n_small + b) ^ scalars[0]) * 2 * half, 2 * half)
            small[pl.ds(at, half)] = small_refs[b][g, :, :columns]
            small[pl.ds(at + half, half)] = small_refs[b][g, :, columns:]
    before = jnp.concatenate([halo[:HALO], halo[HALO:]], axis=1).astype(F32)
    before = jnp.where(scalars[1] > 0, before, 0.0)
    xf = jnp.concatenate([before, x[...].astype(F32)], axis=0)
    q = lax.rsqrt(jnp.mean(xf * xf, axis=-1, keepdims=True) + EPSILON)
    normed = (xf * q * gain[...]).astype(BF16)
    scale[...] = jnp.broadcast_to(q[HALO:], scale.shape)
    adapter_low = dot(normed, down[...])
    low_out[...] = adapter_low[HALO:]
    adapter_low = adapter_low.astype(BF16)
    low[...] = adapter_low
    nrm[...] = normed
    buffer[...] = dot(normed, small[:, :n2]) + dot(adapter_low, amap[...])
    pre = conv_forward(buffer, tokens, cmw[...], cmb[...], cols[...])
    pre_map[...] = pre
    maps[...] = (pre * sigmoid(pre)).astype(BF16)
    raw = dot(normed[HALO:], small[:, n2 : n2 + heads]) + sbias[...]
    raw = raw + dot(adapter_low[HALO:], astep[...])
    step = jnp.maximum(raw, 0.0) + jnp.log(1.0 + jnp.exp(-jnp.abs(raw)))
    sig_out[...] = sigmoid(raw)
    rate = -jnp.exp(dlog[...])
    drop = step * rate * LOG2E
    lower = triangle()
    sums = []
    for c in range(tokens // CHUNK):
        sums.append(dot(lower, drop[c * CHUNK : (c + 1) * CHUNK], precision=EXACT))
    base = jnp.zeros_like(sums[0][0:1])
    bases = []
    for c in range(tokens // CHUNK):
        bases.append(base)
        base = base + sums[c][CHUNK - 1 : CHUNK]
    column = cols[...]
    cum = jnp.concatenate(sums, axis=0)
    whole = jnp.concatenate([s + b for s, b in zip(sums, bases)], axis=0)
    left = jnp.concatenate([s[CHUNK - 1 : CHUNK] - s for s in sums], axis=0)
    quant[0] = split3(cum)
    quant[1] = split3(step)
    quant[2] = split3(jnp.exp2(cum) * column[:, 3:4])
    quant[3] = split3(jnp.exp2(left) * column[:, 4:5])
    quant[4] = split3(jnp.exp2(whole) * column[:, 5:6])
    quant[5] = split3(jnp.exp2(base - whole) * column[:, 6:7])


def values_kernel(
    heads, plan, first, count, scalars, nrm, low, aw, cw, cb, maps, quant, cols, rows, *rest
):
    n_w = pieces_of(plan)
    w_refs, rest = rest[:n_w], rest[-10:]
    values, slope_out, y_out, s_out, masked, in_t, buffer, wide_buffer, wbuf, sems = rest
    j = pl.program_id(0)
    slot = stream(plan, scalars, w_refs, wbuf, sems, j, 0, count, j + first)
    tokens = maps.shape[0]
    chunks = tokens // CHUNK
    n = maps.shape[1] // 2

    @pl.when(j == 0)
    def _():
        for c in range(chunks):
            b = maps[chunk_rows(c), :n]
            scores = dot_nt(maps[chunk_rows(c), n:], b)
            masked[c] = jnp.where(allowed_mask(cols, rows, c), scores, 0.0)
            in_t[c] = transpose(b)
        for lag in range(3):
            wide_buffer[lag] = jnp.broadcast_to(cols[:, lag : lag + 1], wide_buffer.shape[1:])

    buffer[...] = dot(nrm[...], wbuf[slot]) + dot(low[...], aw[...])
    subs = buffer.shape[1] // SUB
    lane_low = lax.broadcasted_iota(jnp.int32, (CHUNK, 128), 1) < 64

    def body(i, carry):
        lanes = lanes_of(i)
        base = ((j + first) * subs + i) * (SUB // 64)
        weight = cw[:, lanes]
        pre = cb[:, lanes] + weight[0:1] * buffer[HALO : HALO + tokens, lanes]
        for lag in range(1, 4):
            keep = jnp.concatenate([wide_buffer[lag - 1]] * 2, axis=1)
            moved = buffer[HALO - lag : HALO - lag + tokens, lanes]
            pre = pre + weight[lag : lag + 1] * (moved * keep)
        s = sigmoid(pre)
        slope_out[:, lanes] = (s * (1.0 + pre * (1.0 - s))).astype(BF16)
        v = (pre * s).astype(BF16)
        values[:, lanes] = v
        wide = spread_matrix(heads, SUB, base, 64)
        v = v.astype(F32)
        vp = dot(quant[1], wide) * v
        row = dot_nt(row_matrix(heads, 8, base), quant[0])
        pair_wide = [spread_matrix(heads, 2 * CHUNK, base + 2 * p, CHUNK) for p in range(2)]
        state = None
        for c in range(chunks):
            rs = chunk_rows(c)
            cum_c = quant[0, rs]
            mask2 = jnp.concatenate([masked[c], masked[c]], axis=1)
            inside = []
            for p in range(2):
                r2 = jnp.concatenate(
                    [row[2 * p : 2 * p + 1, rs], row[2 * p + 1 : 2 * p + 2, rs]], axis=1
                )
                decay = jnp.exp2(jnp.minimum(dot(cum_c, pair_wide[p]) - r2, 0.0))
                vbd = two_heads(vp[rs, p * 128 : (p + 1) * 128], lane_low)
                inside.append(dot((decay * mask2).astype(BF16), vbd))
            y = jnp.concatenate(inside, axis=1)
            enter = dot(quant[2, rs], wide)
            if c > 0:
                y = y + enter * dot(maps[rs, n:], state.astype(BF16))
            y_out[rs, lanes] = y.astype(y_out.dtype)
            end = dot(quant[3, rs], wide)
            fresh = dot(in_t[c], (end * vp[rs]).astype(BF16))
            state = fresh if c == 0 else state * enter[CHUNK - 1 : CHUNK] + fresh
        s_out[:, lanes] = state.astype(s_out.dtype)
        return carry

    lax.fori_loop(0, subs, body, 0)


def gate_kernel(plan, count, scalars, nrm, low, aw, *rest):
    n_w = pieces_of(plan)
    w_refs, (act_out, slope_out, wbuf, sems) = rest[:n_w], rest[n_w:]
    j = pl.program_id(0)
    slot = stream(plan, scalars, w_refs, wbuf, sems, j, 0, count, j)

    def body(i, carry):
        lanes = lanes_of(i)
        gate = dot(nrm[HALO:], wbuf[slot, :, lanes]) + dot(low[HALO:], aw[:, lanes])
        s = sigmoid(gate)
        act_out[:, lanes] = (gate * s).astype(BF16)
        slope_out[:, lanes] = (s * (1.0 + gate * (1.0 - s))).astype(BF16)
        return carry

    lax.fori_loop(0, act_out.shape[1] // SUB, body, 0)


def gated_kernel(
    heads, plan, count, n_s, scalars, cot, up, amixed, act_in, act_slope, y_in, values, skip, gain, quant, maps, *rest
):
    n_w = pieces_of(plan)
    states, w_refs, rest = rest[:n_s], rest[n_s : n_s + n_w], rest[n_s + n_w :]
    gg_out, r_out, gy_out, gz_out, g_out, mlow_out, tab_up, tab_mixed, *rest = rest
    grad, ys, ggs, squares, inner, out_t, gml, low, scaled, wbuf, sems = rest
    j = pl.program_id(0)
    n = maps.shape[1] // 2
    part = act_in.shape[1]
    subs = part // SUB

    @pl.when(j == 0)
    def _():
        gml[...] = dot_nt(cot[...], up[...])
        low[...] = jnp.zeros_like(low)
        inner[...] = jnp.zeros_like(inner)
        squares[...] = jnp.zeros_like(squares)
        out_t[...] = transpose(maps[:, n:])

    @pl.when(j < count)
    def _():
        slot = stream(plan, scalars, w_refs, wbuf, sems, j, 0, count, j)
        thin = gml[...].astype(BF16)

        def body(i, carry):
            lanes = lanes_of(i)
            gradient = dot(cot[...], wbuf[slot, :, lanes]) + dot(thin, amixed[:, lanes])
            grad[j, :, lanes] = gradient
            wide = spread_matrix(heads, SUB, (j * subs + i) * (SUB // 64), 64)
            state = added(states, lanes).astype(BF16)
            entering = dot(quant[0], wide) * dot(maps[:, n:], state)
            y = y_in[:, lanes].astype(F32) + entering
            y = y + skip[:, lanes] * values[:, lanes].astype(F32)
            ys[j, :, lanes] = y
            gated = y * act_in[:, lanes].astype(F32)
            scaled_up = (gated * gain[:, lanes]).astype(BF16)
            ggs[j, :, lanes] = scaled_up
            gg_out[:, lanes] = scaled_up
            square = gated * gated
            squares[...] += square[:, :128] + square[:, 128:]
            term = scaled_up.astype(F32) * gradient
            inner[...] += term[:, :128] + term[:, 128:]
            return carry

        lax.fori_loop(0, subs, body, 0, unroll=True)
        low[...] += dot_nt(ggs[j], amixed[...])

    @pl.when(j >= count)
    def _():
        k = j - count
        size = count * part
        r = lax.rsqrt(jnp.sum(squares[...], axis=-1, keepdims=True) / size + EPSILON)
        cube = r * r * r * (jnp.sum(inner[...], axis=-1, keepdims=True) / size)

        @pl.when(k == 0)
        def _():
            r_out[...] = jnp.broadcast_to(r, r_out.shape)
            scaled[...] = transpose(gml[...] * r)
            mixed_low = low[...] * r
            mlow_out[...] = mixed_low.astype(BF16)
            tab_up[...] = dot(transpose(mixed_low), cot[...])

        tab_mixed[...] = dot(scaled[...], ggs[k])

        def body(i, carry):
            lanes = lanes_of(i)
            y = ys[k, :, lanes]
            act = act_in[:, lanes].astype(F32)
            grad_gated = (grad[k, :, lanes] * gain[:, lanes]) * r - y * act * cube
            gy = grad_gated * act
            gy_out[:, lanes] = gy.astype(BF16)
            gz_out[:, lanes] = (grad_gated * y * act_slope[:, lanes].astype(F32)).astype(BF16)
            enter = dot(quant[0], spread_matrix(heads, SUB, (k * subs + i) * (SUB // 64), 64))
            g_out[:, lanes] = dot(out_t[...], (enter * gy).astype(BF16)).astype(g_out.dtype)
            return carry

        lax.fori_loop(0, subs, body, 0, unroll=True)


def backward_kernel(
    heads, first, count, n_s, scalars, values, gy_in, maps, quant, cols, rows, *rest
):
    s_refs, rest = rest[:n_s], rest[-15:]
    dx_out, gmaps_out, r_out, masked, allowed, mixed, grad_b, grad_c, *rest = rest
    col_p, row_p, carry_a, carry_b, ends, in_b, out_b = rest
    j = pl.program_id(0)
    tokens = maps.shape[0]
    chunks = tokens // CHUNK
    n = maps.shape[1] // 2
    subs = values.shape[1] // SUB
    here = count * subs * (SUB // 64)

    @pl.when(j == 0)
    def _():
        for c in range(chunks):
            rs = chunk_rows(c)
            ok = allowed_mask(cols, rows, c, transposed=True)
            scores = dot_nt(maps[rs, :n], maps[rs, n:])
            masked[c] = jnp.where(ok, scores, 0.0)
            allowed[c] = jnp.where(ok, 1.0, 0.0)
            in_b[c] = transpose(maps[rs, :n])
            out_b[c] = transpose(maps[rs, n:])
        for ref in (mixed, grad_b, grad_c, carry_b, ends):
            ref[...] = jnp.zeros_like(ref)

    lane_low = lax.broadcasted_iota(jnp.int32, (CHUNK, 128), 1) < 64
    ones = jnp.ones((8, CHUNK), BF16)
    by_pair = row_picks(2, CHUNK)
    by_head = row_picks(SUB // 64, 64)
    by_head_f = row_picks(SUB // 64, 64, F32)

    def body(i, carry):
        lanes = lanes_of(i)
        block = j * subs + i
        base = (first * subs + block) * (SUB // 64)
        wide = spread_matrix(heads, SUB, base, 64)
        vp = dot(quant[1], wide) * values[:, lanes].astype(F32)
        row = dot_nt(row_matrix(heads, 8, base), quant[0])
        pair_wide = [spread_matrix(heads, 2 * CHUNK, base + 2 * p, CHUNK) for p in range(2)]
        enters, lefts, states = [], [], []
        state = added(s_refs, lanes)
        for c in range(chunks):
            rs = chunk_rows(c)
            enters.append(dot(quant[2, rs], wide))
            lefts.append(dot(quant[3, rs], wide))
            states.append(state)
            if c < chunks - 1:
                fresh = dot(in_b[c], (lefts[c] * vp[rs]).astype(BF16))
                state = state * enters[c][CHUNK - 1 : CHUNK] + fresh
        adjoint = None
        for c in range(chunks - 1, -1, -1):
            rs = chunk_rows(c)
            cum_c = quant[0, rs]
            gy = gy_in[rs, lanes].astype(F32)
            mask2 = jnp.concatenate([masked[c], masked[c]], axis=1)
            dx = []
            for p in range(2):
                pair = slice(p * 128, (p + 1) * 128)
                r2 = jnp.concatenate(
                    [row[2 * p : 2 * p + 1, rs], row[2 * p + 1 : 2 * p + 2, rs]], axis=1
                )
                decay = jnp.exp2(jnp.minimum(r2 - dot(cum_c, pair_wide[p]), 0.0))
                gbd = two_heads(gy[:, pair], lane_low)
                dx.append(dot((decay * mask2).astype(BF16), gbd))
                part = decay * dot_nt(vp[rs, pair].astype(BF16), gbd)
                mixed[c] += part[:, :CHUNK] + part[:, CHUNK:]
                weighed = (part * mask2).astype(BF16)
                col_p[block * 2 + p, :, rs] = dot_nt(by_pair, weighed)
                row_p[block * 2 + p, :, 2 * c * CHUNK : 2 * (c + 1) * CHUNK] = dot(ones, weighed)
            dx = jnp.concatenate(dx, axis=1)
            entering = enters[c] * gy
            carried = entering * dot(maps[rs, n:], states[c].astype(BF16))
            carry_a[block, :, rs] = dot_nt(by_head, carried.astype(BF16))
            entering = entering.astype(BF16)
            grad_c[rs] += dot_nt(entering, states[c].astype(BF16))
            last = enters[c][CHUNK - 1 : CHUNK]
            if adjoint is not None:
                adj = adjoint.astype(BF16)
                leaving = lefts[c] * dot(maps[rs, :n], adj)
                dx = dx + leaving
                carry_b[block, :, rs] = dot_nt(by_head, (vp[rs] * leaving).astype(BF16))
                grad_b[rs] += dot_nt((lefts[c] * vp[rs]).astype(BF16), adj)
                through = jnp.sum(adjoint * states[c], axis=0, keepdims=True) * last
                through = jnp.sum(by_head_f * through, axis=1, keepdims=True)
                ends[block, :, rs] = jnp.broadcast_to(through, (8, CHUNK))
            dx_out[rs, lanes] = dx.astype(dx_out.dtype)
            if c > 0:
                fresh = dot(out_b[c], entering)
                adjoint = fresh if adjoint is None else adjoint * last + fresh
        return carry

    lax.fori_loop(0, subs, body, 0, unroll=True)

    @pl.when(j == count - 1)
    def _():
        suffix, prefix = triangle(), triangle(strict_upper=True)
        plain = head_rows(carry_a, here, SUB // 64) - head_rows(col_p, here, 2)
        for q in range(2):
            lanes = [(2 * c + q) * CHUNK for c in range(chunks)]
            plain = plain + head_rows(row_p, here, 2, lanes, q)
        left = head_rows(carry_b, here, SUB // 64)
        sums = head_rows(ends, here, SUB // 64)
        for c in range(chunks):
            rs = chunk_rows(c)
            w = mixed[c] * allowed[c]
            gb = grad_b[rs] + dot(w.astype(BF16), maps[rs, n:])
            gc = grad_c[rs] + dot(w.T.astype(BF16), maps[rs, :n])
            gmaps_out[rs] = jnp.concatenate([gb, gc], axis=1)
            r_out[:, rs] = (
                dot(plain[:, rs], suffix, precision=EXACT)
                + dot(left[:, rs], prefix, precision=EXACT)
                + sums[:, rs]
            )


def finish_kernel(
    heads, count, n_s, n_r, scalars, values, dx_in, gy_in, slope, maps, quant_step, quant_enter, quant_left,
    skip, sig, dlog, pre_map, *rest
):
    gmap_refs, r_refs, rest = rest[:n_r], rest[n_r : 2 * n_r], rest[2 * n_r :]
    s_refs, g_refs, rest = rest[:n_s], rest[n_s : 2 * n_s], rest[2 * n_s :]
    c_out, cmap_out, gstep_out, col_g, carry_b, grad_b, ends = rest
    j = pl.program_id(0)
    tokens = maps.shape[0]
    n = maps.shape[1] // 2
    subs = values.shape[1] // SUB

    @pl.when(j == 0)
    def _():
        grad_b[...] = jnp.zeros_like(grad_b)

    by_head = row_picks(SUB // 64, 64)
    by_head_f = row_picks(SUB // 64, 64, F32)

    def body(i, carry):
        lanes = lanes_of(i)
        base = (j * subs + i) * (SUB // 64)
        wide = spread_matrix(heads, SUB, base, 64)
        block = j * subs + i
        v = values[:, lanes].astype(F32)
        step = dot(quant_step[0], wide)
        left = dot(quant_left[0], wide)
        vp = step * v
        adjoint = added(g_refs, lanes)
        both = adjoint * added(s_refs, lanes)
        adjoint = adjoint.astype(BF16)
        more = left * dot(maps[:, :n], adjoint)
        dx = dx_in[:, lanes].astype(F32) + more
        carry_b[block] = dot_nt(by_head, (vp * more).astype(BF16))
        col_g[block] = dot_nt(by_head, (v * dx).astype(BF16))
        grad_b[...] += dot_nt((left * vp).astype(BF16), adjoint)
        last = dot(quant_enter[0, tokens - 16 :], wide)[15:16]
        through = jnp.sum(both, axis=0, keepdims=True) * last
        through = jnp.sum(by_head_f * through, axis=1, keepdims=True)
        ends[block] = jnp.broadcast_to(through, (8, CHUNK))
        dv = step * dx + skip[:, lanes] * gy_in[:, lanes].astype(F32)
        c_out[:, lanes] = (dv * slope[:, lanes].astype(F32)).astype(BF16)
        return carry

    lax.fori_loop(0, subs, body, 0, unroll=True)

    @pl.when(j == count - 1)
    def _():
        prefix = triangle(strict_upper=True)
        run = head_rows(ends, heads, SUB // 64)
        left = head_rows(carry_b, heads, SUB // 64)
        grads = head_rows(col_g, heads, SUB // 64)
        rate = -jnp.exp(dlog[...]).T
        for c in range(tokens // CHUNK):
            rs = chunk_rows(c)
            total = jnp.concatenate([ref[:, rs] for ref in r_refs], axis=0)
            total = total + dot(left[:, rs], prefix, precision=EXACT) + run
            run = run + jnp.sum(left[:, rs], axis=1, keepdims=True)
            raw = grads[:, rs] + rate * total
            gstep_out[rs] = (raw.T * sig[rs]).astype(BF16)
        gmaps = gmap_refs[0][...]
        for ref in gmap_refs[1:]:
            gmaps = gmaps + ref[...]
        gb = gmaps[:, :n] + grad_b[...]
        g = jnp.concatenate([gb, gmaps[:, n:]], axis=1)
        pm = pre_map[...]
        sm = sigmoid(pm)
        cmap_out[...] = (g * (sm * (1.0 + pm * (1.0 - sm)))).astype(cmap_out.dtype)


def conv_backward(buffer, tokens, weight, cols):
    result = weight[0:1] * buffer[0:tokens, :]
    for lag in range(1, 4):
        result = result + weight[lag : lag + 1] * (
            buffer[lag : lag + tokens, :] * cols[:, 7 + lag : 8 + lag]
        )
    return result


def tables_kernel(
    count, heads_here, scalars, c_in, c_halo, cmap, cmap_halo, glow_in, tab_gate, tab_mixed, tab_up, cw, cmw, ainner,
    amap, astep, gstep, low, low_f, nrm, cols, gi_out, gmap_out, glow_out, *rest
):
    packs, (buffer, glow, low_t) = rest[:count], rest[count:]
    j = pl.program_id(0)
    tokens = gi_out.shape[0]
    subs = gi_out.shape[1] // SUB

    @pl.when(j == 0)
    def _():
        low_t[...] = transpose(low[HALO:])
        buffer[:tokens] = cmap[...].astype(F32)
        buffer[tokens:] = cmap_halo[...].astype(F32)
        gmap = conv_backward(buffer, tokens, cmw[...], cols[...])
        exact_low = low_f[...].T
        tab_map = dot(exact_low, gmap, precision=EXACT)
        tab_step = dot(exact_low, gstep[...].astype(F32), precision=EXACT)
        rank = tab_map.shape[0]
        lane = lax.broadcasted_iota(jnp.int32, (rank, 128), 1)
        last = packs[0].shape[1] - 128
        for k, pack in enumerate(packs):
            steps = tab_step[:, k * heads_here : (k + 1) * heads_here]
            steps = jnp.concatenate([steps, jnp.zeros((rank, 128 - heads_here), F32)], axis=1)
            if k == 0:
                steps = jnp.where(lane == heads_here, scalars[3].astype(F32), steps)
            pack[:, last:] = steps.astype(BF16)
            pack[:, last - tab_map.shape[1] : last] = tab_map.astype(BF16)
        gmap = gmap.astype(BF16)
        gmap_out[...] = gmap
        glow[...] = glow_in[...] + dot_nt(gmap, amap[...]) + dot_nt(gstep[...], astep[...])

    def body(i, carry):
        lanes = lanes_of(i)
        buffer[:tokens] = c_in[:, lanes].astype(F32)
        buffer[tokens:] = c_halo[:, lanes].astype(F32)
        gi_out[:, lanes] = conv_backward(buffer, tokens, cw[:, lanes], cols[...]).astype(BF16)
        return carry

    lax.fori_loop(0, subs, body, 0, unroll=True)
    glow[...] += dot_nt(gi_out[...], ainner[...])
    tab_inner = dot(low_t[...], gi_out[...])
    part = gi_out.shape[1]
    for k, pack in enumerate(packs):

        @pl.when(j == k)
        def _(pack=pack):
            pack[:, :part] = tab_gate[...].astype(BF16)
            pack[:, part : 2 * part] = tab_inner.astype(BF16)
            pack[:, 2 * part : 3 * part] = tab_mixed[...].astype(BF16)

    @pl.when(j == count - 1)
    def _():
        glow_out[...] = glow[...].astype(BF16)
        down = dot(transpose(glow[...]), nrm[HALO:])
        down = down.astype(BF16)
        width = down.shape[1]
        for pack in packs:
            pack[:, 3 * part : 3 * part + width] = down
            pack[:, 3 * part + width : 3 * part + 2 * width] = tab_up[...].astype(BF16)


def out_kernel(plan, count, scalars, x, gg, up, r_in, mlow, *rest):
    n_w = pieces_of(plan)
    w_refs = rest[:n_w]
    out, total, wbuf, sems = rest[n_w:]
    j = pl.program_id(0)
    slot = stream(plan, scalars, w_refs, wbuf, sems, j, 0, count, j)
    term = dot_nt(gg[...], wbuf[slot])

    @pl.when(j == 0)
    def _():
        total[...] = term

    @pl.when(j > 0)
    def _():
        total[...] += term

    @pl.when(j == count - 1)
    def _():
        branch = total[...] * r_in[:, 0:1]
        out[...] = (x[...].astype(F32) + branch + dot(mlow[...], up[...])).astype(BF16)


def gate_rows_kernel(plan, count, scalars, gz, agate, low, *rest):
    n_w = pieces_of(plan)
    w_refs = rest[:n_w]
    total, glow, tab_gate, low_t, wbuf, sems = rest[n_w:]
    j = pl.program_id(0)
    slot = stream(plan, scalars, w_refs, wbuf, sems, j, 0, count, j)

    @pl.when(j == 0)
    def _():
        low_t[...] = transpose(low[HALO:])

    term = dot_nt(gz[...], wbuf[slot])
    thin = dot_nt(gz[...], agate[...])
    tab_gate[...] = dot(low_t[...], gz[...])

    @pl.when(j == 0)
    def _():
        total[...] = term
        glow[...] = thin

    @pl.when(j > 0)
    def _():
        total[...] += term
        glow[...] += thin


def input_kernel(
    plan, count, scalars, start, gi, gmap, gstep, glow, small, down, x, cot, scale, gain, *rest
):
    n_w = pieces_of(plan)
    w_refs = rest[:n_w]
    out, total, wbuf, sems = rest[n_w:]
    j = pl.program_id(0)
    slot = stream(plan, scalars, w_refs, wbuf, sems, j, 0, count, j)

    @pl.when(j == 0)
    def _():
        n2, heads = gmap.shape[1], gstep.shape[1]
        total[...] = (
            start[...]
            + dot_nt(gmap[...], small[:, :n2])
            + dot_nt(gstep[...], small[:, n2 : n2 + heads])
        )

    total[...] += dot_nt(gi[...], wbuf[slot])

    @pl.when(j == count - 1)
    def _():
        q = scale[:, 0:1]
        xf = x[...].astype(F32)
        normed_grad = total[...] + dot_nt(glow[...], down[...])
        weighted = normed_grad * gain[...]
        mean = jnp.mean(xf * weighted, axis=-1, keepdims=True)
        out[...] = q * weighted - xf * (q * q * q * mean) + cot[...].astype(F32)


def whole(shape):
    return pl.BlockSpec(shape, lambda *_: (0,) * len(shape))


def call(kernel, steps, in_specs, out_specs, out_shape, scratch, micros, aliases=None):
    return pl.pallas_call(
        kernel,
        grid_spec=pltpu.PrefetchScalarGridSpec(
            num_scalar_prefetch=1,
            grid=(steps,),
            in_specs=in_specs,
            out_specs=out_specs,
            scratch_shapes=scratch,
        ),
        out_shape=out_shape,
        input_output_aliases=aliases or {},
        compiler_params=pltpu.CompilerParams(
            dimension_semantics=("arbitrary",), vmem_limit_bytes=56 * 2**20
        ),
        cost_estimate=pl.CostEstimate(
            flops=int(micros * 1.1e9), bytes_accessed=int(micros * 1e6), transcendentals=0
        ),
    )


def shape(dims, kind):
    return jax.ShapeDtypeStruct(dims, kind)


def xor(v, m, ndp):
    return lax.ppermute(v, "dp", [(i, i ^ m) for i in range(ndp)])


def around(v, k, nz):
    return lax.ppermute(v, "tensor", [(i, (i + k) % nz) for i in range(nz)])


def all_slots(v, nz):
    return [v] + [around(v, k, nz) for k in range(1, nz)]


def after(v, *others):
    return lax.optimization_barrier((v, others))[0]


def split_rows(v):
    high = lax.optimization_barrier(v.astype(BF16))
    rest = v - high.astype(F32)
    middle = lax.optimization_barrier(rest.astype(BF16))
    return jnp.concatenate([high, middle, (rest - middle.astype(F32)).astype(BF16)], axis=0)


def joined_rows(v):
    high, middle, low = jnp.split(v.astype(F32), 3, axis=0)
    return high + middle + low


def shards(
    layer_in,
    cotangent,
    segment_ids,
    adapter_ids,
    norm_gain,
    inner_weight,
    map_weight,
    step_weight,
    conv_inner_weight,
    conv_inner_bias,
    conv_map_weight,
    conv_map_bias,
    step_bias,
    decay_log,
    skip_gain,
    gate_gain,
    out_weight,
    adapter_down,
    adapter_inner,
    adapter_map,
    adapter_step,
    adapter_mixed,
    adapter_up,
):
    ndp, nz = lax.axis_size("dp"), lax.axis_size("tensor")
    z = lax.axis_index("tensor")
    x, cot = layer_in[0], cotangent[0]
    tokens, width = x.shape
    rows_here = inner_weight.shape[0]
    part = gate_gain.shape[0]
    inner = part * nz
    heads_here = step_bias.shape[0]
    heads = heads_here * nz
    adapters, _, rank = adapter_down.shape
    n2 = map_weight.shape[1]
    n = n2 // 2
    chunks = tokens // CHUNK
    ext = tokens + HALO
    nq = 3 * heads
    up_one = [(i, i + 1) for i in range(nz - 1)]
    down_one = [(i + 1, i) for i in range(nz - 1)]
    chip_plan = ndp == 8 and nz == 4 and rows_here % 64 == 0

    pick = adapter_ids[0]
    tail = x[tokens - HALO :]
    thin_rows = jnp.concatenate([step_bias, decay_log, skip_gain])[None]
    packed = jnp.concatenate(
        [
            conv_inner_weight,
            conv_inner_bias[None],
            gate_gain[None],
            jnp.pad(thin_rows, ((0, 0), (0, part - 3 * heads_here))),
        ],
        axis=0,
    )
    thin = jnp.concatenate([step_weight.T, adapter_step[pick].T], axis=1)
    tables = jnp.concatenate(
        [adapter_inner[pick].reshape(2 * rank, part), adapter_mixed[pick].T], axis=0
    )
    first_block, gate_block, out_block = inner_weight[:, 1], inner_weight[:, 0], out_weight.T

    if chip_plan:
        scalars = jnp.stack([lax.axis_index("dp") % 2, z, z, pick]).astype(jnp.int32)
        chips = ndp // 2
        small_rows = rows_here // 2
        rest_rows = (nz - 1) * rows_here
        same_core = [[2 * g + core for g in range(chips)] for core in (0, 1)]

        def plan_of(which):
            def entries(first, low):
                return tuple(
                    (first + b, g, low, rows_here, 2 * g + b)
                    for g in range(chips)
                    for b in (0, 1)
                )

            return (entries(0, which * rows_here),) + tuple(
                entries(2, k * rows_here) for k in range(nz - 1)
            )

        plan_in, plan_gate, plan_out = plan_of(0), plan_of(1), plan_of(2)

        def spread(v):
            return lax.all_gather(v, "dp", axis_index_groups=same_core)

        def both(v):
            return [v, xor(v, 1, ndp)]

        wide_thin = jnp.pad(thin, ((0, 0), (0, part - thin.shape[1])))
        tail = jnp.concatenate(jnp.split(tail, 2, axis=1), axis=0)
        lead = jnp.concatenate([first_block, tail, split_rows(packed), wide_thin], axis=0)
        lead = jnp.pad(lead, ((0, -lead.shape[0] % 16), (0, 0)))
        own_block = jnp.concatenate([first_block, gate_block, out_block], axis=0)
        owns = spread(own_block)
        z1 = all_slots(lead, nz)
        others = jnp.concatenate([gate_block, out_block, tables], axis=0)
        z2 = all_slots(after(others, z1), nz)
        low_at = rows_here + 2 * HALO
        halo = z1[1]
        halo_spec = pl.BlockSpec((2 * HALO, part), lambda j, sc: (rows_here // (2 * HALO), 0))
        at = low_at + 3 * packed.shape[0]
        packed = [joined_rows(v[low_at:at]) for v in z1]
        thin = jnp.concatenate([v[at : at + heads_here, : thin.shape[1]] for v in z1], axis=0).T
        small = jnp.concatenate([map_weight, thin[:rows_here]], axis=1)
        small = jnp.pad(small, ((0, 0), (0, part // 2 - small.shape[1])))
        small = jnp.concatenate([small[:small_rows], small[small_rows:]], axis=1)
        s1 = jnp.concatenate([v[:rows_here] for v in z1[1:]] + [small], axis=0)
        rest1 = spread(after(s1, owns))
        s2 = jnp.concatenate([v[:rows_here] for v in z2[1:]], axis=0)
        rest2 = spread(after(s2, rest1))
        s3 = jnp.concatenate([v[rows_here : 2 * rows_here] for v in z2[1:]], axis=0)
        rest3 = spread(after(s3, rest1))
        tables = [v[2 * rows_here :] for v in z2]
        small_spec = pl.BlockSpec(
            (chips, small_rows, part), lambda j, sc: (0, rest_rows // small_rows, 0)
        )
    else:
        scalars = jnp.stack([jnp.zeros_like(z), z, z, pick]).astype(jnp.int32)
        plan_in = tuple(((0, 0, k * width, width, 0),) for k in range(nz))
        plan_gate = plan_out = plan_in
        tail = jnp.concatenate(jnp.split(tail, 2, axis=1), axis=0)
        halo = lax.ppermute(tail, "tensor", up_one)
        halo_spec = pl.BlockSpec((2 * HALO, part), lambda j, sc: (0, 0))

        def plain(block):
            block = lax.all_gather(block, "dp", axis=0, tiled=True)
            return [jnp.concatenate(all_slots(block, nz), axis=0)[None]]

        w_inner, w_gate, w_out = plain(first_block), plain(gate_block), plain(out_block)
        packed, tables = all_slots(packed, nz), all_slots(tables, nz)
        thin = jnp.concatenate(all_slots(thin, nz), axis=0).T
        small = jnp.concatenate([map_weight, thin[:rows_here]], axis=1)
        small = jnp.pad(small, ((0, 0), (0, part // 2 - small.shape[1])))
        small = lax.all_gather(small, "dp", axis=0, tiled=True)
        small = [jnp.concatenate(jnp.split(small, 2, axis=0), axis=1)[None]]
        small_spec = pl.BlockSpec((1, width // 2, part), lambda j, sc: (0, 0, 0))
    astep = thin[rows_here : rows_here + rank]
    wide_rows = jnp.concatenate([v[:6] for v in packed], axis=1)
    conv_w, conv_b, gain = wide_rows[:4], wide_rows[4:5], wide_rows[5:6]
    thin_rows = jnp.stack([v[6, : 3 * heads_here].reshape(3, heads_here) for v in packed], axis=1)
    thin_rows = thin_rows.reshape(3, heads)
    sbias, dlog = thin_rows[0:1], thin_rows[1:2]
    skip = jnp.repeat(thin_rows[2], inner // heads)[None]
    tables = jnp.concatenate(tables, axis=1)
    two = tables[: 2 * rank].reshape(rank, 2, inner)
    agate, ainner, amixed = two[:, 0], two[:, 1], tables[2 * rank :]
    down, amap, up = adapter_down[pick], adapter_map[pick], adapter_up[pick]

    segment = segment_ids[0]
    padded = jnp.pad(segment, (HALO, HALO), constant_values=-1)
    near = lax.dynamic_slice(padded, (z * tokens,), (tokens + 2 * HALO,))
    own = near[HALO : HALO + tokens]
    by_chunk = own.reshape(chunks, CHUNK)
    before = jnp.concatenate([near[HALO - 1 : HALO], by_chunk[:-1, -1]])
    columns = [near[HALO - k : HALO - k + tokens] == own for k in (1, 2, 3)]
    columns += [
        (by_chunk == before[:, None]).reshape(tokens),
        (by_chunk == by_chunk[:, -1:]).reshape(tokens),
        own == near[HALO - 1],
        own == own[tokens - 1],
        own,
    ]
    columns += [near[HALO + k : HALO + k + tokens] == own for k in (1, 2, 3)]
    cols = jnp.stack([c.astype(F32) for c in columns], axis=1)
    rows = jnp.broadcast_to(own.astype(F32)[None], (8, tokens))

    if chip_plan:
        ready = (cols, rows, conv_w, conv_b, gain, skip, sbias, dlog, astep, ainner, amap, down)
        owns, rest1 = after((owns, rest1), ready)
        owns, rest1 = both(owns), both(rest1)
        w_inner = owns + rest1
        small = rest1
    n_w = len(w_inner)

    def by_slot(height, first=0):
        return pl.BlockSpec((height, part), lambda j, sc: (0, j + first))

    def turned(height, by):
        return pl.BlockSpec((height, part), lambda j, sc: (0, lax.rem(j + by + 2 * nz, nz)))

    def quantity(*which):
        if len(which) == 1:
            return pl.BlockSpec((1, tokens, nq), lambda j, sc: (which[0], 0, 0))
        return pl.BlockSpec((len(which), tokens, nq), lambda j, sc: (0, 0, 0))

    anywhere = pl.BlockSpec(memory_space=pl.ANY)

    def wide_out(kind=BF16, height=tokens):
        return shape((height, inner), kind)

    def weight_scratch():
        return [
            pltpu.VMEM((2, width, part), BF16),
            pltpu.SemaphoreType.DMA((2, max(len(entries) for entries in plan_in + plan_out))),
        ]


    columns = part // 2
    nrm, scale, low, low_f, maps, pre_map, quant, sig, small_full = call(
        functools.partial(front_kernel, len(small)),
        1,
        [
            whole(x.shape), halo_spec, whole((1, width)), whole((width, rank)), whole((rank, n2)),
            whole((rank, heads)), whole((4, n2)), whole((1, n2)), whole((1, heads)),
            whole((1, heads)), whole(cols.shape),
        ]
        + [small_spec] * len(small),
        [
            whole((ext, width)), whole((tokens, 128)), whole((ext, rank)), whole((tokens, rank)),
            whole((tokens, n2)), whole((tokens, n2)), whole((6, tokens, nq)), whole((tokens, heads)),
            whole((width, columns)),
        ],
        [
            shape((ext, width), BF16), shape((tokens, 128), F32), shape((ext, rank), BF16),
            shape((tokens, rank), F32), shape((tokens, n2), BF16), shape((tokens, n2), F32),
            shape((6, tokens, nq), BF16), shape((tokens, heads), F32), shape((width, columns), BF16),
        ],
        [pltpu.VMEM((ext, n2), F32)],
        8,
    )(
        scalars, x, halo, norm_gain[None], down, amap, astep, conv_map_weight, conv_map_bias[None],
        sbias, dlog, cols, *small,
    )

    results = []
    half = nz
    for first in range(0, nz, half):
        base_args = [scalars, nrm, low, ainner, conv_w, conv_b, maps, quant, cols, rows, *w_inner]
        results = call(
            functools.partial(values_kernel, heads, plan_in, first, half),
            half,
            [
                whole(nrm.shape), whole(low.shape), by_slot(rank, first), by_slot(4, first),
                by_slot(1, first), whole(maps.shape), quantity(0, 1, 2, 3), whole(cols.shape),
                whole(rows.shape),
            ]
            + [anywhere] * (n_w + len(results)),
            [by_slot(tokens, first)] * 3 + [by_slot(n, first)],
            [wide_out(), wide_out(), wide_out(), wide_out(BF16, n)],
            [
                pltpu.VMEM((chunks, CHUNK, CHUNK), F32), pltpu.VMEM((chunks, n, CHUNK), BF16),
                pltpu.VMEM((ext, part), F32), pltpu.VMEM((3, tokens, 128), F32),
            ]
            + weight_scratch(),
            15,
            {len(base_args) + i: i for i in range(len(results))},
        )(*base_args, *results)
    values, slope, y_local, s_local = results

    ent_last = quant[4, tokens - 1].reshape(3, heads).astype(F32).sum(0)
    through = jnp.repeat(ent_last, inner // heads)[None]
    hops = min(nz - 1, 1 + (DOC_MOST - 2) // tokens)

    def carry(local, pairs, turn):
        got = [lax.ppermute(local, "tensor", pairs)]
        for hop in range(1, hops):
            passed = got[-1].astype(F32) * jnp.roll(through, -turn * hop * part, axis=1)
            got.append(lax.ppermute(passed.astype(BF16), "tensor", pairs))
        return got

    s_in = carry(s_local, up_one, 1)
    from_left = [turned(n, -1 - hop) for hop in range(hops)]
    from_right = [turned(n, 1 + hop) for hop in range(hops)]

    if chip_plan:
        w_gate = owns + both(after(rest2, values))
    act, act_slope = call(
        functools.partial(gate_kernel, plan_gate, nz),
        nz,
        [whole(nrm.shape), whole(low.shape), by_slot(rank)] + [anywhere] * n_w,
        [by_slot(tokens), by_slot(tokens)],
        [wide_out(), wide_out()],
        weight_scratch(),
        10,
    )(scalars, after(nrm, s_local), low, agate, *w_gate)
    if chip_plan:
        w_out = owns + both(after(rest3, s_in[-1], act))

    def slot_in(height, phase, by=0):
        def index(j, sc):
            at = (jnp.minimum(j, nz - 1), jnp.maximum(j - nz, 0), lax.rem(j, nz))[phase]
            return (0, lax.rem(at + by + 2 * nz, nz))

        return pl.BlockSpec((height, part), index)

    gg, r_gate, gy, gz, g_local, mixed_low, tab_up, tab_mixed = call(
        functools.partial(gated_kernel, heads, plan_out, nz, hops),
        2 * nz,
        [
            whole(cot.shape), whole(up.shape), slot_in(rank, 0), slot_in(tokens, 2),
            slot_in(tokens, 1), slot_in(tokens, 0), slot_in(tokens, 0), slot_in(1, 0), slot_in(1, 2), quantity(4),
            whole(maps.shape),
        ]
        + [slot_in(n, 0, -1 - hop) for hop in range(hops)]
        + [anywhere] * n_w,
        [
            slot_in(tokens, 0), whole((tokens, 128)), slot_in(tokens, 1), slot_in(tokens, 1),
            slot_in(n, 1), whole((tokens, rank)), whole(up.shape), slot_in(rank, 1),
        ],
        [
            wide_out(), shape((tokens, 128), F32), wide_out(), wide_out(), wide_out(BF16, n),
            shape((tokens, rank), BF16), shape(up.shape, F32), wide_out(F32, rank),
        ],
        [
            pltpu.VMEM((nz, tokens, part), F32), pltpu.VMEM((nz, tokens, part), F32),
            pltpu.VMEM((nz, tokens, part), BF16), pltpu.VMEM((tokens, 128), F32),
            pltpu.VMEM((tokens, 128), F32), pltpu.VMEM((n, tokens), BF16),
            pltpu.VMEM((tokens, rank), F32), pltpu.VMEM((tokens, rank), F32),
            pltpu.VMEM((rank, tokens), BF16),
        ]
        + weight_scratch(),
        26,
    )(
        scalars, cot, up, amixed, act, act_slope, y_local, values, skip, gain, quant, maps, *s_in, *w_out,
    )

    g_in = carry(g_local, down_one, -1)
    dx, gmaps, r_local = [], [], []
    count = nz // 2 if nz % 2 == 0 else nz
    for first in range(0, nz, count):
        here = count * part // SUB
        heads_two = count * heads_here // 2
        args = [
            scalars, values, gy if first == 0 else after(gy, g_in[0]), maps, quant, cols, rows, *s_in
        ]
        dx, gmaps_part, r_part = call(
            functools.partial(backward_kernel, heads, first, count, hops),
            count,
            [
                by_slot(tokens, first), by_slot(tokens, first), whole(maps.shape),
                quantity(0, 1, 2, 3), whole(cols.shape), whole(rows.shape),
            ]
            + [turned(n, first - 1 - hop) for hop in range(hops)]
            + [anywhere] * (first > 0),
            [by_slot(tokens, first), whole((tokens, n2)), whole((2 * heads_two, tokens))],
            [wide_out(), shape((tokens, n2), F32), shape((2 * heads_two, tokens), F32)],
            [
                pltpu.VMEM((chunks, CHUNK, CHUNK), F32), pltpu.VMEM((chunks, CHUNK, CHUNK), F32),
                pltpu.VMEM((chunks, CHUNK, CHUNK), F32), pltpu.VMEM((tokens, n), F32),
                pltpu.VMEM((tokens, n), F32), pltpu.VMEM((heads_two, 8, tokens), F32),
                pltpu.VMEM((heads_two, 8, 2 * tokens), F32), pltpu.VMEM((here, 8, tokens), F32),
                pltpu.VMEM((here, 8, tokens), F32), pltpu.VMEM((here, 8, tokens), F32),
                pltpu.VMEM((chunks, n, CHUNK), BF16), pltpu.VMEM((chunks, n, CHUNK), BF16),
            ],
            18,
            {len(args): 0} if first > 0 else None,
        )(*args, *([dx] if first > 0 else []))
        gmaps.append(gmaps_part)
        r_local.append(r_part)

    c_all, cmap, gstep = call(
        functools.partial(finish_kernel, heads, nz, hops, len(gmaps)),
        nz,
        [
            by_slot(tokens), by_slot(tokens), by_slot(tokens), by_slot(tokens), whole(maps.shape),
            quantity(1), quantity(4), quantity(5), by_slot(1), whole(sig.shape), whole(dlog.shape),
            whole(pre_map.shape),
        ]
        + [whole(v.shape) for v in gmaps + r_local]
        + from_left
        + from_right,
        [by_slot(tokens), whole((tokens, n2)), whole((tokens, heads))],
        [wide_out(), shape((tokens, n2), F32), shape((tokens, heads), BF16)],
        [
            pltpu.VMEM((inner // SUB, 8, tokens), F32), pltpu.VMEM((inner // SUB, 8, tokens), F32),
            pltpu.VMEM((tokens, n), F32), pltpu.VMEM((inner // SUB, 8, CHUNK), F32),
        ],
        12,
    )(
        scalars, values, dx, gy, slope, maps, quant, quant, quant, skip, sig, dlog, pre_map, *gmaps,
        *r_local, *s_in, *g_in,
    )

    c_halo = lax.ppermute(
        jnp.concatenate([c_all[:HALO], cmap[:HALO].astype(BF16)], axis=1), "tensor", down_one
    )
    start, glow_gate, tab_gate = call(
        functools.partial(gate_rows_kernel, plan_gate, nz),
        nz,
        [by_slot(tokens), by_slot(rank), whole(low.shape)] + [anywhere] * n_w,
        [whole((tokens, width)), whole((tokens, rank)), by_slot(rank)],
        [shape((tokens, width), F32), shape((tokens, rank), F32), wide_out(F32, rank)],
        [pltpu.VMEM((rank, tokens), BF16)] + weight_scratch(),
        11,
    )(scalars, after(gz, c_all), agate, low, *w_gate)
    total_width = 3 * part + 2 * width + n2 + 128
    gi, gmap, glow, *packs = call(
        functools.partial(tables_kernel, nz, heads_here),
        nz,
        [
            by_slot(tokens), turned(HALO, 1), whole(cmap.shape), whole((HALO, n2)),
            whole((tokens, rank)), by_slot(rank), by_slot(rank), whole(up.shape), by_slot(4),
            whole((4, n2)), by_slot(rank), whole(amap.shape),
            whole(astep.shape), whole(gstep.shape), whole(low.shape), whole(low_f.shape),
            whole(nrm.shape), whole(cols.shape),
        ],
        [
            by_slot(tokens), whole((tokens, n2)), whole((tokens, rank)),
            *[whole((rank, total_width))] * nz,
        ],
        [
            wide_out(), shape((tokens, n2), BF16), shape((tokens, rank), BF16),
            *[shape((rank, total_width), BF16)] * nz,
        ],
        [
            pltpu.VMEM((ext, SUB), F32), pltpu.VMEM((tokens, rank), F32),
            pltpu.VMEM((rank, tokens), BF16),
        ],
        10,
    )(
        scalars, c_all, c_halo[:, :inner], cmap, c_halo[:, inner:], glow_gate, tab_gate, tab_mixed, tab_up,
        conv_w, conv_map_weight, ainner, amap, astep, gstep, low, low_f, nrm, cols,
    )

    input_grad = call(
        functools.partial(input_kernel, plan_in, nz),
        nz,
        [
            whole((tokens, width)), by_slot(tokens), whole(gmap.shape), whole(gstep.shape),
            whole(glow.shape), whole(small_full.shape), whole(down.shape),
            whole(x.shape), whole(cot.shape), whole(scale.shape), whole((1, width)),
        ]
        + [anywhere] * n_w,
        whole(x.shape),
        shape(x.shape, F32),
        [pltpu.VMEM((tokens, width), F32)] + weight_scratch(),
        14,
    )(
        scalars, start, gi, gmap, gstep, glow, small_full, down, x, cot, scale,
        norm_gain[None], *w_inner,
    )

    total = packs[0].astype(F32)
    for k in range(1, nz):
        total = total + around(packs[k], -k, nz).astype(F32)
    total = total.astype(BF16)
    layer_out = call(
        functools.partial(out_kernel, plan_out, nz),
        nz,
        [
            whole(x.shape), by_slot(tokens), whole(up.shape), whole(r_gate.shape),
            whole((tokens, rank)),
        ]
        + [anywhere] * n_w,
        whole(x.shape),
        shape(x.shape, BF16),
        [pltpu.VMEM((tokens, width), F32)] + weight_scratch(),
        12,
    )(scalars, x, after(gg, total), up, r_gate, mixed_low, *w_out)

    if chip_plan:
        every = jnp.stack([total] + [xor(total, m, ndp) for m in (2, 4, 6)])
        every = jnp.concatenate([every, xor(every, 1, ndp)], axis=0)
    else:
        every = lax.all_gather(total, "dp")
    every = every.astype(F32)
    hot = (every[:, 0, total_width - 128 + heads_here][:, None] == jnp.arange(adapters)[None, :].astype(F32)).astype(F32)
    summed = jnp.einsum("sa,src->arc", hot, every, precision=EXACT)
    grad_inner = summed[:, :, : 2 * part].reshape(adapters, rank, 2, part)
    grad_mixed = jnp.swapaxes(summed[:, :, 2 * part : 3 * part], 1, 2)
    at = 3 * part
    grad_down = jnp.swapaxes(summed[:, :, at : at + width], 1, 2)
    grad_up = summed[:, :, at + width : at + 2 * width]
    at = at + 2 * width
    grad_map = summed[:, :, at : at + n2]
    grad_step = summed[:, :, at + n2 : at + n2 + heads_here]
    return (
        layer_out[None], input_grad[None], grad_down, grad_inner, grad_map, grad_step, grad_mixed, grad_up
    )


def solution(mesh):
    return jax.shard_map(
        shards,
        mesh=mesh,
        in_specs=(
            P("dp", "tensor", None),
            P("dp", "tensor", None),
            P("dp", None),
            P("dp"),
            P(),
            P("dp", None, "tensor"),
            P("dp", None),
            P("dp", "tensor"),
            P(None, "tensor"),
            P("tensor"),
            P(),
            P(),
            P("tensor"),
            P("tensor"),
            P("tensor"),
            P("tensor"),
            P("tensor", "dp"),
            P(),
            P(None, None, None, "tensor"),
            P(),
            P(None, None, "tensor"),
            P(None, "tensor", None),
            P(),
        ),
        out_specs=(
            P("dp", "tensor", None),
            P("dp", "tensor", None),
            P(),
            P(None, None, None, "tensor"),
            P(),
            P(None, None, "tensor"),
            P(None, "tensor", None),
            P(),
        ),
        check_vma=False,
    )
```
